128 devices in a mesh: ctx: 16 (over z, x_hi, core), exp: 8 (over x_lo, y).
Axes of the slice: x: 4 (x_hi: 2, x_lo: 2; x = x_hi * 2 + x_lo), y: 4, z: 4, core: 2. Of those that a mesh axis runs over, the one named last changes fastest.
Arguments:
- tokens: bfloat16 [8, 2048, 768], P('exp', 'ctx'), may hold values from -6 to 6
- cotangent: bfloat16 [8, 2048, 768], P('exp', 'ctx'), may hold values from -6 to 6
- routes: int32 [8, 2048, 1], P('exp', 'ctx'), may hold values from 0 to 15; in each aligned block of 128 rows (0 to 127, 128 to 255, ..., all dimensions but the last counted through in order) at most 10 rows name the same one
- query_weight: bfloat16 [768, 768], P(('ctx', 'exp')), may hold values from -0.0546875 to 0.0546875
- kv_weight: bfloat16 [768, 1536], P(('ctx', 'exp')), may hold values from -0.21875 to 0.21875
- out_weight: bfloat16 [768, 768], P(('ctx', 'exp')), may hold values from -3.5 to 3.5
- norm_gain_one: bfloat16 [768], P(('ctx', 'exp')), may hold values from 0.5 to 1.5
- norm_gain_two: bfloat16 [768], P(('ctx', 'exp')), may hold values from 0.5 to 1.5
- router_weight: bfloat16 [768, 16], P(('ctx', 'exp')), may hold values from -0.15625 to 0.15625
- bias_table: bfloat16 [384], P(('ctx', 'exp')), may hold values from -5 to 5
- expert_in: bfloat16 [16, 768, 3072], P('exp', None, 'ctx'), may hold values from -0.21875 to 0.21875
- expert_out: bfloat16 [16, 3072, 768], P('exp', 'ctx'), may hold values from -1.75 to 1.75
Outputs:
- mixed: bfloat16 [8, 2048, 768], P('exp', 'ctx')
- grad_tokens: float32 [8, 2048, 768], P('exp', 'ctx')
- grad_query_weight: float32 [768, 768], P(('ctx', 'exp'))
- grad_kv_weight: float32 [768, 1536], P(('ctx', 'exp'))
- grad_out_weight: float32 [768, 768], P(('ctx', 'exp'))
- grad_norm_gain_one: float32 [768], P(('ctx', 'exp'))
- grad_norm_gain_two: float32 [768], P(('ctx', 'exp'))
- grad_router_weight: float32 [768, 16], P(('ctx', 'exp'))
- grad_bias_table: float32 [384], P(('ctx', 'exp'))
- grad_expert_in: float32 [16, 768, 3072], P('exp', None, 'ctx')
- grad_expert_out: float32 [16, 3072, 768], P('exp', 'ctx')
The draws below stay inside these ranges and needn't reach their ends.
Inputs may be any that keep to these rules, and one draw needn't show every extreme that they name: `routes`: in the rows of one device each expert is named at most 10 times, a bound that some block reaches.
All inputs are finite; a program needn't handle non-finite values.
Results may differ from the reference program's by a relative error of at most 0.018.
Values may be sent and summed in bfloat16 or wider, within the bound.
A program may use at most 128 MiB of HBM per device.

```python
import math
import jax
import jax.numpy as jnp
import numpy as np
from jax import lax

D = 768
HEADS = 12
HEAD_DIM = 64
FF = 3072
NUM_BUCKETS = 32
TOK_DEV = 128
EXPERTS = 16
CAP = 10
SEQS = 8
LEN = 2048


def steps_of(stream_key, shape, cuts, smallest, high):
    gain = 1.0
    for position, blocks in cuts:
        heights = jax.random.uniform(jax.random.fold_in(jax.random.fold_in(stream_key, 6), position), (blocks,), jnp.float32, smallest / len(cuts), high / len(cuts))
        gain = gain * jnp.repeat(jnp.exp(heights), shape[position] // blocks).reshape((-1,) + (1,) * (len(shape) - 1 - position))
    return gain


def deal_out(key, own, number, rows, number_of, top, most, skew):
    ranking = jax.random.permutation(key, number_of)
    packed, ordinary = shares(number_of, rows * top, most, skew, True), shares(number_of, rows * top, most, skew, False)
    places = jnp.arange(number_of)

    def named(lengths, offset_by):
        used = int((lengths > 0).sum())
        fixed = max(1, used // 4)
        moved = fixed + (places - fixed + offset_by * (used - fixed)) % max(1, number_of - fixed)
        return jnp.zeros((number_of,), jnp.int32).at[ranking[jnp.where(places < fixed, places, moved)]].set(jnp.asarray(lengths, jnp.int32))

    lengths = jnp.where(number % 4 == 0, named(packed, number // 4), named(ordinary, number - number // 4 - 1))
    mixed = jax.random.permutation(jax.random.fold_in(own, 3), number_of)
    giver, sink = mixed[0:number_of // 2 * 2:2], mixed[1:number_of // 2 * 2:2]
    room = jnp.minimum(lengths[giver] - 1, most - lengths[sink]) // 2
    room = jnp.where((giver == ranking[0]) | (sink == ranking[0]) | (lengths[sink] == 0), 0, jnp.maximum(room, 0))
    moved = jax.random.randint(jax.random.fold_in(own, 4), (number_of // 2,), 0, 1 << 20) % (room + 1)
    lengths = lengths.at[giver].add(-moved).at[sink].add(moved)
    members = jnp.searchsorted(jnp.cumsum(lengths), jnp.arange(rows * top), side="right").astype(jnp.int32)
    grid = members.reshape(top, rows).T
    grid = grid[jax.random.permutation(jax.random.fold_in(own, 1), rows)]
    offset_by = jax.random.randint(jax.random.fold_in(own, 2), (rows, 1), 0, top)
    return jnp.take_along_axis(grid, (jnp.arange(top)[None, :] + offset_by) % top, axis=1)


def shares(count, total, bound, skew, full):
    portions = [(1 << 20) // math.isqrt(grade ** skew) + 1 for grade in range(1, count + 1)]
    largest = bound if full else min(bound, max(-(-total // count), total * portions[0] // sum(portions)))
    least = 1 if total - largest >= count - 1 else 0
    given, rest = [largest] + [least] * (count - 1), total - largest - least * (count - 1)
    while rest > 0:
        candidates = [i for i in range(1, count) if given[i] < largest] or [i for i in range(1, count) if given[i] < bound]
        mass, left = sum([portions[i] for i in candidates]), rest
        for i in candidates:
            addition = min(bound - given[i], max(1, left * portions[i] // mass), rest)
            given[i] = given[i] + addition
            rest = rest - addition
    return np.array(given)


def bell_draw(key, dims, scale, reach, shards=(), kind=jnp.bfloat16):
    result = scale * jax.random.normal(key, dims, jnp.float32)
    if shards:
        result = result * steps_of(key, dims, shards, -0.22, 0.18)
    return jnp.clip(result, -reach, reach).astype(kind)


def setup_inputs(seed: int = 0) -> dict:
    streams_of = jax.random.split(jax.random.key(seed), 13)
    tokens = bell_draw(streams_of[0], (SEQS, LEN, D), 1.0, 6.0, ((0, 8), (1, 16)))
    cotangent = bell_draw(streams_of[1], (SEQS, LEN, D), 1.0, 6.0, ((0, 8), (1, 16)))
    routes_keys = jax.random.split(jax.random.fold_in(streams_of[2], 1), SEQS * LEN // TOK_DEV)
    routes_turns = jax.random.permutation(jax.random.fold_in(streams_of[2], 3), SEQS * LEN // TOK_DEV)
    routes = jax.vmap(lambda own, number: deal_out(jax.random.fold_in(streams_of[2], 2), own, number, TOK_DEV, EXPERTS, 1, CAP, 1))(routes_keys, routes_turns).reshape((SEQS, LEN, 1))
    query_weight = bell_draw(streams_of[3], (D, D), (16 * D) ** -0.5, 0.0546875, ((0, 128),))
    kv_weight = bell_draw(streams_of[4], (D, 2 * D), D ** -0.5, 0.21875, ((0, 128),))
    out_weight = bell_draw(streams_of[5], (D, D), (max(D // 256, 1)) ** -0.5, 3.5, ((0, 128),))
    norm_gain_one = jnp.clip(1.0 + 0.1 * jax.random.normal(streams_of[6], (D,), jnp.float32), 0.5, 1.5).astype(jnp.bfloat16)
    norm_gain_two = jnp.clip(1.0 + 0.1 * jax.random.normal(streams_of[7], (D,), jnp.float32), 0.5, 1.5).astype(jnp.bfloat16)
    router_weight = bell_draw(streams_of[8], (D, EXPERTS), (2 * D) ** -0.5, 0.15625, ((0, 128),))
    bias_table = bell_draw(streams_of[9], (NUM_BUCKETS * HEADS,), 1.0, 5.0, ((0, 128),))
    expert_in = bell_draw(streams_of[10], (EXPERTS, D, FF), D ** -0.5, 0.21875, ((0, 8), (2, 16)))
    expert_out = bell_draw(streams_of[11], (EXPERTS, FF, D), (max(FF // 256, 1)) ** -0.5, 1.75, ((0, 8), (1, 16)))
    return {"tokens": tokens, "cotangent": cotangent, "routes": routes, "query_weight": query_weight, "kv_weight": kv_weight, "out_weight": out_weight, "norm_gain_one": norm_gain_one, "norm_gain_two": norm_gain_two, "router_weight": router_weight, "bias_table": bias_table, "expert_in": expert_in, "expert_out": expert_out}


epsilon = 1e-06
bucket_edges = (12, 16, 23, 32, 46, 64, 91)

@jax.custom_vjp
def low(v):
    return lax.optimization_barrier(v.astype(jnp.bfloat16)).astype(jnp.float32)

@jax.custom_vjp
def low_back(v):
    return v

def low_keep(v):
    return (low(v), None)

def low_pass(kept, grad):
    return (grad,)

def back_keep(v):
    return (v, None)

def back_low(kept, grad):
    return (low(grad),)
low.defvjp(low_keep, low_pass)
low_back.defvjp(back_keep, back_low)

def rms_scale(values_in, gain_vec):
    return values_in * lax.rsqrt(lax.optimization_barrier(jnp.mean(values_in * values_in, axis=-1, keepdims=True)) + epsilon) * gain_vec

def bucket_ids(query_location, key_pos):
    offset = key_pos[None, :] - query_location[:, None]
    distance = jnp.abs(offset)
    far_bucket = jnp.full(distance.shape, 8, jnp.int32)
    for edge_value in bucket_edges:
        far_bucket = far_bucket + (distance >= edge_value).astype(jnp.int32)
    half_bucket = jnp.where(distance < 8, distance, far_bucket)
    return half_bucket + NUM_BUCKETS // 2 * (offset > 0).astype(jnp.int32)

def reference(tokens, cotangent, routes, query_weight, kv_weight, out_weight, norm_gain_one, norm_gain_two, router_weight, bias_table, expert_in, expert_out):
    highest = lax.Precision.HIGHEST
    route_ids = routes.reshape(-1).astype(jnp.int32)
    token_total = route_ids.shape[0]
    block_total = token_total // TOK_DEV
    choose = (route_ids.reshape(block_total, TOK_DEV, 1) == jnp.arange(EXPERTS, dtype=jnp.int32)[None, None, :]).astype(jnp.int32)
    earlier = jnp.cumsum(choose, axis=1) - choose
    slot_index = lax.optimization_barrier(jnp.sum(earlier * choose, axis=2)).reshape(-1).astype(jnp.int32)
    row_index = jnp.arange(token_total, dtype=jnp.int32) // TOK_DEV * CAP + slot_index
    choose_wide = choose.reshape(token_total, EXPERTS).astype(jnp.float32)
    query_rows = min(512, LEN)
    query_starts = jnp.arange(LEN // query_rows, dtype=jnp.int32) * query_rows
    key_pos = jnp.arange(LEN, dtype=jnp.int32)

    def forward(x_all, w_query, w_kv, w_out, gain_one, gain_two, w_router, table_flat, w_in, w_expert_out):
        position_bias_matrix = table_flat.reshape(NUM_BUCKETS, HEADS)
        x_rows = x_all.reshape(token_total, D)
        h_one = low(rms_scale(x_rows, gain_one))
        queries = low_back(low(jnp.dot(h_one, w_query, precision=highest)))
        keyval = jnp.dot(h_one, w_kv, precision=highest)
        keys_all = low_back(low(keyval[:, :D]))
        values_all = low_back(low(keyval[:, D:]))

        def attend_sequence(triple):
            key_heads = triple[1].reshape(LEN, HEADS, HEAD_DIM)
            per_head_values = triple[2].reshape(LEN, HEADS, HEAD_DIM)

            def attend_block(query_pair):
                block_queries = query_pair[0].reshape(query_rows, HEADS, HEAD_DIM)
                query_location = query_pair[1] + jnp.arange(query_rows, dtype=jnp.int32)
                pair_bias = jnp.transpose(position_bias_matrix[bucket_ids(query_location, key_pos)], (2, 0, 1))
                products = jnp.einsum('qhd,khd->hqk', block_queries, key_heads, precision=highest)
                scores = low_back(products) + pair_bias
                soft_probs = jax.nn.softmax(scores, axis=-1)
                block_result_rows = jnp.einsum('hqk,khd->qhd', low(soft_probs), per_head_values, precision=highest)
                return block_result_rows.reshape(query_rows, D)
            block_outs = lax.map(jax.checkpoint(attend_block), (triple[0].reshape(LEN // query_rows, query_rows, D), query_starts))
            return block_outs.reshape(LEN, D)
        attended = lax.map(attend_sequence, (queries.reshape(SEQS, LEN, D), keys_all.reshape(SEQS, LEN, D), values_all.reshape(SEQS, LEN, D)))
        attended_low = low_back(low(attended.reshape(token_total, D)))
        residual = x_rows + low_back(jnp.dot(attended_low, w_out, precision=highest))
        h_two = low(rms_scale(residual, gain_two))
        route_probs = jax.nn.softmax(jnp.dot(h_two, w_router, precision=highest), axis=-1)
        gate_value = lax.optimization_barrier(jnp.sum(route_probs * choose_wide, axis=1))
        buffer = low_back(jnp.zeros((EXPERTS, block_total * CAP, D), jnp.float32).at[route_ids, row_index].set(h_two))
        pre_act = low_back(jnp.einsum('erd,edf->erf', buffer, w_in, precision=highest))
        hidden = low(jax.nn.gelu(pre_act))
        expert_y = low_back(low(jnp.einsum('erf,efd->erd', hidden, w_expert_out, precision=highest)))
        layer_out = residual + gate_value[:, None] * expert_y[route_ids, row_index]
        return layer_out.reshape(SEQS, LEN, D)
    layer_out, backward = jax.vjp(forward, tokens.astype(jnp.float32), query_weight.astype(jnp.float32), kv_weight.astype(jnp.float32), out_weight.astype(jnp.float32), norm_gain_one.astype(jnp.float32), norm_gain_two.astype(jnp.float32), router_weight.astype(jnp.float32), bias_table.astype(jnp.float32), expert_in.astype(jnp.float32), expert_out.astype(jnp.float32))
    gradients = backward(cotangent.astype(jnp.float32))
    return (layer_out.astype(jnp.bfloat16), gradients[0], gradients[1], gradients[2], gradients[3], gradients[4], gradients[5], gradients[6], gradients[7], gradients[8], gradients[9])
```

```python
import functools

import jax
import jax.numpy as jnp
from jax import lax
from jax.experimental import pallas as pl
from jax.experimental.pallas import tpu as pltpu
from jax.sharding import PartitionSpec as P

MESH = pl.DeviceIdType.MESH
HEADS = 12
HEAD_DIM = 64
BUCKETS = 32
TOK = 128
D = 768
CAP = 10
SLOTS = 48
CTX, EXP, ZED = 16, 8, 4
LEN = TOK * CTX
QUERIES = 256
CHUNK = 128
epsilon = 1e-06
bucket_edges = (12, 16, 23, 32, 46, 64, 91)
low = jnp.bfloat16
wide = jnp.float32
ANY = pl.BlockSpec(memory_space=pl.ANY)


def spot():
    c, e = lax.axis_index("ctx"), lax.axis_index("exp")
    return c, e, c // 4, (c // 2) % 2, c % 2


def greet(peers):
    barrier = pltpu.get_barrier_semaphore()
    for peer in peers:
        pl.semaphore_signal(barrier, inc=1, device_id=peer, device_id_type=MESH)
    pl.semaphore_wait(barrier, len(peers))


def push(src, dst, send, recv, to):
    return pltpu.make_async_remote_copy(
        src_ref=src, dst_ref=dst, send_sem=send, recv_sem=recv, device_id=to, device_id_type=MESH
    )


def group(kind):
    c, e, z, xh, k = spot()
    if kind == "exp":
        return EXP, e, lambda i: (c, i)
    if kind == "z":
        return ZED, z, lambda i: (i * 4 + xh * 2 + k, e)
    if kind == "x":
        return 2, xh, lambda i: (z * 4 + i * 2 + k, e)
    return 2, k, lambda i: (z * 4 + xh * 2 + i, e)


def swap_kernel(kind, axis, x, out, here, send, recv):
    size, me, device = group(kind)
    part = (lambda i: x) if axis is None else (lambda i: x.at[(slice(None),) * axis + (i,)])
    peers = [lax.rem(me + i, size) for i in range(1, size)]
    greet([device(p) for p in peers])
    copies = [
        push(part(p), out.at[me], send.at[i], recv.at[i], device(p)) for i, p in enumerate(peers)
    ]
    for copy in copies:
        copy.start()
    own = pltpu.make_async_copy(part(me), out.at[me], here)
    own.start()
    for copy in copies:
        copy.wait()
    own.wait()


def swap(x, kind, ident, axis=None):
    size = {"exp": EXP, "z": ZED, "x": 2, "core": 2}[kind]
    block = x.shape if axis is None else x.shape[:axis] + x.shape[axis + 1 :]
    return pl.pallas_call(
        functools.partial(swap_kernel, kind, axis),
        out_shape=jax.ShapeDtypeStruct((size, *block), x.dtype),
        in_specs=[ANY],
        out_specs=ANY,
        scratch_shapes=[
            pltpu.SemaphoreType.DMA,
            pltpu.SemaphoreType.DMA((size - 1,)),
            pltpu.SemaphoreType.DMA((size - 1,)),
        ],
        compiler_params=pltpu.CompilerParams(collective_id=ident, has_side_effects=True),
    )(x)


def weights_kernel(x, out, here, send, recv):
    c, e, z, xh, k = spot()
    zs = [lax.rem(z + i, 4) for i in range(1, 4)]
    back = [lax.rem(z + 4 - i, 4) for i in range(1, 4)]
    at = lambda z, xh, k: z * 4 + xh * 2 + k
    side, twin = (at(z, 1 - xh, k), e), (at(z, xh, 1 - k), e)
    rows = [(at(p, xh, k), e) for p in zs]
    greet([side, twin, *rows])
    mine, theirs = at(z, xh, k), at(z, 1 - xh, k)
    across = push(x, out.at[mine], send.at[0], recv.at[0], side)
    across.start()
    first = [push(x, out.at[mine], send.at[1 + i], recv.at[1 + i], d) for i, d in enumerate(rows)]
    for copy in first:
        copy.start()
    own = pltpu.make_async_copy(x, out.at[mine], here)
    own.start()
    pair = [push(x, out.at[mine], send.at[7], recv.at[7], twin)]
    pair[0].start()

    def hand(n, block):
        copy = push(out.at[block], out.at[block], send.at[7 + n], recv.at[7 + n], twin)
        copy.start()
        pair.append(copy)

    across.wait_recv()
    second = [
        push(out.at[theirs], out.at[theirs], send.at[4 + i], recv.at[4 + i], d)
        for i, d in enumerate(rows)
    ]
    for copy in second:
        copy.start()
    hand(1, theirs)
    for i, p in enumerate(back):
        first[i].wait_recv()
        hand(2 + i, at(p, xh, k))
    for i, p in enumerate(back):
        second[i].wait_recv()
        hand(5 + i, at(p, 1 - xh, k))
    for copy in pair:
        copy.wait()
    across.wait_send()
    for copy in first + second:
        copy.wait_send()
    own.wait()


def gather_weights(x, ident):
    return pl.pallas_call(
        weights_kernel,
        out_shape=jax.ShapeDtypeStruct((CTX, *x.shape), x.dtype),
        in_specs=[ANY],
        out_specs=ANY,
        scratch_shapes=[
            pltpu.SemaphoreType.DMA,
            pltpu.SemaphoreType.DMA((15,)),
            pltpu.SemaphoreType.DMA((15,)),
        ],
        compiler_params=pltpu.CompilerParams(collective_id=ident, has_side_effects=True),
    )(x)


def quad_kernel(x, out, here, send, recv):
    c, e, z, xh, k = spot()
    at = lambda xh, k: z * 4 + xh * 2 + k
    side, twin = (at(1 - xh, k), e), (at(xh, 1 - k), e)
    mine, theirs = xh * 2 + k, (1 - xh) * 2 + k
    greet([side, twin])
    across = push(x, out.at[:, :, mine], send.at[0], recv.at[0], side)
    across.start()
    pair = push(x, out.at[:, :, mine], send.at[1], recv.at[1], twin)
    pair.start()
    own = pltpu.make_async_copy(x, out.at[:, :, mine], here)
    own.start()
    across.wait_recv()
    hand = push(out.at[:, :, theirs], out.at[:, :, theirs], send.at[2], recv.at[2], twin)
    hand.start()
    across.wait_send()
    pair.wait()
    hand.wait()
    own.wait()


def gather_experts(x, ident):
    return pl.pallas_call(
        quad_kernel,
        out_shape=jax.ShapeDtypeStruct((2, 2, 4, *x.shape[2:]), x.dtype),
        in_specs=[ANY],
        out_specs=ANY,
        scratch_shapes=[
            pltpu.SemaphoreType.DMA,
            pltpu.SemaphoreType.DMA((3,)),
            pltpu.SemaphoreType.DMA((3,)),
        ],
        compiler_params=pltpu.CompilerParams(collective_id=ident, has_side_effects=True),
    )(x)


def head_of(c):
    return jnp.minimum((c // 4) * 3 + c % 4, HEADS - 1)


def owns(c):
    return c % 4 < 3


def columns(c):
    return pl.ds(pl.multiple_of(c * TOK, TOK), TOK)


def to_heads_kernel(x, out, here, send, recv):
    c, e, z, xh, k = spot()
    peers = [lax.rem(c + i, CTX) for i in range(1, CTX)]
    greet([(p, e) for p in peers])
    copies = [
        push(x.at[:, head_of(p)], out.at[:, :, columns(c)], send.at[i], recv.at[i], (p, e))
        for i, p in enumerate(peers)
    ]
    own = pltpu.make_async_copy(x.at[:, head_of(c)], out.at[:, :, columns(c)], here)
    for p, copy in zip(peers, copies):
        pl.when(owns(p))(copy.start)
    pl.when(owns(c))(own.start)
    for p, copy in zip(peers, copies):
        pl.when(owns(p))(copy.wait_send)
        pl.when(owns(c))(copy.wait_recv)
    pl.when(owns(c))(own.wait)


def from_heads_kernel(x, out, here, send, recv):
    c, e, z, xh, k = spot()
    peers = [lax.rem(c + i, CTX) for i in range(1, CTX)]
    sources = [lax.rem(c + CTX - i, CTX) for i in range(1, CTX)]
    greet([(p, e) for p in peers])
    copies = [
        push(x.at[:, :, columns(p)], out.at[:, head_of(c)], send.at[i], recv.at[i], (p, e))
        for i, p in enumerate(peers)
    ]
    own = pltpu.make_async_copy(x.at[:, :, columns(c)], out.at[:, head_of(c)], here)

    @pl.when(owns(c))
    def _():
        for copy in copies:
            copy.start()
        own.start()

    for s, copy in zip(sources, copies):
        pl.when(owns(c))(copy.wait_send)
        pl.when(owns(s))(copy.wait_recv)
    pl.when(owns(c))(own.wait)


def heads_call(kernel, x, shape, ident):
    return pl.pallas_call(
        kernel,
        out_shape=jax.ShapeDtypeStruct(shape, x.dtype),
        in_specs=[ANY],
        out_specs=ANY,
        scratch_shapes=[
            pltpu.SemaphoreType.DMA,
            pltpu.SemaphoreType.DMA((CTX - 1,)),
            pltpu.SemaphoreType.DMA((CTX - 1,)),
        ],
        compiler_params=pltpu.CompilerParams(collective_id=ident, has_side_effects=True),
    )(x)


def to_heads(x, ident):
    return heads_call(to_heads_kernel, x, (x.shape[0], HEAD_DIM, LEN), ident)


def from_heads(x, ident):
    return heads_call(from_heads_kernel, x, (x.shape[0], HEADS, HEAD_DIM, TOK), ident)


def near_buckets():
    shape = (6 * CHUNK, QUERIES)
    offset = (
        lax.broadcasted_iota(jnp.int32, shape, 0)
        - 2 * CHUNK
        - lax.broadcasted_iota(jnp.int32, shape, 1)
    )
    distance = jnp.abs(offset)
    far = jnp.full(shape, 8, jnp.int32)
    for edge in bucket_edges:
        far = far + (distance >= edge).astype(jnp.int32)
    return jnp.where(distance < 8, distance, far) + jnp.where(offset > 0, BUCKETS // 2, 0)


def tile_rows(chunk, block):
    tile = jnp.clip(chunk - 2 * block + 2, 0, 5)
    return pl.ds(pl.multiple_of(tile * CHUNK, CHUNK), CHUNK)


def chunk_rows(chunk):
    return pl.ds(pl.multiple_of(chunk * CHUNK, CHUNK), CHUNK)


def forward_kernel(qkv_ref, table_ref, p_ref, o_ref, low_ref, inv_ref, keys, bias, scores):
    block = pl.program_id(0)

    @pl.when(block == 0)
    def _():
        keys[...] = qkv_ref[1].T
        ids = near_buckets()
        tiles = jnp.zeros(ids.shape, wide)
        for b in range(BUCKETS):
            tiles = jnp.where(ids == b, table_ref[b], tiles)
        bias[...] = tiles

    here = pl.ds(pl.multiple_of(block * QUERIES, QUERIES), QUERIES)
    queries = qkv_ref[0, :, here]

    def score(chunk, top):
        rows = chunk_rows(chunk)
        part = jnp.dot(keys[rows, :], queries, preferred_element_type=wide)
        part = part + bias[tile_rows(chunk, block), :]
        scores[rows, :] = part
        return jnp.maximum(top, jnp.max(part.reshape(CHUNK // 8, 8, QUERIES), axis=0))

    top = lax.fori_loop(
        0, LEN // CHUNK, score, jnp.full((8, QUERIES), -1e30, wide), unroll=2
    )
    top = jnp.max(top, axis=0, keepdims=True)

    def weigh(chunk, total):
        rows = chunk_rows(chunk)
        part = jnp.exp(scores[rows, :] - top)
        p_ref[rows, :] = part.astype(low)
        return total + jnp.sum(part.reshape(CHUNK // 8, 8, QUERIES), axis=0)

    total = lax.fori_loop(0, LEN // CHUNK, weigh, jnp.zeros((8, QUERIES), wide), unroll=2)
    inverse = 1.0 / jnp.sum(total, axis=0, keepdims=True)
    out = jnp.dot(qkv_ref[2], p_ref[...], preferred_element_type=wide) * inverse
    o_ref[...] = out
    low_ref[0] = out.astype(low)
    inv_ref[...] = inverse


def attend(qkv, table):
    whole = lambda *shape: pl.BlockSpec(shape, lambda i: (0,) * len(shape))
    return pl.pallas_call(
        forward_kernel,
        grid=(LEN // QUERIES,),
        out_shape=(
            jax.ShapeDtypeStruct((LEN, LEN), low),
            jax.ShapeDtypeStruct((HEAD_DIM, LEN), wide),
            jax.ShapeDtypeStruct((1, HEAD_DIM, LEN), low),
            jax.ShapeDtypeStruct((1, LEN), wide),
        ),
        in_specs=[whole(3, HEAD_DIM, LEN), pl.BlockSpec(memory_space=pltpu.SMEM)],
        out_specs=(
            pl.BlockSpec((LEN, QUERIES), lambda i: (0, i)),
            pl.BlockSpec((HEAD_DIM, QUERIES), lambda i: (0, i)),
            pl.BlockSpec((1, HEAD_DIM, QUERIES), lambda i: (0, 0, i)),
            pl.BlockSpec((1, QUERIES), lambda i: (0, i)),
        ),
        scratch_shapes=[
            pltpu.VMEM((LEN, HEAD_DIM), low),
            pltpu.VMEM((6 * CHUNK, QUERIES), wide),
            pltpu.VMEM((LEN, QUERIES), wide),
        ],
        compiler_params=pltpu.CompilerParams(vmem_limit_bytes=32 << 20),
    )(qkv, table)


def backward_kernel(
    qkv_ref, p_ref, o_ref, inv_ref, do_ref, grad_ref, sums_ref, values, dk, dv, tiles, slopes
):
    block = pl.program_id(0)

    @pl.when(block == 0)
    def _():
        values[...] = qkv_ref[2].T
        dk[...] = jnp.zeros(dk.shape, wide)
        dv[...] = jnp.zeros(dv.shape, wide)
        tiles[...] = jnp.zeros(tiles.shape, wide)

    here = pl.ds(pl.multiple_of(block * QUERIES, QUERIES), QUERIES)
    scaled = (do_ref[0].astype(wide) * inv_ref[...]).astype(low)
    delta = jnp.sum(scaled.astype(wide) * o_ref[...], axis=0, keepdims=True)

    def slope(chunk, carry):
        rows = chunk_rows(chunk)
        part = jnp.dot(values[rows, :], scaled, preferred_element_type=wide)
        part = p_ref[rows, :].astype(wide) * (part - delta)
        slopes[rows, :] = part.astype(low)
        near = tile_rows(chunk, block)
        tiles[near, :] = tiles[near, :] + part
        return carry

    lax.fori_loop(0, LEN // CHUNK, slope, 0, unroll=2)
    grad_ref[0, :, here] = jnp.dot(
        qkv_ref[1], slopes[...], preferred_element_type=wide
    ).astype(low)
    queries = qkv_ref[0, :, here].T
    turned = scaled.T

    def gather(chunk, carry):
        rows = pl.ds(pl.multiple_of(chunk * 512, 512), 512)
        dk[rows, :] = dk[rows, :] + jnp.dot(
            slopes[rows, :], queries, preferred_element_type=wide
        )
        dv[rows, :] = dv[rows, :] + jnp.dot(p_ref[rows, :], turned, preferred_element_type=wide)
        return carry

    lax.fori_loop(0, LEN // 512, gather, 0)

    @pl.when(block == LEN // QUERIES - 1)
    def _():
        grad_ref[1] = dk[...].T.astype(low)
        grad_ref[2] = dv[...].T.astype(low)
        sums_ref[...] = tiles[...]


def attend_back(qkv, probs, out, inverse, grad_out):
    whole = lambda *shape: pl.BlockSpec(shape, lambda i: (0,) * len(shape))
    return pl.pallas_call(
        backward_kernel,
        grid=(LEN // QUERIES,),
        out_shape=(
            jax.ShapeDtypeStruct((3, HEAD_DIM, LEN), low),
            jax.ShapeDtypeStruct((6 * CHUNK, QUERIES), wide),
        ),
        in_specs=[
            whole(3, HEAD_DIM, LEN),
            pl.BlockSpec((LEN, QUERIES), lambda i: (0, i)),
            pl.BlockSpec((HEAD_DIM, QUERIES), lambda i: (0, i)),
            pl.BlockSpec((1, QUERIES), lambda i: (0, i)),
            pl.BlockSpec((1, HEAD_DIM, QUERIES), lambda i: (0, 0, i)),
        ],
        out_specs=(whole(3, HEAD_DIM, LEN), whole(6 * CHUNK, QUERIES)),
        scratch_shapes=[
            pltpu.VMEM((LEN, HEAD_DIM), low),
            pltpu.VMEM((LEN, HEAD_DIM), wide),
            pltpu.VMEM((LEN, HEAD_DIM), wide),
            pltpu.VMEM((6 * CHUNK, QUERIES), wide),
            pltpu.VMEM((LEN, QUERIES), low),
        ],
        compiler_params=pltpu.CompilerParams(vmem_limit_bytes=32 << 20),
    )(qkv, probs, out, inverse, grad_out)


def rms_scale(values_in, gain_vec):
    return (
        values_in
        * lax.rsqrt(jnp.mean(values_in * values_in, axis=-1, keepdims=True) + epsilon)
        * gain_vec
    )


def dot(a, b, dims=(1, 0)):
    return lax.dot_general(
        a, b, (((dims[0],), (dims[1],)), ((), ())), preferred_element_type=wide
    )


def shards(
    tokens,
    cotangent,
    routes,
    query_weight,
    kv_weight,
    out_weight,
    norm_gain_one,
    norm_gain_two,
    router_weight,
    bias_table,
    expert_in,
    expert_out,
):
    highest = lax.Precision.HIGHEST
    experts = 16
    x_rows = tokens[0].astype(wide)
    c = lax.axis_index("ctx")

    matrix = jnp.concatenate([query_weight, kv_weight, out_weight], axis=1).reshape(16, 1152)
    small = jnp.concatenate(
        [
            router_weight,
            norm_gain_one[:, None],
            norm_gain_two[:, None],
            jnp.pad(bias_table, (0, 3))[:, None],
        ],
        axis=1,
    ).reshape(1, 114)
    packed = jnp.concatenate([matrix, jnp.pad(small, ((0, 15), (0, 14)))], axis=1)
    eight = swap(packed, "exp", 1)
    block = jnp.concatenate(
        [
            eight[:, :, :1152].reshape(48, 4 * D),
            jnp.pad(eight[:, 0, 1152:1266].reshape(48, 19), ((0, 0), (0, 109))),
        ],
        axis=1,
    )
    full = gather_weights(block, 2).reshape(D, 4 * D + 128)
    experts_here = gather_experts(
        jnp.stack([jnp.swapaxes(expert_in, 1, 2), expert_out]), 3
    ).reshape(2, 2, D, D)
    qkv_full = full[:, : 3 * D]
    out_full = full[:, 3 * D : 4 * D]
    router_wide = full[:, 4 * D : 4 * D + 16].astype(wide)
    gain_one = full[:, 4 * D + 16].astype(wide)
    gain_two = full[:, 4 * D + 17].astype(wide)
    table = full[:, 4 * D + 18].astype(wide).reshape(128, 6)[:, :3].reshape(BUCKETS, HEADS)
    head = head_of(c)
    my_head = (jnp.arange(HEADS, dtype=jnp.int32) == head) & owns(c)
    head_table = jnp.sum(jnp.where(my_head[None, :], table, 0.0), axis=1)

    normed_one, norm_one_back = jax.vjp(rms_scale, x_rows, gain_one)
    h_one = normed_one.astype(low)
    qkv = dot(qkv_full, h_one, (0, 1)).astype(low).reshape(3, HEADS, HEAD_DIM, TOK)
    head_qkv = to_heads(qkv, 4)
    probs, attended, attended_head, inverse = attend(head_qkv, head_table)
    attended_low = from_heads(attended_head, 5).reshape(D, TOK)
    residual = x_rows + dot(attended_low, out_full, (0, 0))
    normed_two, norm_two_back = jax.vjp(rms_scale, residual, gain_two)
    h_two = normed_two.astype(low)
    h_two_wide = h_two.astype(wide)
    route_probs = jax.nn.softmax(jnp.dot(h_two_wide, router_wide, precision=highest), axis=-1)

    route_ids = routes[0, :, 0]
    choose = route_ids[:, None] == jnp.arange(experts, dtype=jnp.int32)[None, :]
    choose_wide = choose.astype(wide)
    index = jnp.arange(TOK, dtype=jnp.int32)
    before = (index[None, :] < index[:, None]).astype(low)
    earlier = dot(before, choose.astype(low))
    slot = jnp.sum(earlier * choose_wide, axis=1).astype(jnp.int32)
    target = route_ids // 2 * SLOTS + route_ids % 2 * CAP + slot
    target = jnp.concatenate([target, target + 2 * CAP])
    dispatch = (
        jnp.arange(EXP * SLOTS, dtype=jnp.int32)[:, None] == target[None, :]
    ).astype(low)
    gate_value = jnp.sum(route_probs * choose_wide, axis=1)
    grad_out = cotangent[0].astype(wide)
    grad_y = (gate_value[:, None] * grad_out).astype(low)
    outgoing = dot(dispatch, jnp.concatenate([h_two, grad_y])).astype(low)
    received = swap(outgoing.reshape(EXP, SLOTS, D), "exp", 6, 0).reshape(EXP * SLOTS, D)

    row = jnp.arange(4 * 80, dtype=jnp.int32)
    source = row % 80 // CAP * SLOTS + row // 80 * CAP + row % CAP
    compact = (source[:, None] == jnp.arange(EXP * SLOTS, dtype=jnp.int32)[None, :]).astype(low)
    lists = swap(dot(compact, received).astype(low), "z", 7).reshape(ZED, 4, 80, D)
    partial, grads_in, grads_out = [], [], []
    for n in range(2):
        rows = lists[:, n].reshape(ZED * 80, D)
        grads = lists[:, 2 + n].reshape(ZED * 80, D)
        weight_in, weight_out = experts_here[0, n], experts_here[1, n]
        pre_act = dot(rows, weight_in, (1, 1))
        hidden_wide, gelu_back = jax.vjp(jax.nn.gelu, pre_act)
        hidden = hidden_wide.astype(low)
        grad_hidden = dot(grads, weight_out, (1, 1))
        grad_pre = gelu_back(grad_hidden)[0].astype(low)
        partial.append(dot(hidden, weight_out).astype(low).reshape(ZED, 80, D))
        partial.append(dot(grad_pre, weight_in).astype(low).reshape(ZED, 80, D))
        grads_in.append(dot(grad_pre, rows, (0, 0)).astype(low))
        grads_out.append(dot(hidden, grads, (0, 0)).astype(low))
    partial = jnp.stack([partial[0], partial[2], partial[1], partial[3]], axis=1)
    summed = jnp.sum(
        swap(partial.reshape(ZED, 320, D), "z", 8, 0).astype(wide), axis=0
    ).astype(low)
    back = swap(dot(compact, summed, (0, 0)).astype(low).reshape(EXP, SLOTS, D), "exp", 9, 0)
    returned = dot(dispatch, back.reshape(EXP * SLOTS, D), (0, 0))
    expert_tokens, grad_h_two = returned[:TOK], returned[TOK:]

    mixed_rows = (residual + gate_value[:, None] * expert_tokens).astype(low)
    grad_gate = jnp.sum(grad_out * expert_tokens, axis=1)
    grad_choice = choose_wide * grad_gate[:, None]
    grad_logits = route_probs * (
        grad_choice - jnp.sum(route_probs * grad_choice, axis=1, keepdims=True)
    )
    grad_router = jnp.dot(h_two_wide.T, grad_logits, precision=highest)
    grad_h_two = grad_h_two + jnp.dot(grad_logits, router_wide.T, precision=highest)
    grad_resid_norm, grad_gain_two = norm_two_back(grad_h_two)
    grad_residual = grad_out + grad_resid_norm
    grad_branch = grad_residual.astype(low)
    grad_attended = dot(out_full, grad_branch, (1, 1)).astype(low)
    head_grad = to_heads(grad_attended.reshape(1, HEADS, HEAD_DIM, TOK), 10)
    head_grads, tile_sums = attend_back(head_qkv, probs, attended, inverse, head_grad)
    grad_qkv = from_heads(head_grads, 11).reshape(3 * D, TOK)

    expert_grads = jnp.stack([jnp.stack(grads_in), jnp.stack(grads_out)])
    expert_grads = swap(expert_grads.reshape(2, 2, 2, 2, 192, D), "core", 12, 3)
    expert_grads = jnp.sum(expert_grads.astype(wide), axis=0).astype(low)
    expert_grads = jnp.sum(swap(expert_grads, "x", 13, 2).astype(wide), axis=0)
    grad_expert_in = jnp.swapaxes(expert_grads[0], 1, 2)
    grad_expert_out = expert_grads[1]

    grad_h_one = dot(grad_qkv, qkv_full, (0, 1))
    grad_x_norm, grad_gain_one = norm_one_back(grad_h_one)
    grad_tokens = grad_residual + grad_x_norm
    bucket_sums = jnp.sum(
        jnp.where(
            near_buckets()[None] == jnp.arange(BUCKETS, dtype=jnp.int32)[:, None, None],
            tile_sums[None],
            0.0,
        ),
        axis=(1, 2),
    )
    grad_table = jnp.where(my_head[None, :], bucket_sums[:, None], 0.0)
    table_column = jnp.pad(grad_table.reshape(128, 3), ((0, 0), (0, 3))).reshape(D, 1)
    shared = jnp.concatenate(
        [
            dot(h_one, grad_qkv, (0, 1)).astype(low),
            dot(attended_low, grad_branch).astype(low),
            grad_router.astype(low),
            grad_gain_one[:, None].astype(low),
            grad_gain_two[:, None].astype(low),
            table_column.astype(low),
            jnp.zeros((D, 109), low),
        ],
        axis=1,
    )
    total = lambda v: jnp.sum(v.astype(wide), axis=0)
    shared = total(swap(shared.reshape(8, 2, 48, 3200), "core", 14, 1)).astype(low)
    shared = total(swap(shared.reshape(4, 2, 48, 3200), "z", 15, 0)).astype(low)
    shared = total(swap(shared, "x", 16, 0)).astype(low)
    lines = jnp.concatenate(
        [
            shared[:, : 4 * D].reshape(EXP, 16, 1152),
            jnp.pad(
                shared[:, 4 * D : 4 * D + 19].reshape(EXP, 1, 114), ((0, 0), (0, 15), (0, 14))
            ),
        ],
        axis=2,
    )
    lines = total(swap(lines, "exp", 17, 0))
    matrix = lines[:, :1152].reshape(6, 4 * D)
    small = lines[0, 1152:1266].reshape(6, 19)
    return (
        mixed_rows[None],
        grad_tokens[None],
        matrix[:, :D],
        matrix[:, D : 3 * D],
        matrix[:, 3 * D :],
        small[:, 16],
        small[:, 17],
        small[:, :16],
        small[:3, 18],
        grad_expert_in,
        grad_expert_out,
    )


def solution(mesh):
    rows = P("exp", "ctx", None)
    shared, vector = P(("ctx", "exp"), None), P(("ctx", "exp"))
    expert_in, expert_out = P("exp", None, "ctx"), P("exp", "ctx", None)
    return jax.shard_map(
        shards,
        mesh=mesh,
        in_specs=(rows, rows, rows, shared, shared, shared, vector, vector, shared, vector)
        + (expert_in, expert_out),
        out_specs=(rows, rows, shared, shared, shared, vector, vector, shared, vector)
        + (expert_in, expert_out),
        check_vma=False,
    )
```

```python
import functools

import jax
import jax.numpy as jnp
from jax import lax
from jax.experimental import pallas as pl
from jax.experimental.pallas import tpu as pltpu
from jax.sharding import PartitionSpec as P

MESH = pl.DeviceIdType.MESH
HEADS = 12
HEAD_DIM = 64
BUCKETS = 32
TOK = 128
D = 768
CAP = 10
SLOTS = 48
CTX, EXP, ZED = 16, 8, 4
LEN = TOK * CTX
QUERIES = 256
CHUNK = 128
epsilon = 1e-06
bucket_edges = (12, 16, 23, 32, 46, 64, 91)
low = jnp.bfloat16
wide = jnp.float32
ANY = pl.BlockSpec(memory_space=pl.ANY)


def spot():
    c, e = lax.axis_index("ctx"), lax.axis_index("exp")
    return c, e, c // 4, (c // 2) % 2, c % 2


def greet(peers):
    barrier = pltpu.get_barrier_semaphore()
    for peer in peers:
        pl.semaphore_signal(barrier, inc=1, device_id=peer, device_id_type=MESH)
    pl.semaphore_wait(barrier, len(peers))


def push(src, dst, send, recv, to):
    return pltpu.make_async_remote_copy(
        src_ref=src, dst_ref=dst, send_sem=send, recv_sem=recv, device_id=to, device_id_type=MESH
    )


def group(kind):
    c, e, z, xh, k = spot()
    if kind == "exp":
        return EXP, e, lambda i: (c, i)
    if kind == "z":
        return ZED, z, lambda i: (i * 4 + xh * 2 + k, e)
    if kind == "x":
        return 2, xh, lambda i: (z * 4 + i * 2 + k, e)
    return 2, k, lambda i: (z * 4 + xh * 2 + i, e)


SIZES = {"exp": EXP, "z": ZED, "x": 2, "core": 2}


def swaps_kernel(plan, *refs):
    n = len(plan)
    xs, outs, (send, recv, here) = refs[:n], refs[n : 2 * n], refs[2 * n :]
    peers = {}
    for kind, axis, keep in plan:
        size, me, device = group(kind)
        peers[kind] = [device(lax.rem(me + i, size)) for i in range(1, size)]
    greet([p for kind in peers for p in peers[kind]])
    copies, count = [], 0
    for (kind, axis, keep), x, out in zip(plan, xs, outs):
        size, me, device = group(kind)
        part = (lambda i: x) if axis is None else (lambda i: x.at[(slice(None),) * axis + (i,)])
        for i in range(1, size):
            to = lax.rem(me + i, size)
            slot = me if keep else i - 1
            copy = push(part(to), out.at[slot], send.at[count], recv.at[count], device(to))
            copy.start()
            copies.append(copy)
            count += 1
    for n, ((kind, axis, keep), x, out) in enumerate(zip(plan, xs, outs)):
        if keep:
            size, me, device = group(kind)
            own = x if axis is None else x.at[(slice(None),) * axis + (me,)]
            copy = pltpu.make_async_copy(own, out.at[me], here.at[n])
            copy.start()
            copies.append(copy)
    for copy in copies:
        copy.wait()


def swaps(ident, *items):
    shapes, total = [], 0
    for x, kind, axis, keep in items:
        block = x.shape if axis is None else x.shape[:axis] + x.shape[axis + 1 :]
        shapes.append(jax.ShapeDtypeStruct((SIZES[kind] - (not keep), *block), x.dtype))
        total += SIZES[kind] - 1
    return pl.pallas_call(
        functools.partial(swaps_kernel, [item[1:] for item in items]),
        out_shape=shapes,
        in_specs=[ANY] * len(items),
        out_specs=[ANY] * len(items),
        scratch_shapes=[
            pltpu.SemaphoreType.DMA((total,)),
            pltpu.SemaphoreType.DMA((total,)),
            pltpu.SemaphoreType.DMA((len(items),)),
        ],
        compiler_params=pltpu.CompilerParams(collective_id=ident, has_side_effects=True),
    )(*[item[0] for item in items])


def swap(x, kind, ident, axis=None):
    return swaps(ident, (x, kind, axis, True))[0]


def add_up(x, kind, axis, others):
    mine = lax.dynamic_index_in_dim(x, group(kind)[1], axis, keepdims=False)
    return mine.astype(wide) + jnp.sum(others.astype(wide), axis=0)


def weights_kernel(x, w, out, wide_out, here, send, recv):
    c, e, z, xh, k = spot()
    zs = [lax.rem(z + i, 4) for i in range(1, 4)]
    back = [lax.rem(z + 4 - i, 4) for i in range(1, 4)]
    at = lambda z, xh, k: z * 4 + xh * 2 + k
    side, twin = (at(z, 1 - xh, k), e), (at(z, xh, 1 - k), e)
    rows = [(at(p, xh, k), e) for p in zs]
    greet([side, twin, *rows])
    mine, theirs = at(z, xh, k), at(z, 1 - xh, k)
    across = push(x, out.at[mine], send.at[0], recv.at[0], side)
    across.start()
    first = [push(x, out.at[mine], send.at[1 + i], recv.at[1 + i], d) for i, d in enumerate(rows)]
    for copy in first:
        copy.start()
    own = pltpu.make_async_copy(x, out.at[mine], here.at[0])
    own.start()
    pair = [push(x, out.at[mine], send.at[7], recv.at[7], twin)]
    pair[0].start()
    slab = lambda xh, k: wide_out.at[:, :, xh * 2 + k]
    w_across = push(w, slab(xh, k), send.at[15], recv.at[15], side)
    w_across.start()
    pair.append(push(w, slab(xh, k), send.at[16], recv.at[16], twin))
    pair[1].start()
    w_own = pltpu.make_async_copy(w, slab(xh, k), here.at[1])
    w_own.start()

    def hand(n, block):
        copy = push(out.at[block], out.at[block], send.at[7 + n], recv.at[7 + n], twin)
        copy.start()
        pair.append(copy)

    across.wait_recv()
    second = [
        push(out.at[theirs], out.at[theirs], send.at[4 + i], recv.at[4 + i], d)
        for i, d in enumerate(rows)
    ]
    for copy in second:
        copy.start()
    hand(1, theirs)
    for i, p in enumerate(back):
        first[i].wait_recv()
        hand(2 + i, at(p, xh, k))
    w_across.wait_recv()
    other = slab(1 - xh, k)
    pair.append(push(other, other, send.at[17], recv.at[17], twin))
    pair[-1].start()
    for i, p in enumerate(back):
        second[i].wait_recv()
        hand(5 + i, at(p, 1 - xh, k))
    for copy in pair:
        copy.wait()
    across.wait_send()
    w_across.wait_send()
    for copy in first + second:
        copy.wait_send()
    own.wait()
    w_own.wait()


def gather_weights(x, w, ident):
    return pl.pallas_call(
        weights_kernel,
        out_shape=(
            jax.ShapeDtypeStruct((CTX, *x.shape), x.dtype),
            jax.ShapeDtypeStruct((2, 2, 4, *w.shape[2:]), w.dtype),
        ),
        in_specs=[ANY, pl.BlockSpec(memory_space=pltpu.VMEM)],
        out_specs=(ANY, ANY),
        scratch_shapes=[
            pltpu.SemaphoreType.DMA((2,)),
            pltpu.SemaphoreType.DMA((18,)),
            pltpu.SemaphoreType.DMA((18,)),
        ],
        compiler_params=pltpu.CompilerParams(
            collective_id=ident, has_side_effects=True, vmem_limit_bytes=16 << 20
        ),
    )(x, w)


def head_of(c):
    return jnp.minimum((c // 4) * 3 + c % 4, HEADS - 1)


def owns(c):
    return c % 4 < 3


def columns(c):
    return pl.ds(pl.multiple_of(c * TOK, TOK), TOK)


def to_heads_kernel(x, out, here, send, recv):
    c, e, z, xh, k = spot()
    peers = [lax.rem(c + i, CTX) for i in range(1, CTX)]
    greet([(p, e) for p in peers])
    copies = [
        push(x.at[:, head_of(p)], out.at[:, :, columns(c)], send.at[i], recv.at[i], (p, e))
        for i, p in enumerate(peers)
    ]
    own = pltpu.make_async_copy(x.at[:, head_of(c)], out.at[:, :, columns(c)], here)
    for p, copy in zip(peers, copies):
        pl.when(owns(p))(copy.start)
    pl.when(owns(c))(own.start)
    for p, copy in zip(peers, copies):
        pl.when(owns(p))(copy.wait_send)
        pl.when(owns(c))(copy.wait_recv)
    pl.when(owns(c))(own.wait)


def from_heads_kernel(x, out, here, send, recv):
    c, e, z, xh, k = spot()
    peers = [lax.rem(c + i, CTX) for i in range(1, CTX)]
    sources = [lax.rem(c + CTX - i, CTX) for i in range(1, CTX)]
    greet([(p, e) for p in peers])
    copies = [
        push(x.at[:, :, columns(p)], out.at[:, head_of(c)], send.at[i], recv.at[i], (p, e))
        for i, p in enumerate(peers)
    ]
    own = pltpu.make_async_copy(x.at[:, :, columns(c)], out.at[:, head_of(c)], here)

    @pl.when(owns(c))
    def _():
        for copy in copies:
            copy.start()
        own.start()

    for s, copy in zip(sources, copies):
        pl.when(owns(c))(copy.wait_send)
        pl.when(owns(s))(copy.wait_recv)
    pl.when(owns(c))(own.wait)


def heads_call(kernel, x, shape, ident):
    return pl.pallas_call(
        kernel,
        out_shape=jax.ShapeDtypeStruct(shape, x.dtype),
        in_specs=[ANY],
        out_specs=ANY,
        scratch_shapes=[
            pltpu.SemaphoreType.DMA,
            pltpu.SemaphoreType.DMA((CTX - 1,)),
            pltpu.SemaphoreType.DMA((CTX - 1,)),
        ],
        compiler_params=pltpu.CompilerParams(collective_id=ident, has_side_effects=True),
    )(x)


def to_heads(x, ident):
    return heads_call(to_heads_kernel, x, (x.shape[0], HEAD_DIM, LEN), ident)


def from_heads(x, ident):
    return heads_call(from_heads_kernel, x, (x.shape[0], HEADS, HEAD_DIM, TOK), ident)


def near_buckets():
    shape = (6 * CHUNK, QUERIES)
    offset = (
        lax.broadcasted_iota(jnp.int32, shape, 0)
        - 2 * CHUNK
        - lax.broadcasted_iota(jnp.int32, shape, 1)
    )
    distance = jnp.abs(offset)
    far = jnp.full(shape, 8, jnp.int32)
    for edge in bucket_edges:
        far = far + (distance >= edge).astype(jnp.int32)
    return jnp.where(distance < 8, distance, far) + jnp.where(offset > 0, BUCKETS // 2, 0)


def tile_rows(chunk, block):
    tile = jnp.clip(chunk - 2 * block + 2, 0, 5)
    return pl.ds(pl.multiple_of(tile * CHUNK, CHUNK), CHUNK)


def chunk_rows(chunk):
    return pl.ds(pl.multiple_of(chunk * CHUNK, CHUNK), CHUNK)


def forward_kernel(qkv_ref, table_ref, p_ref, o_ref, low_ref, inv_ref, keys, bias, scores):
    block = pl.program_id(0)

    @pl.when(block == 0)
    def _():
        keys[...] = qkv_ref[1].T
        ids = near_buckets()
        tiles = jnp.zeros(ids.shape, wide)
        for b in range(BUCKETS):
            tiles = jnp.where(ids == b, table_ref[b], tiles)
        bias[...] = tiles

    here = pl.ds(pl.multiple_of(block * QUERIES, QUERIES), QUERIES)
    queries = qkv_ref[0, :, here]

    def score(chunk, top):
        rows = chunk_rows(chunk)
        part = jnp.dot(keys[rows, :], queries, preferred_element_type=wide)
        part = part + bias[tile_rows(chunk, block), :]
        scores[rows, :] = part
        return jnp.maximum(top, jnp.max(part.reshape(CHUNK // 8, 8, QUERIES), axis=0))

    top = lax.fori_loop(
        0, LEN // CHUNK, score, jnp.full((8, QUERIES), -1e30, wide), unroll=2
    )
    top = jnp.max(top, axis=0, keepdims=True)

    def weigh(chunk, total):
        rows = chunk_rows(chunk)
        part = jnp.exp(scores[rows, :] - top)
        p_ref[rows, :] = part.astype(low)
        return total + jnp.sum(part.reshape(CHUNK // 8, 8, QUERIES), axis=0)

    total = lax.fori_loop(0, LEN // CHUNK, weigh, jnp.zeros((8, QUERIES), wide), unroll=2)
    inverse = 1.0 / jnp.sum(total, axis=0, keepdims=True)
    out = jnp.dot(qkv_ref[2], p_ref[...], preferred_element_type=wide) * inverse
    o_ref[...] = out
    low_ref[0] = out.astype(low)
    inv_ref[...] = inverse


def attend(qkv, table):
    whole = lambda *shape: pl.BlockSpec(shape, lambda i: (0,) * len(shape))
    return pl.pallas_call(
        forward_kernel,
        grid=(LEN // QUERIES,),
        out_shape=(
            jax.ShapeDtypeStruct((LEN, LEN), low),
            jax.ShapeDtypeStruct((HEAD_DIM, LEN), wide),
            jax.ShapeDtypeStruct((1, HEAD_DIM, LEN), low),
            jax.ShapeDtypeStruct((1, LEN), wide),
        ),
        in_specs=[whole(3, HEAD_DIM, LEN), pl.BlockSpec(memory_space=pltpu.SMEM)],
        out_specs=(
            pl.BlockSpec((LEN, QUERIES), lambda i: (0, i)),
            pl.BlockSpec((HEAD_DIM, QUERIES), lambda i: (0, i)),
            pl.BlockSpec((1, HEAD_DIM, QUERIES), lambda i: (0, 0, i)),
            pl.BlockSpec((1, QUERIES), lambda i: (0, i)),
        ),
        scratch_shapes=[
            pltpu.VMEM((LEN, HEAD_DIM), low),
            pltpu.VMEM((6 * CHUNK, QUERIES), wide),
            pltpu.VMEM((LEN, QUERIES), wide),
        ],
        compiler_params=pltpu.CompilerParams(vmem_limit_bytes=32 << 20),
    )(qkv, table)


def backward_kernel(
    qkv_ref, p_ref, o_ref, inv_ref, do_ref, grad_ref, sums_ref, values, dk, dv, tiles, slopes
):
    block = pl.program_id(0)

    @pl.when(block == 0)
    def _():
        values[...] = qkv_ref[2].T
        dk[...] = jnp.zeros(dk.shape, wide)
        dv[...] = jnp.zeros(dv.shape, wide)
        tiles[...] = jnp.zeros(tiles.shape, wide)

    here = pl.ds(pl.multiple_of(block * QUERIES, QUERIES), QUERIES)
    scaled = (do_ref[0].astype(wide) * inv_ref[...]).astype(low)
    delta = jnp.sum(scaled.astype(wide) * o_ref[...], axis=0, keepdims=True)

    def slope(chunk, carry):
        rows = chunk_rows(chunk)
        part = jnp.dot(values[rows, :], scaled, preferred_element_type=wide)
        part = p_ref[rows, :].astype(wide) * (part - delta)
        slopes[rows, :] = part.astype(low)
        near = tile_rows(chunk, block)
        tiles[near, :] = tiles[near, :] + part
        return carry

    lax.fori_loop(0, LEN // CHUNK, slope, 0, unroll=2)
    grad_ref[0, :, here] = jnp.dot(
        qkv_ref[1], slopes[...], preferred_element_type=wide
    ).astype(low)
    queries = qkv_ref[0, :, here].T
    turned = scaled.T

    def gather(chunk, carry):
        rows = pl.ds(pl.multiple_of(chunk * 512, 512), 512)
        dk[rows, :] = dk[rows, :] + jnp.dot(
            slopes[rows, :], queries, preferred_element_type=wide
        )
        dv[rows, :] = dv[rows, :] + jnp.dot(p_ref[rows, :], turned, preferred_element_type=wide)
        return carry

    lax.fori_loop(0, LEN // 512, gather, 0)

    @pl.when(block == LEN // QUERIES - 1)
    def _():
        grad_ref[1] = dk[...].T.astype(low)
        grad_ref[2] = dv[...].T.astype(low)
        sums_ref[...] = tiles[...]


def attend_back(qkv, probs, out, inverse, grad_out):
    whole = lambda *shape: pl.BlockSpec(shape, lambda i: (0,) * len(shape))
    return pl.pallas_call(
        backward_kernel,
        grid=(LEN // QUERIES,),
        out_shape=(
            jax.ShapeDtypeStruct((3, HEAD_DIM, LEN), low),
            jax.ShapeDtypeStruct((6 * CHUNK, QUERIES), wide),
        ),
        in_specs=[
            whole(3, HEAD_DIM, LEN),
            pl.BlockSpec((LEN, QUERIES), lambda i: (0, i)),
            pl.BlockSpec((HEAD_DIM, QUERIES), lambda i: (0, i)),
            pl.BlockSpec((1, QUERIES), lambda i: (0, i)),
            pl.BlockSpec((1, HEAD_DIM, QUERIES), lambda i: (0, 0, i)),
        ],
        out_specs=(whole(3, HEAD_DIM, LEN), whole(6 * CHUNK, QUERIES)),
        scratch_shapes=[
            pltpu.VMEM((LEN, HEAD_DIM), low),
            pltpu.VMEM((LEN, HEAD_DIM), wide),
            pltpu.VMEM((LEN, HEAD_DIM), wide),
            pltpu.VMEM((6 * CHUNK, QUERIES), wide),
            pltpu.VMEM((LEN, QUERIES), low),
        ],
        compiler_params=pltpu.CompilerParams(vmem_limit_bytes=32 << 20),
    )(qkv, probs, out, inverse, grad_out)


def rms_scale(values_in, gain_vec):
    return (
        values_in
        * lax.rsqrt(jnp.mean(values_in * values_in, axis=-1, keepdims=True) + epsilon)
        * gain_vec
    )


def dot(a, b, dims=(1, 0)):
    return lax.dot_general(
        a, b, (((dims[0],), (dims[1],)), ((), ())), preferred_element_type=wide
    )


def shards(
    tokens,
    cotangent,
    routes,
    query_weight,
    kv_weight,
    out_weight,
    norm_gain_one,
    norm_gain_two,
    router_weight,
    bias_table,
    expert_in,
    expert_out,
):
    highest = lax.Precision.HIGHEST
    experts = 16
    x_rows = tokens[0].astype(wide)
    c = lax.axis_index("ctx")

    matrix = jnp.concatenate([query_weight, kv_weight, out_weight], axis=1).reshape(16, 1152)
    small = jnp.concatenate(
        [
            router_weight,
            norm_gain_one[:, None],
            norm_gain_two[:, None],
            jnp.pad(bias_table, (0, 3))[:, None],
        ],
        axis=1,
    ).reshape(1, 114)
    packed = jnp.concatenate([matrix, jnp.pad(small, ((0, 15), (0, 14)))], axis=1)
    eight = swap(packed, "exp", 1)
    block = jnp.concatenate(
        [
            eight[:, :, :1152].reshape(48, 4 * D),
            jnp.pad(eight[:, 0, 1152:1266].reshape(48, 19), ((0, 0), (0, 109))),
        ],
        axis=1,
    )
    experts_local = jnp.stack([jnp.swapaxes(expert_in, 1, 2), expert_out])
    full, experts_here = gather_weights(block, experts_local, 2)
    full = full.reshape(D, 4 * D + 128)
    experts_here = experts_here.reshape(2, 2, D, D)
    qkv_full = full[:, : 3 * D]
    out_full = full[:, 3 * D : 4 * D]
    router_wide = full[:, 4 * D : 4 * D + 16].astype(wide)
    gain_one = full[:, 4 * D + 16].astype(wide)
    gain_two = full[:, 4 * D + 17].astype(wide)
    table = full[:, 4 * D + 18].astype(wide).reshape(128, 6)[:, :3].reshape(BUCKETS, HEADS)
    head = head_of(c)
    my_head = (jnp.arange(HEADS, dtype=jnp.int32) == head) & owns(c)
    head_table = jnp.sum(jnp.where(my_head[None, :], table, 0.0), axis=1)

    normed_one, norm_one_back = jax.vjp(rms_scale, x_rows, gain_one)
    h_one = normed_one.astype(low)
    qkv = dot(qkv_full, h_one, (0, 1)).astype(low).reshape(3, HEADS, HEAD_DIM, TOK)
    head_qkv = to_heads(qkv, 4)
    probs, attended, attended_head, inverse = attend(head_qkv, head_table)
    attended_low = from_heads(attended_head, 5).reshape(D, TOK)
    residual = x_rows + dot(attended_low, out_full, (0, 0))
    normed_two, norm_two_back = jax.vjp(rms_scale, residual, gain_two)
    h_two = normed_two.astype(low)
    h_two_wide = h_two.astype(wide)
    route_probs = jax.nn.softmax(jnp.dot(h_two_wide, router_wide, precision=highest), axis=-1)

    route_ids = routes[0, :, 0]
    choose = route_ids[:, None] == jnp.arange(experts, dtype=jnp.int32)[None, :]
    choose_wide = choose.astype(wide)
    index = jnp.arange(TOK, dtype=jnp.int32)
    before = (index[None, :] < index[:, None]).astype(low)
    earlier = dot(before, choose.astype(low))
    slot = jnp.sum(earlier * choose_wide, axis=1).astype(jnp.int32)
    target = route_ids // 2 * SLOTS + route_ids % 2 * CAP + slot
    target = jnp.concatenate([target, target + 2 * CAP])
    dispatch = (
        jnp.arange(EXP * SLOTS, dtype=jnp.int32)[:, None] == target[None, :]
    ).astype(low)
    gate_value = jnp.sum(route_probs * choose_wide, axis=1)
    grad_out = cotangent[0].astype(wide)
    grad_y = (gate_value[:, None] * grad_out).astype(low)
    outgoing = dot(dispatch, jnp.concatenate([h_two, grad_y])).astype(low)
    received = swap(outgoing.reshape(EXP, SLOTS, D), "exp", 6, 0).reshape(EXP * SLOTS, D)

    row = jnp.arange(4 * 80, dtype=jnp.int32)
    source = row % 80 // CAP * SLOTS + row // 80 * CAP + row % CAP
    compact = (source[:, None] == jnp.arange(EXP * SLOTS, dtype=jnp.int32)[None, :]).astype(low)
    lists = swap(dot(compact, received).astype(low), "z", 7).reshape(ZED, 4, 80, D)
    partial, grads_in, grads_out = [], [], []
    for n in range(2):
        rows = lists[:, n].reshape(ZED * 80, D)
        grads = lists[:, 2 + n].reshape(ZED * 80, D)
        weight_in, weight_out = experts_here[0, n], experts_here[1, n]
        pre_act = dot(rows, weight_in, (1, 1))
        hidden_wide, gelu_back = jax.vjp(jax.nn.gelu, pre_act)
        hidden = hidden_wide.astype(low)
        grad_hidden = dot(grads, weight_out, (1, 1))
        grad_pre = gelu_back(grad_hidden)[0].astype(low)
        partial.append(dot(hidden, weight_out).astype(low).reshape(ZED, 80, D))
        partial.append(dot(grad_pre, weight_in).astype(low).reshape(ZED, 80, D))
        grads_in.append(dot(grad_pre, rows, (0, 0)).astype(low))
        grads_out.append(dot(hidden, grads, (0, 0)).astype(low))
    partial = jnp.stack([partial[0], partial[2], partial[1], partial[3]], axis=1)
    partial = partial.reshape(ZED, 320, D)
    summed = add_up(partial, "z", 0, swaps(8, (partial, "z", 0, False))[0]).astype(low)
    spread = dot(compact, summed, (0, 0)).astype(low).reshape(EXP, SLOTS, D)
    expert_grads = jnp.stack([jnp.stack(grads_in), jnp.stack(grads_out)])
    expert_grads = expert_grads.reshape(2, 2, 2, 2, 192, D)
    back, others = swaps(9, (spread, "exp", 0, True), (expert_grads, "core", 3, False))
    expert_grads = add_up(expert_grads, "core", 3, others).astype(low)
    returned = dot(dispatch, back.reshape(EXP * SLOTS, D), (0, 0))
    expert_tokens, grad_h_two = returned[:TOK], returned[TOK:]

    mixed_rows = (residual + gate_value[:, None] * expert_tokens).astype(low)
    grad_gate = jnp.sum(grad_out * expert_tokens, axis=1)
    grad_choice = choose_wide * grad_gate[:, None]
    grad_logits = route_probs * (
        grad_choice - jnp.sum(route_probs * grad_choice, axis=1, keepdims=True)
    )
    grad_router = jnp.dot(h_two_wide.T, grad_logits, precision=highest)
    grad_h_two = grad_h_two + jnp.dot(grad_logits, router_wide.T, precision=highest)
    grad_resid_norm, grad_gain_two = norm_two_back(grad_h_two)
    grad_residual = grad_out + grad_resid_norm
    grad_branch = grad_residual.astype(low)
    grad_attended = dot(out_full, grad_branch, (1, 1)).astype(low)
    head_grad = to_heads(grad_attended.reshape(1, HEADS, HEAD_DIM, TOK), 10)
    head_grads, tile_sums = attend_back(head_qkv, probs, attended, inverse, head_grad)
    grad_qkv = from_heads(head_grads, 11).reshape(3 * D, TOK)

    grad_h_one = dot(grad_qkv, qkv_full, (0, 1))
    grad_x_norm, grad_gain_one = norm_one_back(grad_h_one)
    grad_tokens = grad_residual + grad_x_norm
    bucket_sums = jnp.sum(
        jnp.where(
            near_buckets()[None] == jnp.arange(BUCKETS, dtype=jnp.int32)[:, None, None],
            tile_sums[None],
            0.0,
        ),
        axis=(1, 2),
    )
    grad_table = jnp.where(my_head[None, :], bucket_sums[:, None], 0.0)
    table_column = jnp.pad(grad_table.reshape(128, 3), ((0, 0), (0, 3))).reshape(D, 1)
    shared = jnp.concatenate(
        [
            dot(h_one, grad_qkv, (0, 1)).astype(low),
            dot(attended_low, grad_branch).astype(low),
            grad_router.astype(low),
            grad_gain_one[:, None].astype(low),
            grad_gain_two[:, None].astype(low),
            table_column.astype(low),
            jnp.zeros((D, 109), low),
        ],
        axis=1,
    )
    shared = shared.reshape(8, 2, 48, 3200)
    shared = add_up(shared, "core", 1, swaps(14, (shared, "core", 1, False))[0])
    shared = shared.astype(low).reshape(4, 2, 48, 3200)
    others, expert_others = swaps(15, (shared, "z", 0, False), (expert_grads, "x", 2, False))
    expert_grads = add_up(expert_grads, "x", 2, expert_others)
    grad_expert_in = jnp.swapaxes(expert_grads[0], 1, 2)
    grad_expert_out = expert_grads[1]
    shared = add_up(shared, "z", 0, others).astype(low)
    shared = add_up(shared, "x", 0, swaps(16, (shared, "x", 0, False))[0]).astype(low)
    lines = jnp.concatenate(
        [
            shared[:, : 4 * D].reshape(EXP, 16, 1152),
            jnp.pad(
                shared[:, 4 * D : 4 * D + 19].reshape(EXP, 1, 114), ((0, 0), (0, 15), (0, 14))
            ),
        ],
        axis=2,
    )
    lines = add_up(lines, "exp", 0, swaps(17, (lines, "exp", 0, False))[0])
    matrix = lines[:, :1152].reshape(6, 4 * D)
    small = lines[0, 1152:1266].reshape(6, 19)
    return (
        mixed_rows[None],
        grad_tokens[None],
        matrix[:, :D],
        matrix[:, D : 3 * D],
        matrix[:, 3 * D :],
        small[:, 16],
        small[:, 17],
        small[:, :16],
        small[:3, 18],
        grad_expert_in,
        grad_expert_out,
    )


def solution(mesh):
    rows = P("exp", "ctx", None)
    shared, vector = P(("ctx", "exp"), None), P(("ctx", "exp"))
    expert_in, expert_out = P("exp", None, "ctx"), P("exp", "ctx", None)
    return jax.shard_map(
        shards,
        mesh=mesh,
        in_specs=(rows, rows, rows, shared, shared, shared, vector, vector, shared, vector)
        + (expert_in, expert_out),
        out_specs=(rows, rows, shared, shared, shared, vector, vector, shared, vector)
        + (expert_in, expert_out),
        check_vma=False,
    )
```

```python
import functools

import jax
import jax.numpy as jnp
from jax import lax
from jax.experimental import pallas as pl
from jax.experimental.pallas import tpu as pltpu
from jax.sharding import PartitionSpec as P

MESH = pl.DeviceIdType.MESH
HEADS = 12
HEAD_DIM = 64
BUCKETS = 32
TOK = 128
D = 768
CAP = 10
SLOTS = 48
CTX, EXP, ZED = 16, 8, 4
LEN = TOK * CTX
QUERIES = 256
CHUNK = 128
epsilon = 1e-06
bucket_edges = (12, 16, 23, 32, 46, 64, 91)
low = jnp.bfloat16
wide = jnp.float32
ANY = pl.BlockSpec(memory_space=pl.ANY)


def spot():
    c, e = lax.axis_index("ctx"), lax.axis_index("exp")
    return c, e, c // 4, (c // 2) % 2, c % 2


def greet(peers):
    barrier = pltpu.get_barrier_semaphore()
    for peer in peers:
        pl.semaphore_signal(barrier, inc=1, device_id=peer, device_id_type=MESH)
    pl.semaphore_wait(barrier, len(peers))


def push(src, dst, send, recv, to):
    return pltpu.make_async_remote_copy(
        src_ref=src, dst_ref=dst, send_sem=send, recv_sem=recv, device_id=to, device_id_type=MESH
    )


def group(kind):
    c, e, z, xh, k = spot()
    if kind == "exp":
        return EXP, e, lambda i: (c, i)
    if kind == "z":
        return ZED, z, lambda i: (i * 4 + xh * 2 + k, e)
    if kind == "x":
        return 2, xh, lambda i: (z * 4 + i * 2 + k, e)
    if kind == "core":
        return 2, k, lambda i: (z * 4 + xh * 2 + i, e)
    if kind == "quad":
        return 4, xh * 2 + k, lambda i: (z * 4 + i, e)
    return CTX, c, lambda i: (i, e)


SIZES = {"exp": EXP, "z": ZED, "x": 2, "core": 2, "quad": 4}


def head_of(c):
    return jnp.minimum((c // 4) * 3 + c % 4, HEADS - 1)


def owns(c):
    return c % 4 < 3


def columns(c):
    return pl.ds(pl.multiple_of(c * TOK, TOK), TOK)


def when(condition, step):
    if condition is None:
        step()
    else:
        pl.when(condition)(step)


def heads_parts(kind, me, x, out):
    if kind == "to_heads":
        return lambda to: x.at[:, head_of(to)], out.at[:, :, columns(me)], None, owns
    if kind == "from_heads":
        return lambda to: x.at[:, :, columns(to)], out.at[:, head_of(me)], owns, None
    return lambda to: x.at[to], out.at[head_of(me)], owns, None


def swaps_kernel(plan, *refs):
    n = len(plan)
    xs, outs, (send, recv, here) = refs[:n], refs[n : 2 * n], refs[2 * n :]
    kinds = dict.fromkeys("ctx" if kind not in SIZES else kind for kind, axis, keep in plan)
    if "ctx" in kinds:
        kinds = [kind for kind in kinds if kind in ("ctx", "exp")]
    peers = []
    for kind in kinds:
        size, me, device = group(kind)
        peers += [device(lax.rem(me + i, size)) for i in range(1, size)]
    greet(peers)
    copies, count = [], 0
    for (kind, axis, keep), x, out in zip(plan, xs, outs):
        size, me, device = group(kind)
        if kind in SIZES:
            part = lambda i: x if axis is None else x.at[(slice(None),) * axis + (i,)]
            sends = receives = None
        else:
            part, place, sends, receives = heads_parts(kind, me, x, out)
        for i in range(1, size):
            to, source = lax.rem(me + i, size), lax.rem(me + size - i, size)
            if kind in SIZES:
                place = out.at[me if keep else i - 1]
            copy = push(part(to), place, send.at[count], recv.at[count], device(to))
            if sends is not None:
                out_if, in_if = sends(me), sends(source)
            elif receives is not None:
                out_if, in_if = receives(to), receives(me)
            else:
                out_if = in_if = None
            when(out_if, copy.start)
            copies.append((copy, out_if, in_if))
            count += 1
    own = []
    for n, ((kind, axis, keep), x, out) in enumerate(zip(plan, xs, outs)):
        size, me, device = group(kind)
        if kind in SIZES and keep:
            part = x if axis is None else x.at[(slice(None),) * axis + (me,)]
            own.append((pltpu.make_async_copy(part, out.at[me], here.at[n]), None))
        elif kind not in SIZES:
            part, place, sends, receives = heads_parts(kind, me, x, out)
            own.append((pltpu.make_async_copy(part(me), place, here.at[n]), owns(me)))
    for copy, condition in own:
        when(condition, copy.start)
    for copy, out_if, in_if in copies:
        when(out_if, copy.wait_send)
        when(in_if, copy.wait_recv)
    for copy, condition in own:
        when(condition, copy.wait)


def swaps(ident, *items):
    shapes, total = [], 0
    for x, kind, axis, keep in items:
        block = x.shape if axis is None else x.shape[:axis] + x.shape[axis + 1 :]
        if kind == "to_heads":
            shape = (x.shape[0], HEAD_DIM, LEN)
        elif kind == "from_heads":
            shape = (x.shape[0], HEADS, HEAD_DIM, TOK)
        elif kind == "head_rows":
            shape = (HEADS, *x.shape[1:])
        else:
            shape = (SIZES[kind] - (not keep), *block)
        shapes.append(jax.ShapeDtypeStruct(shape, x.dtype))
        total += SIZES.get(kind, CTX) - 1
    return pl.pallas_call(
        functools.partial(swaps_kernel, [item[1:] for item in items]),
        out_shape=shapes,
        in_specs=[ANY] * len(items),
        out_specs=[ANY] * len(items),
        scratch_shapes=[
            pltpu.SemaphoreType.DMA((total,)),
            pltpu.SemaphoreType.DMA((total,)),
            pltpu.SemaphoreType.DMA((len(items),)),
        ],
        compiler_params=pltpu.CompilerParams(collective_id=ident, has_side_effects=True),
    )(*[item[0] for item in items])


def swap(x, kind, ident, axis=None):
    return swaps(ident, (x, kind, axis, True))[0]


def add_up(x, kind, axis, others):
    mine = lax.dynamic_index_in_dim(x, group(kind)[1], axis, keepdims=False)
    return mine.astype(wide) + jnp.sum(others.astype(wide), axis=0)


def weights_kernel(x, w, out, wide_out, here, send, recv):
    c, e, z, xh, k = spot()
    zs = [lax.rem(z + i, 4) for i in range(1, 4)]
    back = [lax.rem(z + 4 - i, 4) for i in range(1, 4)]
    at = lambda z, xh, k: z * 4 + xh * 2 + k
    side, twin = (at(z, 1 - xh, k), e), (at(z, xh, 1 - k), e)
    rows = [(at(p, xh, k), e) for p in zs]
    greet([side, twin, *rows])
    mine, theirs = at(z, xh, k), at(z, 1 - xh, k)
    across = push(x, out.at[mine], send.at[0], recv.at[0], side)
    across.start()
    first = [push(x, out.at[mine], send.at[1 + i], recv.at[1 + i], d) for i, d in enumerate(rows)]
    for copy in first:
        copy.start()
    own = pltpu.make_async_copy(x, out.at[mine], here.at[0])
    own.start()
    pair = [push(x, out.at[mine], send.at[7], recv.at[7], twin)]
    pair[0].start()
    slab = lambda xh, k: wide_out.at[:, :, xh * 2 + k]
    w_across = push(w, slab(xh, k), send.at[15], recv.at[15], side)
    w_across.start()
    pair.append(push(w, slab(xh, k), send.at[16], recv.at[16], twin))
    pair[1].start()
    w_own = pltpu.make_async_copy(w, slab(xh, k), here.at[1])
    w_own.start()

    def hand(n, block):
        copy = push(out.at[block], out.at[block], send.at[7 + n], recv.at[7 + n], twin)
        copy.start()
        pair.append(copy)

    across.wait_recv()
    second = [
        push(out.at[theirs], out.at[theirs], send.at[4 + i], recv.at[4 + i], d)
        for i, d in enumerate(rows)
    ]
    for copy in second:
        copy.start()
    hand(1, theirs)
    for i, p in enumerate(back):
        first[i].wait_recv()
        hand(2 + i, at(p, xh, k))
    w_across.wait_recv()
    other = slab(1 - xh, k)
    pair.append(push(other, other, send.at[17], recv.at[17], twin))
    pair[-1].start()
    for i, p in enumerate(back):
        second[i].wait_recv()
        hand(5 + i, at(p, 1 - xh, k))
    for copy in pair:
        copy.wait()
    across.wait_send()
    w_across.wait_send()
    for copy in first + second:
        copy.wait_send()
    own.wait()
    w_own.wait()


def gather_weights(x, w, ident):
    return pl.pallas_call(
        weights_kernel,
        out_shape=(
            jax.ShapeDtypeStruct((CTX, *x.shape), x.dtype),
            jax.ShapeDtypeStruct((2, 2, 4, *w.shape[2:]), w.dtype),
        ),
        in_specs=[ANY, pl.BlockSpec(memory_space=pltpu.VMEM)],
        out_specs=(ANY, ANY),
        scratch_shapes=[
            pltpu.SemaphoreType.DMA((2,)),
            pltpu.SemaphoreType.DMA((18,)),
            pltpu.SemaphoreType.DMA((18,)),
        ],
        compiler_params=pltpu.CompilerParams(
            collective_id=ident, has_side_effects=True, vmem_limit_bytes=16 << 20
        ),
    )(x, w)


def to_heads(x, ident):
    return swaps(ident, (x, "to_heads", None, True))[0]


def from_heads(x, ident):
    return swaps(ident, (x, "from_heads", None, True))[0]


def spread_tokens(x, out, here, send, recv, step, last):
    c, e, z, xh, k = spot()
    at = lambda z, xh, k: z * 4 + xh * 2 + k
    forth = [lax.rem(z + i, 4) for i in range(1, 4)]
    back = [lax.rem(z + 4 - i, 4) for i in range(1, 4)]
    side, twin = (at(z, 1 - xh, k), e), (at(z, xh, 1 - k), e)
    mine, theirs = at(z, xh, k), at(z, 1 - xh, k)
    held = [mine, theirs] + [at(p, xh, k) for p in back] + [at(p, 1 - xh, k) for p in back]
    across = push(x, out.at[mine], send.at[0], recv.at[0], side)
    first = [
        push(x, out.at[mine], send.at[1 + i], recv.at[1 + i], (at(p, xh, k), e))
        for i, p in enumerate(forth)
    ]
    second = [
        push(out.at[theirs], out.at[theirs], send.at[4 + i], recv.at[4 + i], (at(p, xh, k), e))
        for i, p in enumerate(forth)
    ]
    pair = [
        push(x if n == 0 else out.at[b], out.at[b], send.at[7 + n], recv.at[7 + n], twin)
        for n, b in enumerate(held)
    ]
    own = pltpu.make_async_copy(x, out.at[mine], here)

    @pl.when(step == 0)
    def _():
        greet([side, twin] + [(at(p, xh, k), e) for p in forth])
        for copy in [across, *first, pair[0], own]:
            copy.start()

    @pl.when(step == 2)
    def _():
        across.wait_recv()
        for copy in [*second, pair[1]]:
            copy.start()

    @pl.when(step == 5)
    def _():
        for copy, hand in zip(first, pair[2:5]):
            copy.wait_recv()
            hand.start()

    def finish():
        for copy, hand in zip(second, pair[5:]):
            copy.wait_recv()
            hand.start()
        for copy in pair:
            copy.wait()
        for copy in [across, *first, *second]:
            copy.wait_send()
        own.wait()

    return finish


def near_buckets():
    shape = (6 * CHUNK, QUERIES)
    offset = (
        lax.broadcasted_iota(jnp.int32, shape, 0)
        - 2 * CHUNK
        - lax.broadcasted_iota(jnp.int32, shape, 1)
    )
    distance = jnp.abs(offset)
    far = jnp.full(shape, 8, jnp.int32)
    for edge in bucket_edges:
        far = far + (distance >= edge).astype(jnp.int32)
    return jnp.where(distance < 8, distance, far) + jnp.where(offset > 0, BUCKETS // 2, 0)


def tile_rows(chunk, block):
    tile = jnp.clip(chunk - 2 * block + 2, 0, 5)
    return pl.ds(pl.multiple_of(tile * CHUNK, CHUNK), CHUNK)


def chunk_rows(chunk):
    return pl.ds(pl.multiple_of(chunk * CHUNK, CHUNK), CHUNK)


def forward_kernel(
    qkv_ref, table_ref, tok_ref, p_ref, o_ref, low_ref, inv_ref, all_ref, keys, bias, scores, *sems
):
    block = pl.program_id(0)
    finish = spread_tokens(tok_ref, all_ref, *sems, block, LEN // QUERIES - 1)

    @pl.when(block == 0)
    def _():
        keys[...] = qkv_ref[1].T
        ids = near_buckets()
        tiles = jnp.zeros(ids.shape, wide)
        for b in range(BUCKETS):
            tiles = jnp.where(ids == b, table_ref[b], tiles)
        bias[...] = tiles

    here = pl.ds(pl.multiple_of(block * QUERIES, QUERIES), QUERIES)
    queries = qkv_ref[0, :, here]

    def score(chunk, top):
        rows = chunk_rows(chunk)
        part = jnp.dot(keys[rows, :], queries, preferred_element_type=wide)
        part = part + bias[tile_rows(chunk, block), :]
        scores[rows, :] = part
        return jnp.maximum(top, jnp.max(part.reshape(CHUNK // 8, 8, QUERIES), axis=0))

    top = lax.fori_loop(
        0, LEN // CHUNK, score, jnp.full((8, QUERIES), -1e30, wide), unroll=2
    )
    top = jnp.max(top, axis=0, keepdims=True)

    def weigh(chunk, total):
        rows = chunk_rows(chunk)
        part = jnp.exp(scores[rows, :] - top)
        p_ref[rows, :] = part.astype(low)
        return total + jnp.sum(part.reshape(CHUNK // 8, 8, QUERIES), axis=0)

    total = lax.fori_loop(0, LEN // CHUNK, weigh, jnp.zeros((8, QUERIES), wide), unroll=2)
    inverse = 1.0 / jnp.sum(total, axis=0, keepdims=True)
    out = jnp.dot(qkv_ref[2], p_ref[...], preferred_element_type=wide) * inverse
    o_ref[...] = out
    low_ref[0] = out.astype(low)
    inv_ref[...] = inverse
    pl.when(block == LEN // QUERIES - 1)(finish)


def attend(qkv, table, rows, ident):
    whole = lambda *shape: pl.BlockSpec(shape, lambda i: (0,) * len(shape))
    return pl.pallas_call(
        forward_kernel,
        grid=(LEN // QUERIES,),
        out_shape=(
            jax.ShapeDtypeStruct((LEN, LEN), low),
            jax.ShapeDtypeStruct((HEAD_DIM, LEN), wide),
            jax.ShapeDtypeStruct((1, HEAD_DIM, LEN), low),
            jax.ShapeDtypeStruct((1, LEN), wide),
            jax.ShapeDtypeStruct((CTX, *rows.shape), rows.dtype),
        ),
        in_specs=[whole(3, HEAD_DIM, LEN), pl.BlockSpec(memory_space=pltpu.SMEM), ANY],
        out_specs=(
            pl.BlockSpec((LEN, QUERIES), lambda i: (0, i)),
            pl.BlockSpec((HEAD_DIM, QUERIES), lambda i: (0, i)),
            pl.BlockSpec((1, HEAD_DIM, QUERIES), lambda i: (0, 0, i)),
            pl.BlockSpec((1, QUERIES), lambda i: (0, i)),
            ANY,
        ),
        scratch_shapes=[
            pltpu.VMEM((LEN, HEAD_DIM), low),
            pltpu.VMEM((6 * CHUNK, QUERIES), wide),
            pltpu.VMEM((LEN, QUERIES), wide),
            pltpu.SemaphoreType.DMA,
            pltpu.SemaphoreType.DMA((15,)),
            pltpu.SemaphoreType.DMA((15,)),
        ],
        compiler_params=pltpu.CompilerParams(
            collective_id=ident, has_side_effects=True, vmem_limit_bytes=32 << 20
        ),
    )(qkv, table, rows)


def backward_kernel(
    qkv_ref, p_ref, o_ref, inv_ref, do_ref, x_ref, grad_ref, sums_ref, y_ref,
    values, dk, dv, tiles, slopes, send, recv,
):
    block = pl.program_id(0)
    size, me, device = group("x")
    across = push(x_ref.at[:, :, 1 - me], y_ref, send, recv, device(1 - me))

    @pl.when(block == 0)
    def _():
        greet([device(1 - me)])
        across.start()

    @pl.when(block == 0)
    def _():
        values[...] = qkv_ref[2].T
        dk[...] = jnp.zeros(dk.shape, wide)
        dv[...] = jnp.zeros(dv.shape, wide)
        tiles[...] = jnp.zeros(tiles.shape, wide)

    here = pl.ds(pl.multiple_of(block * QUERIES, QUERIES), QUERIES)
    scaled = (do_ref[0].astype(wide) * inv_ref[...]).astype(low)
    delta = jnp.sum(scaled.astype(wide) * o_ref[...], axis=0, keepdims=True)

    def slope(chunk, carry):
        rows = chunk_rows(chunk)
        part = jnp.dot(values[rows, :], scaled, preferred_element_type=wide)
        part = p_ref[rows, :].astype(wide) * (part - delta)
        slopes[rows, :] = part.astype(low)
        near = tile_rows(chunk, block)
        tiles[near, :] = tiles[near, :] + part
        return carry

    lax.fori_loop(0, LEN // CHUNK, slope, 0, unroll=2)
    grad_ref[0, :, here] = jnp.dot(
        qkv_ref[1], slopes[...], preferred_element_type=wide
    ).astype(low)
    queries = qkv_ref[0, :, here].T
    turned = scaled.T

    def gather(chunk, carry):
        rows = pl.ds(pl.multiple_of(chunk * 512, 512), 512)
        dk[rows, :] = dk[rows, :] + jnp.dot(
            slopes[rows, :], queries, preferred_element_type=wide
        )
        dv[rows, :] = dv[rows, :] + jnp.dot(p_ref[rows, :], turned, preferred_element_type=wide)
        return carry

    lax.fori_loop(0, LEN // 512, gather, 0)

    @pl.when(block == LEN // QUERIES - 1)
    def _():
        grad_ref[1] = dk[...].T.astype(low)
        grad_ref[2] = dv[...].T.astype(low)
        sums_ref[...] = tiles[...]
        across.wait()


def attend_back(qkv, probs, out, inverse, grad_out, grads, ident):
    whole = lambda *shape: pl.BlockSpec(shape, lambda i: (0,) * len(shape))
    return pl.pallas_call(
        backward_kernel,
        grid=(LEN // QUERIES,),
        out_shape=(
            jax.ShapeDtypeStruct((3, HEAD_DIM, LEN), low),
            jax.ShapeDtypeStruct((6 * CHUNK, QUERIES), wide),
            jax.ShapeDtypeStruct(grads.shape[:2] + grads.shape[3:], grads.dtype),
        ),
        in_specs=[
            whole(3, HEAD_DIM, LEN),
            pl.BlockSpec((LEN, QUERIES), lambda i: (0, i)),
            pl.BlockSpec((HEAD_DIM, QUERIES), lambda i: (0, i)),
            pl.BlockSpec((1, QUERIES), lambda i: (0, i)),
            pl.BlockSpec((1, HEAD_DIM, QUERIES), lambda i: (0, 0, i)),
            ANY,
        ],
        out_specs=(whole(3, HEAD_DIM, LEN), whole(6 * CHUNK, QUERIES), ANY),
        scratch_shapes=[
            pltpu.VMEM((LEN, HEAD_DIM), low),
            pltpu.VMEM((LEN, HEAD_DIM), wide),
            pltpu.VMEM((LEN, HEAD_DIM), wide),
            pltpu.VMEM((6 * CHUNK, QUERIES), wide),
            pltpu.VMEM((LEN, QUERIES), low),
            pltpu.SemaphoreType.DMA,
            pltpu.SemaphoreType.DMA,
        ],
        compiler_params=pltpu.CompilerParams(
            collective_id=ident, has_side_effects=True, vmem_limit_bytes=32 << 20
        ),
    )(qkv, probs, out, inverse, grad_out, grads)


def rms_scale(values_in, gain_vec):
    return (
        values_in
        * lax.rsqrt(jnp.mean(values_in * values_in, axis=-1, keepdims=True) + epsilon)
        * gain_vec
    )


def dot(a, b, dims=(1, 0)):
    return lax.dot_general(
        a, b, (((dims[0],), (dims[1],)), ((), ())), preferred_element_type=wide
    )


def shards(
    tokens,
    cotangent,
    routes,
    query_weight,
    kv_weight,
    out_weight,
    norm_gain_one,
    norm_gain_two,
    router_weight,
    bias_table,
    expert_in,
    expert_out,
):
    highest = lax.Precision.HIGHEST
    experts = 16
    x_rows = tokens[0].astype(wide)
    c = lax.axis_index("ctx")

    matrix = jnp.concatenate([query_weight, kv_weight, out_weight], axis=1).reshape(16, 1152)
    small = jnp.concatenate(
        [
            router_weight,
            norm_gain_one[:, None],
            norm_gain_two[:, None],
            jnp.pad(bias_table, (0, 3))[:, None],
        ],
        axis=1,
    ).reshape(1, 114)
    packed = jnp.concatenate([matrix, jnp.pad(small, ((0, 15), (0, 14)))], axis=1)
    eight = swap(packed, "exp", 1)
    block = jnp.concatenate(
        [
            eight[:, :, :1152].reshape(48, 4 * D),
            jnp.pad(eight[:, 0, 1152:1266].reshape(48, 19), ((0, 0), (0, 109))),
        ],
        axis=1,
    )
    experts_local = jnp.stack([jnp.swapaxes(expert_in, 1, 2), expert_out])
    full, experts_here = gather_weights(block, experts_local, 2)
    full = full.reshape(D, 4 * D + 128)
    experts_here = experts_here.reshape(2, 2, D, D)
    qkv_full = full[:, : 3 * D]
    out_full = full[:, 3 * D : 4 * D]
    router_wide = full[:, 4 * D : 4 * D + 16].astype(wide)
    gain_one = full[:, 4 * D + 16].astype(wide)
    gain_two = full[:, 4 * D + 17].astype(wide)
    table = full[:, 4 * D + 18].astype(wide).reshape(128, 6)[:, :3].reshape(BUCKETS, HEADS)
    head = head_of(c)
    my_head = (jnp.arange(HEADS, dtype=jnp.int32) == head) & owns(c)
    head_table = jnp.sum(jnp.where(my_head[None, :], table, 0.0), axis=1)

    normed_one, norm_one_back = jax.vjp(rms_scale, x_rows, gain_one)
    h_one = normed_one.astype(low)
    qkv = dot(qkv_full, h_one, (0, 1)).astype(low).reshape(3, HEADS, HEAD_DIM, TOK)
    head_qkv = to_heads(qkv, 4)
    place = jnp.arange(D, dtype=jnp.int32)
    place = place // 6 % EXP * TOK + place // 48 * 8 + place % 6
    by_owner = (place[:, None] == jnp.arange(EXP * TOK, dtype=jnp.int32)[None, :]).astype(low)
    probs, attended, attended_head, inverse, h_all = attend(
        head_qkv, head_table, dot(h_one, by_owner).astype(low), 18
    )
    attended_low = from_heads(attended_head, 5).reshape(D, TOK)
    residual = x_rows + dot(attended_low, out_full, (0, 0))
    normed_two, norm_two_back = jax.vjp(rms_scale, residual, gain_two)
    h_two = normed_two.astype(low)
    h_two_wide = h_two.astype(wide)
    route_probs = jax.nn.softmax(jnp.dot(h_two_wide, router_wide, precision=highest), axis=-1)

    route_ids = routes[0, :, 0]
    choose = route_ids[:, None] == jnp.arange(experts, dtype=jnp.int32)[None, :]
    choose_wide = choose.astype(wide)
    index = jnp.arange(TOK, dtype=jnp.int32)
    before = (index[None, :] < index[:, None]).astype(low)
    earlier = dot(before, choose.astype(low))
    slot = jnp.sum(earlier * choose_wide, axis=1).astype(jnp.int32)
    target = route_ids // 2 * SLOTS + route_ids % 2 * CAP + slot
    target = jnp.concatenate([target, target + 2 * CAP])
    dispatch = (
        jnp.arange(EXP * SLOTS, dtype=jnp.int32)[:, None] == target[None, :]
    ).astype(low)
    gate_value = jnp.sum(route_probs * choose_wide, axis=1)
    grad_out = cotangent[0].astype(wide)
    grad_y = (gate_value[:, None] * grad_out).astype(low)
    outgoing = dot(dispatch, jnp.concatenate([h_two, grad_y])).astype(low)
    received = swap(outgoing.reshape(EXP, SLOTS, D), "exp", 6, 0).reshape(EXP * SLOTS, D)

    row = jnp.arange(4 * 80, dtype=jnp.int32)
    source = row % 80 // CAP * SLOTS + row // 80 * CAP + row % CAP
    compact = (source[:, None] == jnp.arange(EXP * SLOTS, dtype=jnp.int32)[None, :]).astype(low)
    lists = swap(dot(compact, received).astype(low), "z", 7).reshape(ZED, 4, 80, D)
    partial, grads_in, grads_out = [], [], []
    for n in range(2):
        rows = lists[:, n].reshape(ZED * 80, D)
        grads = lists[:, 2 + n].reshape(ZED * 80, D)
        weight_in, weight_out = experts_here[0, n], experts_here[1, n]
        pre_act = dot(rows, weight_in, (1, 1))
        hidden_wide, gelu_back = jax.vjp(jax.nn.gelu, pre_act)
        hidden = hidden_wide.astype(low)
        grad_hidden = dot(grads, weight_out, (1, 1))
        grad_pre = gelu_back(grad_hidden)[0].astype(low)
        partial.append(dot(hidden, weight_out).astype(low).reshape(ZED, 80, D))
        partial.append(dot(grad_pre, weight_in).astype(low).reshape(ZED, 80, D))
        grads_in.append(dot(grad_pre, rows, (0, 0)).astype(low))
        grads_out.append(dot(hidden, grads, (0, 0)).astype(low))
    partial = jnp.stack([partial[0], partial[2], partial[1], partial[3]], axis=1)
    partial = partial.reshape(ZED, 320, D)
    summed = add_up(partial, "z", 0, swaps(8, (partial, "z", 0, False))[0]).astype(low)
    spread = dot(compact, summed, (0, 0)).astype(low).reshape(EXP, SLOTS, D)
    expert_grads = jnp.stack([jnp.stack(grads_in), jnp.stack(grads_out)])
    expert_grads = expert_grads.reshape(2, 2, 2, 2, 192, D)
    back, others = swaps(9, (spread, "exp", 0, True), (expert_grads, "core", 3, False))
    expert_grads = add_up(expert_grads, "core", 3, others).astype(low)
    returned = dot(dispatch, back.reshape(EXP * SLOTS, D), (0, 0))
    expert_tokens, grad_h_two = returned[:TOK], returned[TOK:]

    mixed_rows = (residual + gate_value[:, None] * expert_tokens).astype(low)
    grad_gate = jnp.sum(grad_out * expert_tokens, axis=1)
    grad_choice = choose_wide * grad_gate[:, None]
    grad_logits = route_probs * (
        grad_choice - jnp.sum(route_probs * grad_choice, axis=1, keepdims=True)
    )
    grad_router = jnp.dot(h_two_wide.T, grad_logits, precision=highest)
    grad_h_two = grad_h_two + jnp.dot(grad_logits, router_wide.T, precision=highest)
    grad_resid_norm, grad_gain_two = norm_two_back(grad_h_two)
    grad_residual = grad_out + grad_resid_norm
    grad_branch = grad_residual.astype(low)
    grad_attended = dot(out_full, grad_branch, (1, 1)).astype(low)
    late = jnp.concatenate(
        [
            dot(attended_low, grad_branch).astype(low),
            grad_router.astype(low),
            grad_gain_two[:, None].astype(low),
            jnp.zeros((D, 111), low),
        ],
        axis=1,
    ).reshape(ZED, 4, 48, 896)
    head_grad, others = swaps(
        10,
        (grad_attended.reshape(1, HEADS, HEAD_DIM, TOK), "to_heads", None, True),
        (late, "quad", 1, False),
    )
    late = add_up(late, "quad", 1, others).astype(low)
    head_grads, tile_sums, others = attend_back(
        head_qkv, probs, attended, inverse, head_grad, expert_grads, 19
    )
    expert_grads = add_up(expert_grads, "x", 2, others[None])
    grad_expert_in = jnp.swapaxes(expert_grads[0], 1, 2)
    grad_expert_out = expert_grads[1]

    bucket_sums = jnp.sum(
        jnp.where(
            near_buckets()[None] == jnp.arange(BUCKETS, dtype=jnp.int32)[:, None, None],
            tile_sums[None],
            0.0,
        ),
        axis=(1, 2),
    )
    sixth = jnp.arange(EXP * TOK, dtype=jnp.int32) % 8 == 6
    head_weights = dot(h_all.reshape(LEN, EXP * TOK), head_grads.reshape(192, LEN), (0, 1))
    head_weights = head_weights + jnp.where(
        sixth[:, None], jnp.pad(bucket_sums, (0, 192 - BUCKETS))[None, :], 0.0
    )
    head_weights = head_weights.astype(low).reshape(EXP, TOK, 192)
    grad_qkv, others, late_others = swaps(
        11,
        (head_grads, "from_heads", None, True),
        (head_weights, "exp", 0, False),
        (late, "z", 0, False),
    )
    grad_qkv = grad_qkv.reshape(3 * D, TOK)
    head_weights = add_up(head_weights, "exp", 0, others).reshape(CTX, 8, 192)
    late = add_up(late, "z", 0, late_others).reshape(EXP, 6, 896)
    late = jnp.pad(late, ((0, 0), (0, 2), (0, 0)))
    by_head, others = swaps(
        12, (head_weights, "head_rows", None, True), (late, "exp", 0, False)
    )
    late = add_up(late, "exp", 0, others)
    grad_qkv_weight = jnp.transpose(
        by_head[:, :6].reshape(HEADS, 6, 3, HEAD_DIM), (1, 2, 0, 3)
    ).reshape(6, 3 * D)
    own_weight = jnp.concatenate([query_weight, kv_weight], axis=1).astype(wide)
    grad_gain_one = jnp.sum(own_weight * grad_qkv_weight, axis=1) / norm_gain_one.astype(wide)
    grad_table = by_head[:, 6, :BUCKETS].T.reshape(-1)
    grad_table = lax.dynamic_slice(grad_table, (3 * (c * EXP + lax.axis_index("exp")),), (3,))

    grad_h_one = dot(grad_qkv, qkv_full, (0, 1))
    grad_tokens = grad_residual + norm_one_back(grad_h_one)[0]
    return (
        mixed_rows[None],
        grad_tokens[None],
        grad_qkv_weight[:, :D],
        grad_qkv_weight[:, D:],
        late[:6, :D],
        grad_gain_one,
        late[:6, D + 16],
        late[:6, D : D + 16],
        grad_table,
        grad_expert_in,
        grad_expert_out,
    )


def solution(mesh):
    rows = P("exp", "ctx", None)
    shared, vector = P(("ctx", "exp"), None), P(("ctx", "exp"))
    expert_in, expert_out = P("exp", None, "ctx"), P("exp", "ctx", None)
    return jax.shard_map(
        shards,
        mesh=mesh,
        in_specs=(rows, rows, rows, shared, shared, shared, vector, vector, shared, vector)
        + (expert_in, expert_out),
        out_specs=(rows, rows, shared, shared, shared, vector, vector, shared, vector)
        + (expert_in, expert_out),
        check_vma=False,
    )
```

```python
import functools

import jax
import jax.numpy as jnp
from jax import lax
from jax.experimental import pallas as pl
from jax.experimental.pallas import tpu as pltpu
from jax.sharding import PartitionSpec as P

MESH = pl.DeviceIdType.MESH
HEADS = 12
HEAD_DIM = 64
BUCKETS = 32
TOK = 128
D = 768
CAP = 10
SLOTS = 48
CTX, EXP, ZED = 16, 8, 4
LEN = TOK * CTX
QUERIES = 256
CHUNK = 128
epsilon = 1e-06
bucket_edges = (12, 16, 23, 32, 46, 64, 91)
low = jnp.bfloat16
wide = jnp.float32
ANY = pl.BlockSpec(memory_space=pl.ANY)


def spot():
    c, e = lax.axis_index("ctx"), lax.axis_index("exp")
    return c, e, c // 4, (c // 2) % 2, c % 2


def greet(peers):
    barrier = pltpu.get_barrier_semaphore()
    for peer in peers:
        pl.semaphore_signal(barrier, inc=1, device_id=peer, device_id_type=MESH)
    pl.semaphore_wait(barrier, len(peers))


def push(src, dst, send, recv, to):
    return pltpu.make_async_remote_copy(
        src_ref=src, dst_ref=dst, send_sem=send, recv_sem=recv, device_id=to, device_id_type=MESH
    )


def group(kind):
    c, e, z, xh, k = spot()
    if kind == "exp":
        return EXP, e, lambda i: (c, i)
    if kind == "z":
        return ZED, z, lambda i: (i * 4 + xh * 2 + k, e)
    if kind == "x":
        return 2, xh, lambda i: (z * 4 + i * 2 + k, e)
    if kind == "core":
        return 2, k, lambda i: (z * 4 + xh * 2 + i, e)
    if kind == "quad":
        return 4, xh * 2 + k, lambda i: (z * 4 + i, e)
    return CTX, c, lambda i: (i, e)


SIZES = {"exp": EXP, "z": ZED, "x": 2, "core": 2, "quad": 4}


def head_of(c):
    return jnp.minimum((c // 4) * 3 + c % 4, HEADS - 1)


def owns(c):
    return c % 4 < 3


def columns(c):
    return pl.ds(pl.multiple_of(c * TOK, TOK), TOK)


def when(condition, step):
    if condition is None:
        step()
    else:
        pl.when(condition)(step)


def heads_parts(kind, me, x, out):
    if kind == "to_heads":
        return lambda to: x.at[:, head_of(to)], out.at[:, :, columns(me)], None, owns
    if kind == "from_heads":
        return lambda to: x.at[:, :, columns(to)], out.at[head_of(me)], owns, None
    return lambda to: x.at[to], out.at[head_of(me)], owns, None


def swaps_kernel(plan, *refs):
    n = len(plan)
    xs, outs, (send, recv, here) = refs[:n], refs[n : 2 * n], refs[2 * n :]
    kinds = dict.fromkeys("ctx" if kind not in SIZES else kind for kind, axis, keep in plan)
    if "ctx" in kinds:
        kinds = [kind for kind in kinds if kind in ("ctx", "exp")]
    peers = []
    for kind in kinds:
        size, me, device = group(kind)
        peers += [device(lax.rem(me + i, size)) for i in range(1, size)]
    greet(peers)
    copies, count = [], 0
    for (kind, axis, keep), x, out in zip(plan, xs, outs):
        size, me, device = group(kind)
        if kind in SIZES:
            part = lambda i: x if axis is None else x.at[(slice(None),) * axis + (i,)]
            sends = receives = None
        else:
            part, place, sends, receives = heads_parts(kind, me, x, out)
        for i in range(1, size):
            to, source = lax.rem(me + i, size), lax.rem(me + size - i, size)
            if kind in SIZES:
                place = out.at[me if keep else i - 1]
            copy = push(part(to), place, send.at[count], recv.at[count], device(to))
            if sends is not None:
                out_if, in_if = sends(me), sends(source)
            elif receives is not None:
                out_if, in_if = receives(to), receives(me)
            else:
                out_if = in_if = None
            when(out_if, copy.start)
            copies.append((copy, out_if, in_if))
            count += 1
    own = []
    for n, ((kind, axis, keep), x, out) in enumerate(zip(plan, xs, outs)):
        size, me, device = group(kind)
        if kind in SIZES and keep:
            part = x if axis is None else x.at[(slice(None),) * axis + (me,)]
            own.append((pltpu.make_async_copy(part, out.at[me], here.at[n]), None))
        elif kind not in SIZES:
            part, place, sends, receives = heads_parts(kind, me, x, out)
            own.append((pltpu.make_async_copy(part(me), place, here.at[n]), owns(me)))
    for copy, condition in own:
        when(condition, copy.start)
    for copy, out_if, in_if in copies:
        when(out_if, copy.wait_send)
        when(in_if, copy.wait_recv)
    for copy, condition in own:
        when(condition, copy.wait)


def swaps(ident, *items):
    shapes, total = [], 0
    for x, kind, axis, keep in items:
        block = x.shape if axis is None else x.shape[:axis] + x.shape[axis + 1 :]
        if kind == "to_heads":
            shape = (x.shape[0], HEAD_DIM, LEN)
        elif kind == "from_heads":
            shape = (HEADS, x.shape[0], HEAD_DIM, TOK)
        elif kind == "head_rows":
            shape = (HEADS, *x.shape[1:])
        else:
            shape = (SIZES[kind] - (not keep), *block)
        shapes.append(jax.ShapeDtypeStruct(shape, x.dtype))
        total += SIZES.get(kind, CTX) - 1
    return pl.pallas_call(
        functools.partial(swaps_kernel, [item[1:] for item in items]),
        out_shape=shapes,
        in_specs=[ANY] * len(items),
        out_specs=[ANY] * len(items),
        scratch_shapes=[
            pltpu.SemaphoreType.DMA((total,)),
            pltpu.SemaphoreType.DMA((total,)),
            pltpu.SemaphoreType.DMA((len(items),)),
        ],
        compiler_params=pltpu.CompilerParams(
            collective_id=ident, has_side_effects=True, vmem_limit_bytes=2 << 20
        ),
    )(*[item[0] for item in items])


def swap(x, kind, ident, axis=None):
    return swaps(ident, (x, kind, axis, True))[0]


def add_up(x, kind, axis, others):
    mine = lax.dynamic_index_in_dim(x, group(kind)[1], axis, keepdims=False)
    return mine.astype(wide) + jnp.sum(others.astype(wide), axis=0)


def quad_slab(out, xh, k):
    return out.at[:, xh * 2 + k]


def quad_parts(w, out, here, send, recv):
    c, e, z, xh, k = spot()
    side, twin = (z * 4 + (1 - xh) * 2 + k, e), (z * 4 + xh * 2 + 1 - k, e)
    mine, theirs = quad_slab(out, xh, k), quad_slab(out, 1 - xh, k)
    across = push(w, mine, send.at[0], recv.at[0], side)
    pair = push(w, mine, send.at[1], recv.at[1], twin)
    hand = push(theirs, theirs, send.at[2], recv.at[2], twin)
    own = pltpu.make_async_copy(w, mine, here)

    def begin():
        across.start()
        pair.start()
        own.start()

    def forward():
        across.wait_recv()
        hand.start()

    def end():
        across.wait_send()
        pair.wait()
        hand.wait()
        own.wait()

    return begin, forward, end


def spread_parts(x, out, here, send, recv):
    c, e, z, xh, k = spot()
    at = lambda z, xh, k: z * 4 + xh * 2 + k
    forth = [lax.rem(z + i, 4) for i in range(1, 4)]
    back = [lax.rem(z + 4 - i, 4) for i in range(1, 4)]
    side, twin = (at(z, 1 - xh, k), e), (at(z, xh, 1 - k), e)
    mine, theirs = at(z, xh, k), at(z, 1 - xh, k)
    held = [mine, theirs] + [at(p, xh, k) for p in back] + [at(p, 1 - xh, k) for p in back]
    across = push(x, out.at[mine], send.at[0], recv.at[0], side)
    first = [
        push(x, out.at[mine], send.at[1 + i], recv.at[1 + i], (at(p, xh, k), e))
        for i, p in enumerate(forth)
    ]
    second = [
        push(out.at[theirs], out.at[theirs], send.at[4 + i], recv.at[4 + i], (at(p, xh, k), e))
        for i, p in enumerate(forth)
    ]
    pair = [
        push(x if n == 0 else out.at[b], out.at[b], send.at[7 + n], recv.at[7 + n], twin)
        for n, b in enumerate(held)
    ]
    own = pltpu.make_async_copy(x, out.at[mine], here)

    def begin():
        for copy in [across, *first, pair[0], own]:
            copy.start()

    def middle():
        across.wait_recv()
        for copy in [*second, pair[1]]:
            copy.start()

    def late():
        for copy, hand in zip(first, pair[2:5]):
            copy.wait_recv()
            hand.start()

    def end():
        for copy, hand in zip(second, pair[5:]):
            copy.wait_recv()
            hand.start()
        for copy in pair:
            copy.wait()
        for copy in [across, *first, *second]:
            copy.wait_send()
        own.wait()

    return begin, middle, late, end


def cross_peers():
    c, e, z, xh, k = spot()
    at = lambda z, xh, k: (z * 4 + xh * 2 + k, e)
    return [at(z, 1 - xh, k), at(z, xh, 1 - k)] + [at(lax.rem(z + i, 4), xh, k) for i in (1, 2, 3)]


def open_kernel(packed, x, eight, mine, x_all, here, send, recv, x_send, x_recv):
    c, e, z, xh, k = spot()
    exps = [lax.rem(e + i, EXP) for i in range(1, EXP)]
    peers = [lax.rem(c + i, CTX) for i in range(1, CTX)]
    greet([(c, p) for p in exps] + [(p, e) for p in peers])
    x_begin, x_middle, x_late, x_end = spread_parts(x, x_all, here.at[0], x_send, x_recv)
    rows = [
        push(packed, eight.at[e], send.at[i], recv.at[i], (c, p)) for i, p in enumerate(exps)
    ]
    own_rows = pltpu.make_async_copy(packed, eight.at[e], here.at[1])
    for copy in rows:
        copy.start()
    own_rows.start()
    x_begin()
    x_middle()
    for copy in rows:
        copy.wait_recv()
    own_rows.wait()
    heads = [
        push(eight.at[:, head_of(p)], mine.at[c], send.at[6 + i], recv.at[6 + i], (p, e))
        for i, p in enumerate(peers, 1)
    ]
    own_head = pltpu.make_async_copy(eight.at[:, head_of(c)], mine.at[c], here.at[2])
    for p, copy in zip(peers, heads):
        pl.when(owns(p))(copy.start)
    pl.when(owns(c))(own_head.start)
    x_late()
    for p, copy in zip(peers, heads):
        pl.when(owns(p))(copy.wait_send)
        pl.when(owns(c))(copy.wait_recv)
    pl.when(owns(c))(own_head.wait)
    x_end()
    for copy in rows:
        copy.wait_send()


def opening(packed, x, ident):
    shapes = ((EXP, *packed.shape), (CTX, EXP, *packed.shape[1:]), (CTX, *x.shape))
    sems = pltpu.SemaphoreType.DMA
    return pl.pallas_call(
        open_kernel,
        out_shape=[jax.ShapeDtypeStruct(s, low) for s in shapes],
        in_specs=[ANY, ANY],
        out_specs=[ANY] * 3,
        scratch_shapes=[sems((3,)), sems((22,)), sems((22,)), sems((15,)), sems((15,))],
        compiler_params=pltpu.CompilerParams(
            collective_id=ident, has_side_effects=True, vmem_limit_bytes=2 << 20
        ),
    )(packed, x)


def lists_kernel(x, w, x_all, w_all, here, send, recv, w_send, w_recv):
    c, e, z, xh, k = spot()
    greet(cross_peers())
    size, me, device = group("z")
    copies = []
    for i in range(1, size):
        to = device(lax.rem(me + i, size))
        copies.append(push(x, x_all.at[me], send.at[i - 1], recv.at[i - 1], to))
    w_begin, w_forward, w_end = quad_parts(w, w_all, here.at[0], w_send, w_recv)
    own = pltpu.make_async_copy(x, x_all.at[me], here.at[1])
    for copy in copies:
        copy.start()
    w_begin()
    own.start()
    w_forward()
    for copy in copies:
        copy.wait()
    own.wait()
    w_end()


def gather_lists(x, w, ident):
    sems = pltpu.SemaphoreType.DMA
    shapes = ((ZED, *x.shape), (2, 4, *w.shape[1:]))
    return pl.pallas_call(
        lists_kernel,
        out_shape=[jax.ShapeDtypeStruct(s, low) for s in shapes],
        in_specs=[pl.BlockSpec(memory_space=pltpu.VMEM)] * 2,
        out_specs=[ANY] * 2,
        scratch_shapes=[sems((2,))] + [sems((3,))] * 4,
        compiler_params=pltpu.CompilerParams(
            collective_id=ident, has_side_effects=True, vmem_limit_bytes=4 << 20
        ),
    )(x, w)


def return_kernel(x, g, x_out, g_own, g_out, held, total, here, send, recv, g_send, g_recv):
    c, e, z, xh, k = spot()
    greet(cross_peers())
    size, me, device = group("z")
    copies = []
    for i in range(1, size):
        to = lax.rem(me + i, size)
        copies.append(push(x.at[to], x_out.at[i - 1], send.at[i - 1], recv.at[i - 1], device(to)))
    twin, side = group("core")[2](1 - k), group("x")[2](1 - xh)
    across = push(g.at[:, :, 1 - k], held, g_send.at[0], g_recv.at[0], twin)
    across.start()
    for copy in copies:
        copy.start()
    across.wait()

    def add(n, carry):
        a, b, rows = n // 8, n // 4 % 2, pl.ds(pl.multiple_of(n % 4 * 48, 16), 48)
        both = g[a, b, k, rows, :].astype(wide) + held[a, b, rows, :].astype(wide)
        total[a, b, rows, :] = both.astype(low)
        return carry

    lax.fori_loop(0, 16, add, 0)
    other = push(total.at[:, 1 - xh], g_out, g_send.at[1], g_recv.at[1], side)
    other.start()
    own = pltpu.make_async_copy(total.at[:, xh], g_own, here)
    own.start()
    own.wait()
    for copy in copies:
        copy.wait()
    other.wait()


def return_lists(x, g, ident):
    sems = pltpu.SemaphoreType.DMA
    half = (2, *g.shape[3:])
    return pl.pallas_call(
        return_kernel,
        out_shape=[
            jax.ShapeDtypeStruct(s, low) for s in ((ZED - 1, *x.shape[1:]), half, half)
        ],
        in_specs=[ANY, pl.BlockSpec(memory_space=pltpu.VMEM)],
        out_specs=[ANY] * 3,
        scratch_shapes=[
            pltpu.VMEM((2, 2, *g.shape[3:]), low),
            pltpu.VMEM((2, 2, *g.shape[3:]), low),
            sems,
            sems((3,)),
            sems((3,)),
            sems((2,)),
            sems((2,)),
        ],
        compiler_params=pltpu.CompilerParams(
            collective_id=ident, has_side_effects=True, vmem_limit_bytes=7 << 20
        ),
    )(x, g)


def to_heads(x, ident):
    return swaps(ident, (x, "to_heads", None, True))[0]


def from_heads(x, ident):
    return swaps(ident, (x, "from_heads", None, True))[0]


def near_buckets(shape, before):
    offset = (
        lax.broadcasted_iota(jnp.int32, shape, 0)
        - before
        - lax.broadcasted_iota(jnp.int32, shape, 1)
    )
    distance = jnp.abs(offset)
    far = jnp.full(shape, 8, jnp.int32)
    for edge in bucket_edges:
        far = far + (distance >= edge).astype(jnp.int32)
    return jnp.where(distance < 8, distance, far) + jnp.where(offset > 0, BUCKETS // 2, 0)


def tile_rows(chunk, block):
    tile = jnp.clip(chunk - 2 * block + 2, 0, 5)
    return pl.ds(pl.multiple_of(tile * CHUNK, CHUNK), CHUNK)


def chunk_rows(chunk):
    return pl.ds(pl.multiple_of(chunk * CHUNK, CHUNK), CHUNK)


def forward_kernel(
    qkv_ref, table_ref, x_ref, w_ref, p_ref, o_ref, low_ref, inv_ref, x_all, w_all,
    keys, bias, scores, here, x_send, x_recv, w_send, w_recv,
):
    block = pl.program_id(0)
    x_begin, x_middle, x_late, x_end = spread_parts(x_ref, x_all, here.at[0], x_send, x_recv)
    w_begin, w_forward, w_end = quad_parts(w_ref, w_all, here.at[1], w_send, w_recv)

    @pl.when(block == 0)
    def _():
        greet(cross_peers())
        x_begin()
        w_begin()

    @pl.when(block == 2)
    def _():
        x_middle()

    @pl.when(block == 5)
    def _():
        x_late()

    @pl.when(block == 0)
    def _():
        keys[...] = qkv_ref[1].T
        ids = near_buckets(bias.shape, 2 * CHUNK)
        tiles = jnp.zeros(ids.shape, wide)
        for b in range(BUCKETS):
            tiles = jnp.where(ids == b, table_ref[b : b + 1, 0:1], tiles)
        bias[...] = tiles

    here = pl.ds(pl.multiple_of(block * QUERIES, QUERIES), QUERIES)
    queries = qkv_ref[0, :, here]

    def score(chunk, top):
        rows = chunk_rows(chunk)
        part = jnp.dot(keys[rows, :], queries, preferred_element_type=wide)
        part = part + bias[tile_rows(chunk, block), :]
        scores[rows, :] = part
        return jnp.maximum(top, jnp.max(part.reshape(CHUNK // 8, 8, QUERIES), axis=0))

    top = lax.fori_loop(
        0, LEN // CHUNK, score, jnp.full((8, QUERIES), -1e30, wide), unroll=4
    )
    top = jnp.max(top, axis=0, keepdims=True)

    def weigh(chunk, total):
        rows = chunk_rows(chunk)
        part = jnp.exp(scores[rows, :] - top)
        p_ref[rows, :] = part.astype(low)
        return total + jnp.sum(part.reshape(CHUNK // 8, 8, QUERIES), axis=0)

    total = lax.fori_loop(0, LEN // CHUNK, weigh, jnp.zeros((8, QUERIES), wide), unroll=4)
    inverse = 1.0 / jnp.sum(total, axis=0, keepdims=True)
    out = jnp.dot(qkv_ref[2], p_ref[...], preferred_element_type=wide) * inverse
    o_ref[...] = out
    low_ref[0] = out.astype(low)
    inv_ref[...] = inverse


    @pl.when(block == LEN // QUERIES - 1)
    def _():
        w_forward()
        x_end()
        w_end()


def attend(qkv, table, x, w, ident):
    whole = lambda *shape: pl.BlockSpec(shape, lambda i: (0,) * len(shape))
    return pl.pallas_call(
        forward_kernel,
        grid=(LEN // QUERIES,),
        out_shape=(
            pltpu.HBM((LEN, LEN), low),
            jax.ShapeDtypeStruct((HEAD_DIM, LEN), wide),
            jax.ShapeDtypeStruct((1, HEAD_DIM, LEN), low),
            jax.ShapeDtypeStruct((1, LEN), wide),
            jax.ShapeDtypeStruct((CTX, *x.shape), low),
            jax.ShapeDtypeStruct((2, 4, *w.shape[1:]), low),
        ),
        in_specs=[whole(3, HEAD_DIM, LEN), whole(BUCKETS, 128), ANY, ANY],
        out_specs=(
            pl.BlockSpec((LEN, QUERIES), lambda i: (0, i)),
            pl.BlockSpec((HEAD_DIM, QUERIES), lambda i: (0, i)),
            pl.BlockSpec((1, HEAD_DIM, QUERIES), lambda i: (0, 0, i)),
            pl.BlockSpec((1, QUERIES), lambda i: (0, i)),
            ANY,
            ANY,
        ),
        scratch_shapes=[
            pltpu.VMEM((LEN, HEAD_DIM), low),
            pltpu.VMEM((6 * CHUNK, QUERIES), wide),
            pltpu.VMEM((LEN, QUERIES), wide),
            pltpu.SemaphoreType.DMA((2,)),
            pltpu.SemaphoreType.DMA((15,)),
            pltpu.SemaphoreType.DMA((15,)),
            pltpu.SemaphoreType.DMA((3,)),
            pltpu.SemaphoreType.DMA((3,)),
        ],
        compiler_params=pltpu.CompilerParams(
            collective_id=ident, has_side_effects=True, vmem_limit_bytes=11 << 20
        ),
    )(qkv, table, x, w)


def backward_kernel(
    qkv_ref, p_ref, o_ref, inv_ref, do_ref, x_ref, g_ref, l_ref,
    grad_ref, sums_ref, x_all, g_out, l_out,
    values, dk, dv, tiles, slopes, here, x_send, x_recv, send, recv,
):
    block = pl.program_id(0)
    x_begin, x_middle, x_late, x_end = spread_parts(x_ref, x_all, here, x_send, x_recv)
    size, me, device = group("x")
    across = push(g_ref.at[:, 1 - me], g_out, send.at[0], recv.at[0], device(1 - me))
    size, z, device_z = group("z")
    around = []
    for i in range(1, size):
        to = lax.rem(z + i, size)
        around.append(
            push(l_ref.at[to], l_out.at[i - 1], send.at[i], recv.at[i], device_z(to))
        )

    @pl.when(block == 0)
    def _():
        greet(cross_peers())
        x_begin()
        for copy in around:
            copy.start()

    @pl.when(block == 1)
    def _():
        x_middle()
        across.start()

    @pl.when(block == 5)
    def _():
        x_late()

    @pl.when(block == 0)
    def _():
        values[...] = qkv_ref[2].T
        dk[...] = jnp.zeros(dk.shape, wide)
        dv[...] = jnp.zeros(dv.shape, wide)
        tiles[...] = jnp.zeros(tiles.shape, wide)

    here = pl.ds(pl.multiple_of(block * QUERIES, QUERIES), QUERIES)
    scaled = (do_ref[0].astype(wide) * inv_ref[...]).astype(low)
    delta = jnp.sum(scaled.astype(wide) * o_ref[...], axis=0, keepdims=True)

    def slope(chunk, carry):
        rows = chunk_rows(chunk)
        part = jnp.dot(values[rows, :], scaled, preferred_element_type=wide)
        part = p_ref[rows, :].astype(wide) * (part - delta)
        slopes[rows, :] = part.astype(low)
        near = tile_rows(chunk, block)
        tiles[near, :] = tiles[near, :] + part
        return carry

    lax.fori_loop(0, LEN // CHUNK, slope, 0, unroll=4)
    grad_ref[0, :, here] = jnp.dot(
        qkv_ref[1], slopes[...], preferred_element_type=wide
    ).astype(low)
    queries = qkv_ref[0, :, here].T
    turned = scaled.T

    def gather(chunk, carry):
        rows = pl.ds(pl.multiple_of(chunk * 512, 512), 512)
        dk[rows, :] = dk[rows, :] + jnp.dot(
            slopes[rows, :], queries, preferred_element_type=wide
        )
        dv[rows, :] = dv[rows, :] + jnp.dot(p_ref[rows, :], turned, preferred_element_type=wide)
        return carry

    lax.fori_loop(0, LEN // 512, gather, 0)

    @pl.when(block == LEN // QUERIES - 1)
    def _():
        grad_ref[1] = dk[...].T.astype(low)
        grad_ref[2] = dv[...].T.astype(low)
        sums_ref[...] = tiles[...]
        for copy in around:
            copy.wait()
        x_end()
        across.wait()


def attend_back(qkv, probs, out, inverse, grad_out, x, grads, late, ident):
    whole = lambda *shape: pl.BlockSpec(shape, lambda i: (0,) * len(shape))
    return pl.pallas_call(
        backward_kernel,
        grid=(LEN // QUERIES,),
        out_shape=(
            jax.ShapeDtypeStruct((3, HEAD_DIM, LEN), low),
            jax.ShapeDtypeStruct((6 * CHUNK, QUERIES), wide),
            jax.ShapeDtypeStruct((CTX, *x.shape), low),
            jax.ShapeDtypeStruct(grads.shape[:1] + grads.shape[2:], low),
            jax.ShapeDtypeStruct((ZED - 1, *late.shape[1:]), low),
        ),
        in_specs=[
            whole(3, HEAD_DIM, LEN),
            pl.BlockSpec((LEN, QUERIES), lambda i: (0, i)),
            pl.BlockSpec((HEAD_DIM, QUERIES), lambda i: (0, i)),
            pl.BlockSpec((1, QUERIES), lambda i: (0, i)),
            pl.BlockSpec((1, HEAD_DIM, QUERIES), lambda i: (0, 0, i)),
            ANY,
            ANY,
            ANY,
        ],
        out_specs=(whole(3, HEAD_DIM, LEN), whole(6 * CHUNK, QUERIES), ANY, ANY, ANY),
        scratch_shapes=[
            pltpu.VMEM((LEN, HEAD_DIM), low),
            pltpu.VMEM((LEN, HEAD_DIM), wide),
            pltpu.VMEM((LEN, HEAD_DIM), wide),
            pltpu.VMEM((6 * CHUNK, QUERIES), wide),
            pltpu.VMEM((LEN, QUERIES), low),
            pltpu.SemaphoreType.DMA,
            pltpu.SemaphoreType.DMA((15,)),
            pltpu.SemaphoreType.DMA((15,)),
            pltpu.SemaphoreType.DMA((4,)),
            pltpu.SemaphoreType.DMA((4,)),
        ],
        compiler_params=pltpu.CompilerParams(
            collective_id=ident, has_side_effects=True, vmem_limit_bytes=14 << 20
        ),
    )(
        qkv,
        pltpu.with_memory_space_constraint(probs, pltpu.HBM),
        out, inverse, grad_out, x, grads, late
    )


def finish_kernel(
    rows_ref, late_ref, others_ref, wq_ref, wkv_ref, gain_ref,
    gq_ref, gkv_ref, gout_ref, router_ref, gain_one_ref, gain_two_ref, table_ref,
):
    c, e, z, xh, k = spot()
    late = late_ref[e] + jnp.sum(others_ref[...], axis=0)
    gout_ref[...] = late[:6, :D]
    router_ref[...] = late[:6, D + 67 : D + 83]
    gain_two_ref[...] = late[:6, D + 65 : D + 66]
    parts = [
        jnp.concatenate(
            [rows_ref[h, :, n * HEAD_DIM : (n + 1) * HEAD_DIM] for h in range(HEADS)], axis=1
        )[:6]
        for n in range(3)
    ]
    gq_ref[...] = parts[0]
    gkv_ref[:, :D] = parts[1]
    gkv_ref[:, D:] = parts[2]
    along = jnp.sum(wq_ref[...].astype(wide) * parts[0], axis=1, keepdims=True)
    along = along + jnp.sum(wkv_ref[:, :D].astype(wide) * parts[1], axis=1, keepdims=True)
    along = along + jnp.sum(wkv_ref[:, D:].astype(wide) * parts[2], axis=1, keepdims=True)
    gain_one_ref[...] = along / gain_ref[...]
    device = c * EXP + e
    buckets = rows_ref[pl.ds(device % 4 * 3, 3), 6, :]
    chosen = lax.broadcasted_iota(jnp.int32, buckets.shape, 1) == device // 4
    table_ref[...] = jnp.sum(jnp.where(chosen, buckets, 0.0), axis=1, keepdims=True)


def finish(by_head, late, others, wq, wkv, gain):
    shapes = [(6, D), (6, 2 * D), (6, D), (6, 16), (6, 1), (6, 1), (3, 1)]
    return pl.pallas_call(
        finish_kernel,
        out_shape=[jax.ShapeDtypeStruct(s, wide) for s in shapes],
        compiler_params=pltpu.CompilerParams(vmem_limit_bytes=8 << 20),
    )(by_head, late, others, wq, wkv, gain.astype(wide)[:, None])


def plain(kernel, shapes, megabytes, *args):
    return pl.pallas_call(
        kernel,
        out_shape=[jax.ShapeDtypeStruct(shape, kind) for shape, kind in shapes],
        compiler_params=pltpu.CompilerParams(vmem_limit_bytes=megabytes << 20),
    )(*args)


def iota(shape, axis):
    return lax.broadcasted_iota(jnp.int32, shape, axis)


def pack_kernel(wq_ref, wkv_ref, wo_ref, extra_ref, out_ref):
    empty = jnp.zeros((4, 128), wide)
    extra = extra_ref[...].astype(wide)
    wq, wkv, wo = (ref[...].astype(wide) for ref in (wq_ref, wkv_ref, wo_ref))
    for h in range(HEADS):
        at = h * HEAD_DIM
        query, key = wq[:, at : at + HEAD_DIM], wkv[:, at : at + HEAD_DIM]
        value = wkv[:, D + at : D + at + HEAD_DIM]
        upper = jnp.concatenate([query, key], axis=1)
        lower = jnp.concatenate([value, extra], axis=1)
        out_ref[h] = jnp.concatenate([upper, lower, empty], axis=0).astype(low)
    for n in range(3):
        upper, lower = (wo[:, (2 * n + i) * 128 : (2 * n + i + 1) * 128] for i in range(2))
        out_ref[HEADS + n] = jnp.concatenate([upper, lower, empty], axis=0).astype(low)


def six_rows(rows, first):
    shape = (rows // 16 * 6, rows)
    column = iota((1, rows), 1)
    inner = column % 16 - first
    place = jnp.where((inner >= 0) & (inner < 6), column // 16 * 6 + inner, -1)
    return (iota(shape, 0) == place).astype(low)


def project_kernel(mine_ref, x_ref, eight_ref, qkv_ref, h_ref, table_ref, first_ref, second_ref):
    c, e, z, xh, k = spot()
    mine = mine_ref[...]
    upper = jnp.dot(six_rows(2048, 0), mine, preferred_element_type=wide)
    lower = jnp.dot(six_rows(2048, 6), mine, preferred_element_type=wide)
    lower_turned = lower.T
    gain = lower_turned[64:65, :]
    weight_qk, weight_v = upper.T.astype(low), lower_turned[:64].astype(low)
    for n in range(4):
        rows = slice(n * 512, (n + 1) * 512)
        x = x_ref[rows, :].astype(wide)
        scale = lax.rsqrt(jnp.mean(x * x, axis=1, keepdims=True) + epsilon)
        h = (x * scale * gain).astype(low)
        h_ref[rows, :] = h
        both = dot(weight_qk, h, (1, 1)).astype(low)
        qkv_ref[0, :, rows] = both[:64]
        qkv_ref[1, :, rows] = both[64:]
        qkv_ref[2, :, rows] = dot(weight_v, h, (1, 1)).astype(low)
    head = head_of(c)
    column = jnp.broadcast_to(lower[:, 66:67], (D, 128))
    row = iota((BUCKETS, D), 1)
    wanted = (row // 24 == iota((BUCKETS, D), 0)) & (row % 24 == head // 3 * 6 + head % 3)
    table_ref[...] = jnp.dot(wanted.astype(low), column.astype(low), preferred_element_type=wide)
    pick = [six_rows(128, 0), six_rows(128, 6)]
    part = lambda n, i: jnp.dot(
        pick[i], eight_ref[:, n].reshape(128, 128), preferred_element_type=wide
    )
    first_ref[:, :128] = part(0, 1).astype(low)
    for n in range(3):
        for i in range(2):
            at = 128 + (2 * n + i) * 128
            first_ref[:, at : at + 128] = part(HEADS + n, i).astype(low)
    for pair in range(HEADS // 2):
        pieces = []
        for h in (2 * pair, 2 * pair + 1):
            pieces += [part(h, 0), part(h, 1)[:, :64]]
        pieces = jnp.concatenate(pieces, axis=1).astype(low)
        if pair < 2:
            first_ref[:, 896 + pair * 384 : 896 + (pair + 1) * 384] = pieces
        else:
            second_ref[:, (pair - 2) * 384 : (pair - 1) * 384] = pieces


def route_kernel(
    att_ref, x_ref, cot_ref, route_ref, full_ref,
    residual_ref, h_ref, probs_ref, dispatch_ref, out_ref,
):
    wo, small = full_ref[:, 128:896], full_ref[:, :128]
    gain = small.astype(wide).T[65:66, :]
    attended = att_ref[...].astype(wide).T.astype(low)
    residual = x_ref[...].astype(wide) + jnp.dot(attended, wo, preferred_element_type=wide)
    residual_ref[...] = residual
    scale = lax.rsqrt(jnp.mean(residual * residual, axis=1, keepdims=True) + epsilon)
    h_two = (residual * scale * gain).astype(low)
    h_ref[...] = h_two
    logits = jnp.dot(h_two, small, preferred_element_type=wide)[:, 67:83]
    logits = jnp.exp(logits - jnp.max(logits, axis=1, keepdims=True))
    probs = logits / jnp.sum(logits, axis=1, keepdims=True)
    probs_ref[...] = probs
    route = route_ref[...]
    choose = (route == iota((TOK, 16), 1)).astype(wide)
    before = (iota((TOK, TOK), 1) < iota((TOK, TOK), 0)).astype(low)
    earlier = jnp.dot(before, choose.astype(low), preferred_element_type=wide)
    slot = jnp.sum(earlier * choose, axis=1, keepdims=True).astype(jnp.int32)
    target = route // 2 * SLOTS + route % 2 * CAP + slot
    places = iota((TOK, EXP * SLOTS), 1)
    dispatch = jnp.concatenate(
        [(places == target).astype(wide), (places == target + 2 * CAP).astype(wide)], axis=0
    )
    dispatch_ref[...] = dispatch.astype(low)
    gate = jnp.sum(probs * choose, axis=1, keepdims=True)
    grad_y = (gate * cot_ref[...].astype(wide)).astype(low)
    turned = dispatch.T.astype(low)
    out = jnp.dot(turned[:, :TOK], h_two, preferred_element_type=wide)
    out = out + jnp.dot(turned[:, TOK:], grad_y, preferred_element_type=wide)
    out_ref[...] = out.astype(low)


def combine_kernel(
    back_ref, dispatch_ref, residual_ref, cot_ref, probs_ref, route_ref, h_ref, full_ref, att_ref,
    mixed_ref, grad_ref, grad_att_ref, late_ref,
):
    wo, small = full_ref[:, 128:896], full_ref[:, :128]
    gain = small.astype(wide).T[65:66, :]
    returned = jnp.dot(dispatch_ref[...], back_ref[...], preferred_element_type=wide)
    tokens, grad_h = returned[:TOK], returned[TOK:]
    residual, probs = residual_ref[...], probs_ref[...]
    choose = (route_ref[...] == iota((TOK, 16), 1)).astype(wide)
    gate = jnp.sum(probs * choose, axis=1, keepdims=True)
    mixed_ref[...] = (residual + gate * tokens).astype(low)
    grad = cot_ref[...].astype(wide)
    grad_choice = choose * jnp.sum(grad * tokens, axis=1, keepdims=True)
    grad_logits = probs * (grad_choice - jnp.sum(probs * grad_choice, axis=1, keepdims=True))
    spread = (iota((16, 128), 0) + 67 == iota((16, 128), 1)).astype(low)
    upper = grad_logits.astype(low)
    lower = (grad_logits - upper.astype(wide)).astype(low)
    upper = jnp.dot(upper, spread, preferred_element_type=wide).astype(low)
    lower = jnp.dot(lower, spread, preferred_element_type=wide).astype(low)
    grad_h = grad_h + dot(upper, small, (1, 1)) + dot(lower, small, (1, 1))
    scale = lax.rsqrt(jnp.mean(residual * residual, axis=1, keepdims=True) + epsilon)
    along = grad_h * gain
    mean = jnp.mean(along * residual, axis=1, keepdims=True)
    grad = grad + scale * along - (scale * scale * scale * mean) * residual
    grad_ref[...] = grad
    branch = grad.astype(low)
    grad_att_ref[...] = dot(wo, branch, (1, 1)).astype(low)
    late_ref[:, :D] = jnp.dot(att_ref[...], branch, preferred_element_type=wide).astype(low)
    turned = h_ref[...].astype(wide).T.astype(low)
    extra = jnp.dot(turned, upper, preferred_element_type=wide)
    extra = extra + jnp.dot(turned, lower, preferred_element_type=wide)
    gains = (grad_h * residual * scale).T
    gains = jnp.sum(gains, axis=1, keepdims=True)
    late_ref[:, D:] = jnp.where(iota((D, 128), 1) == 65, gains, extra).astype(low)


def rms_scale(values_in, gain_vec):
    return (
        values_in
        * lax.rsqrt(jnp.mean(values_in * values_in, axis=-1, keepdims=True) + epsilon)
        * gain_vec
    )


def dot(a, b, dims=(1, 0)):
    return lax.dot_general(
        a, b, (((dims[0],), (dims[1],)), ((), ())), preferred_element_type=wide
    )


def shards(
    tokens,
    cotangent,
    routes,
    query_weight,
    kv_weight,
    out_weight,
    norm_gain_one,
    norm_gain_two,
    router_weight,
    bias_table,
    expert_in,
    expert_out,
):
    x_rows = tokens[0].astype(wide)

    extra = jnp.concatenate(
        [
            norm_gain_one[:, None],
            norm_gain_two[:, None],
            jnp.pad(bias_table, (0, 3))[:, None],
            router_weight,
            jnp.zeros((6, 45), low),
        ],
        axis=1,
    )
    packed = plain(
        pack_kernel, [((15, 16, 128), low)], 4, query_weight, kv_weight, out_weight, extra
    )[0]
    eight, mine, x_all = opening(packed, tokens[0], 1)
    head_qkv, h_all, head_table, block, block_qkv = plain(
        project_kernel,
        [
            ((3, HEAD_DIM, LEN), low),
            ((LEN, D), low),
            ((BUCKETS, 128), wide),
            ((48, 128 + 2 * D), low),
            ((48, 2 * D), low),
        ],
        28,
        mine.reshape(2048, 128),
        x_all.reshape(LEN, D),
        eight,
    )
    probs, attended, attended_head, inverse, full, experts_out = attend(
        head_qkv, head_table, block, expert_out, 18
    )
    full = full.reshape(D, 2 * D + 128)
    full_out = full[:, :896]
    gain_one = full[:, 64].astype(wide)
    attended_low = from_heads(attended_head, 5).reshape(D, TOK)
    routed = (TOK, D)
    residual, h_two, route_probs, dispatch, outgoing = plain(
        route_kernel,
        [
            (routed, wide),
            (routed, low),
            ((TOK, 16), wide),
            ((2 * TOK, EXP * SLOTS), low),
            ((EXP * SLOTS, D), low),
        ],
        16,
        attended_low,
        tokens[0],
        cotangent[0],
        routes[0],
        full_out,
    )
    received = swap(outgoing.reshape(EXP, SLOTS, D), "exp", 6, 0).reshape(EXP * SLOTS, D)

    row = jnp.arange(4 * 80, dtype=jnp.int32)
    source = row % 80 // CAP * SLOTS + row // 80 * CAP + row % CAP
    compact = (source[:, None] == jnp.arange(EXP * SLOTS, dtype=jnp.int32)[None, :]).astype(low)
    lists, experts_in = gather_lists(
        dot(compact, received).astype(low), jnp.swapaxes(expert_in, 1, 2), 7
    )
    lists = lists.reshape(ZED, 4, 80, D)
    experts_here = experts_in.reshape(2, D, D), experts_out.reshape(2, D, D)
    partial, grads_in, grads_out = [], [], []
    for n in range(2):
        rows = lists[:, n].reshape(ZED * 80, D)
        grads = lists[:, 2 + n].reshape(ZED * 80, D)
        weight_in, weight_out = experts_here[0][n], experts_here[1][n]
        pre_act = dot(rows, weight_in, (1, 1))
        hidden_wide, gelu_back = jax.vjp(jax.nn.gelu, pre_act)
        hidden = hidden_wide.astype(low)
        grad_hidden = dot(grads, weight_out, (1, 1))
        grad_pre = gelu_back(grad_hidden)[0].astype(low)
        partial.append(dot(hidden, weight_out).astype(low).reshape(ZED, 80, D))
        partial.append(dot(grad_pre, weight_in).astype(low).reshape(ZED, 80, D))
        grads_in.append(dot(grad_pre, rows, (0, 0)).astype(low))
        grads_out.append(dot(hidden, grads, (0, 0)).astype(low))
    partial = jnp.stack([partial[0], partial[2], partial[1], partial[3]], axis=1)
    partial = partial.reshape(ZED, 320, D)
    grads_out = jnp.stack(grads_out).reshape(2, 2, 2, 192, D)
    others, grads_own, grads_other = return_lists(partial, grads_out, 8)
    grad_expert_out = grads_own.astype(wide) + grads_other.astype(wide)
    summed = add_up(partial, "z", 0, others).astype(low)
    spread = dot(compact, summed, (0, 0)).astype(low).reshape(EXP, SLOTS, D)
    expert_grads = jnp.stack(grads_in).reshape(2, 2, 2, 192, D)
    back, others = swaps(9, (spread, "exp", 0, True), (expert_grads, "core", 2, False))
    expert_grads = add_up(expert_grads, "core", 2, others).astype(low)
    mixed_rows, grad_residual, grad_attended, late = plain(
        combine_kernel,
        [(routed, low), (routed, wide), ((D, TOK), low), ((D, 896), low)],
        20,
        back.reshape(EXP * SLOTS, D),
        dispatch,
        residual,
        cotangent[0],
        route_probs,
        routes[0],
        h_two,
        full_out,
        attended_low,
    )
    late = late.reshape(8, 2, 48, 896)
    head_grad, others = swaps(
        10,
        (grad_attended.reshape(1, HEADS, HEAD_DIM, TOK), "to_heads", None, True),
        (late, "core", 1, False),
    )
    late = add_up(late, "core", 1, others).astype(low).reshape(ZED, 2, 48, 896)
    head_grads, tile_sums, qkv_full, others, late_others = attend_back(
        head_qkv, probs, attended, inverse, head_grad, block_qkv, expert_grads, late, 19
    )
    qkv_full = qkv_full.reshape(D, 2 * D)
    late = add_up(late, "z", 0, late_others).astype(low)
    grad_expert_in = jnp.swapaxes(add_up(expert_grads, "x", 1, others[None]), 1, 2)

    tile = lambda n, half: tile_sums[n * CHUNK : (n + 1) * CHUNK, half * TOK : (half + 1) * TOK]
    near = jnp.concatenate([tile(n, 0) + tile(n + 1, 1) for n in (1, 2, 3)], axis=0)
    bucket_range = jnp.arange(BUCKETS, dtype=jnp.int32)
    bucket_sums = jnp.sum(
        jnp.where(
            near_buckets(near.shape, CHUNK)[None] == bucket_range[:, None, None], near[None], 0.0
        ),
        axis=(1, 2),
    )
    bucket_sums = bucket_sums + jnp.where(
        bucket_range == BUCKETS // 2 - 1, jnp.sum(tile(0, 0) + tile(0, 1) + tile(1, 1)), 0.0
    )
    bucket_sums = bucket_sums + jnp.where(
        bucket_range == BUCKETS - 1, jnp.sum(tile(4, 0) + tile(5, 0) + tile(5, 1)), 0.0
    )
    sixth = jnp.arange(EXP * TOK, dtype=jnp.int32) % 8 == 6
    place = jnp.arange(D, dtype=jnp.int32)
    place = place // 6 % EXP * TOK + place // 48 * 8 + place % 6
    by_owner = (jnp.arange(EXP * TOK, dtype=jnp.int32)[:, None] == place[None, :]).astype(low)
    head_weights = dot(h_all, head_grads.reshape(192, LEN), (0, 1)).astype(low)
    head_weights = dot(by_owner, head_weights)
    head_weights = head_weights + jnp.where(
        sixth[:, None], jnp.pad(bucket_sums, (0, 192 - BUCKETS))[None, :], 0.0
    )
    head_weights = head_weights.astype(low).reshape(EXP, TOK, 192)
    grad_qkv, others, late_others = swaps(
        11,
        (head_grads, "from_heads", None, True),
        (head_weights, "exp", 0, False),
        (late, "x", 0, False),
    )
    grad_qkv = grad_qkv.reshape(3 * D, TOK)
    head_weights = add_up(head_weights, "exp", 0, others).reshape(CTX, 8, 192)
    late = add_up(late, "x", 0, late_others).reshape(EXP, 6, 896)
    late = jnp.pad(late, ((0, 0), (0, 2), (0, 0)))
    by_head, others = swaps(
        12, (head_weights, "head_rows", None, True), (late, "exp", 0, False)
    )
    finished = finish(by_head, late, others, query_weight, kv_weight, norm_gain_one)

    grad_h_one = dot(grad_qkv[:D], full[:, 896:], (0, 1))
    grad_h_one = grad_h_one + dot(grad_qkv[D:], qkv_full, (0, 1))
    norm_one_back = jax.vjp(lambda x: rms_scale(x, gain_one), x_rows)[1]
    grad_tokens = grad_residual + norm_one_back(grad_h_one)[0]
    return (
        mixed_rows[None],
        grad_tokens[None],
        *finished[:3],
        finished[4][:, 0],
        finished[5][:, 0],
        finished[3],
        finished[6][:, 0],
        grad_expert_in,
        grad_expert_out,
    )


def solution(mesh):
    rows = P("exp", "ctx", None)
    shared, vector = P(("ctx", "exp"), None), P(("ctx", "exp"))
    expert_in, expert_out = P("exp", None, "ctx"), P("exp", "ctx", None)
    return jax.shard_map(
        shards,
        mesh=mesh,
        in_specs=(rows, rows, rows, shared, shared, shared, vector, vector, shared, vector)
        + (expert_in, expert_out),
        out_specs=(rows, rows, shared, shared, shared, vector, vector, shared, vector)
        + (expert_in, expert_out),
        check_vma=False,
    )
```

```python
import functools

import jax
import jax.numpy as jnp
from jax import lax
from jax.experimental import pallas as pl
from jax.experimental.pallas import tpu as pltpu
from jax.sharding import PartitionSpec as P

MESH = pl.DeviceIdType.MESH
HEADS = 12
HEAD_DIM = 64
BUCKETS = 32
TOK = 128
D = 768
CAP = 10
SLOTS = 48
CTX, EXP, ZED = 16, 8, 4
LEN = TOK * CTX
QUERIES = 256
CHUNK = 128
epsilon = 1e-06
bucket_edges = (12, 16, 23, 32, 46, 64, 91)
low = jnp.bfloat16
wide = jnp.float32
ANY = pl.BlockSpec(memory_space=pl.ANY)


def spot():
    c, e = lax.axis_index("ctx"), lax.axis_index("exp")
    return c, e, c // 4, (c // 2) % 2, c % 2


def greet(peers):
    barrier = pltpu.get_barrier_semaphore()
    for peer in peers:
        pl.semaphore_signal(barrier, inc=1, device_id=peer, device_id_type=MESH)
    pl.semaphore_wait(barrier, len(peers))


def push(src, dst, send, recv, to):
    return pltpu.make_async_remote_copy(
        src_ref=src, dst_ref=dst, send_sem=send, recv_sem=recv, device_id=to, device_id_type=MESH
    )


def group(kind):
    c, e, z, xh, k = spot()
    if kind == "exp":
        return EXP, e, lambda i: (c, i)
    if kind == "z":
        return ZED, z, lambda i: (i * 4 + xh * 2 + k, e)
    if kind == "x":
        return 2, xh, lambda i: (z * 4 + i * 2 + k, e)
    if kind == "core":
        return 2, k, lambda i: (z * 4 + xh * 2 + i, e)
    if kind == "quad":
        return 4, xh * 2 + k, lambda i: (z * 4 + i, e)
    return CTX, c, lambda i: (i, e)


SIZES = {"exp": EXP, "z": ZED, "x": 2, "core": 2, "quad": 4}


def head_of(c):
    return jnp.minimum((c // 4) * 3 + c % 4, HEADS - 1)


def owns(c):
    return c % 4 < 3


def columns(c):
    return pl.ds(pl.multiple_of(c * TOK, TOK), TOK)


def when(condition, step):
    if condition is None:
        step()
    else:
        pl.when(condition)(step)


def heads_parts(kind, me, x, out):
    if kind == "to_heads":
        return lambda to: x.at[:, head_of(to)], out.at[:, :, columns(me)], None, owns
    if kind == "from_heads":
        return lambda to: x.at[:, :, columns(to)], out.at[head_of(me)], owns, None
    return lambda to: x.at[to], out.at[head_of(me)], owns, None


def swaps_kernel(plan, *refs):
    n = len(plan)
    xs, outs, (send, recv, here) = refs[:n], refs[n : 2 * n], refs[2 * n :]
    kinds = dict.fromkeys("ctx" if kind not in SIZES else kind for kind, axis, keep in plan)
    if "ctx" in kinds:
        kinds = [kind for kind in kinds if kind in ("ctx", "exp")]
    peers = []
    for kind in kinds:
        size, me, device = group(kind)
        peers += [device(lax.rem(me + i, size)) for i in range(1, size)]
    greet(peers)
    copies, count = [], 0
    for (kind, axis, keep), x, out in zip(plan, xs, outs):
        size, me, device = group(kind)
        if kind in SIZES:
            part = lambda i: x if axis is None else x.at[(slice(None),) * axis + (i,)]
            sends = receives = None
        else:
            part, place, sends, receives = heads_parts(kind, me, x, out)
        for i in range(1, size):
            to, source = lax.rem(me + i, size), lax.rem(me + size - i, size)
            if kind in SIZES:
                place = out.at[me if keep else i - 1]
            copy = push(part(to), place, send.at[count], recv.at[count], device(to))
            if sends is not None:
                out_if, in_if = sends(me), sends(source)
            elif receives is not None:
                out_if, in_if = receives(to), receives(me)
            else:
                out_if = in_if = None
            when(out_if, copy.start)
            copies.append((copy, out_if, in_if))
            count += 1
    own = []
    for n, ((kind, axis, keep), x, out) in enumerate(zip(plan, xs, outs)):
        size, me, device = group(kind)
        if kind in SIZES and keep:
            part = x if axis is None else x.at[(slice(None),) * axis + (me,)]
            own.append((pltpu.make_async_copy(part, out.at[me], here.at[n]), None))
        elif kind not in SIZES:
            part, place, sends, receives = heads_parts(kind, me, x, out)
            own.append((pltpu.make_async_copy(part(me), place, here.at[n]), owns(me)))
    for copy, condition in own:
        when(condition, copy.start)
    for copy, out_if, in_if in copies:
        when(out_if, copy.wait_send)
        when(in_if, copy.wait_recv)
    for copy, condition in own:
        when(condition, copy.wait)


def swaps(ident, *items):
    shapes, total = [], 0
    for x, kind, axis, keep in items:
        block = x.shape if axis is None else x.shape[:axis] + x.shape[axis + 1 :]
        if kind == "to_heads":
            shape = (x.shape[0], HEAD_DIM, LEN)
        elif kind == "from_heads":
            shape = (HEADS, x.shape[0], HEAD_DIM, TOK)
        elif kind == "head_rows":
            shape = (HEADS, *x.shape[1:])
        else:
            shape = (SIZES[kind] - (not keep), *block)
        shapes.append(jax.ShapeDtypeStruct(shape, x.dtype))
        total += SIZES.get(kind, CTX) - 1
    return pl.pallas_call(
        functools.partial(swaps_kernel, [item[1:] for item in items]),
        out_shape=shapes,
        in_specs=[ANY] * len(items),
        out_specs=[ANY] * len(items),
        scratch_shapes=[
            pltpu.SemaphoreType.DMA((total,)),
            pltpu.SemaphoreType.DMA((total,)),
            pltpu.SemaphoreType.DMA((len(items),)),
        ],
        compiler_params=pltpu.CompilerParams(
            collective_id=ident, has_side_effects=True, vmem_limit_bytes=2 << 20
        ),
    )(*[item[0] for item in items])


def swap(x, kind, ident, axis=None):
    return swaps(ident, (x, kind, axis, True))[0]


def add_up(x, kind, axis, others):
    mine = lax.dynamic_index_in_dim(x, group(kind)[1], axis, keepdims=False)
    return mine.astype(wide) + jnp.sum(others.astype(wide), axis=0)


def quad_slab(out, xh, k):
    return out.at[:, xh * 2 + k]


def quad_parts(w, out, here, send, recv):
    c, e, z, xh, k = spot()
    side, twin = (z * 4 + (1 - xh) * 2 + k, e), (z * 4 + xh * 2 + 1 - k, e)
    mine, theirs = quad_slab(out, xh, k), quad_slab(out, 1 - xh, k)
    across = push(w, mine, send.at[0], recv.at[0], side)
    pair = push(w, mine, send.at[1], recv.at[1], twin)
    hand = push(theirs, theirs, send.at[2], recv.at[2], twin)
    own = pltpu.make_async_copy(w, mine, here)

    def begin():
        across.start()
        pair.start()
        own.start()

    def forward():
        across.wait_recv()
        hand.start()

    def end():
        across.wait_send()
        pair.wait()
        hand.wait()
        own.wait()

    return begin, forward, end


def ring_parts(src, at, send, recv):
    c, e, z, xh, k = spot()
    size, me, device = group("z")
    above, below, beyond = (lax.rem(me + i, 4) for i in (1, 3, 2))
    rows = src.shape[0]
    cut = rows // 32 * 16
    upper, lower = pl.ds(0, rows - cut), pl.ds(rows - cut, cut)
    up = push(src, at(me), send.at[0], recv.at[0], device(above))
    down = push(src, at(me), send.at[1], recv.at[1], device(below))
    on_up = at(below).at[upper, :]
    on_down = at(above).at[lower, :]
    on_up = push(on_up, on_up, send.at[2], recv.at[2], device(above))
    on_down = push(on_down, on_down, send.at[3], recv.at[3], device(below))

    def begin():
        up.start()
        down.start()

    def relay():
        up.wait_recv()
        on_up.start()
        down.wait_recv()
        on_down.start()

    def arrive():
        on_up.wait_recv()
        on_down.wait_recv()

    def end():
        for copy in (up, down, on_up, on_down):
            copy.wait_send()

    return begin, relay, arrive, end


def spread_parts(x, out, here, send, recv):
    c, e, z, xh, k = spot()
    at = lambda z, xh, k: z * 4 + xh * 2 + k
    around = [lax.rem(z + i, 4) for i in (3, 1, 2)]
    side, twin = (at(z, 1 - xh, k), e), (at(z, xh, 1 - k), e)
    mine, theirs = at(z, xh, k), at(z, 1 - xh, k)
    held = [mine, theirs] + [at(p, xh, k) for p in around] + [at(p, 1 - xh, k) for p in around]
    across = push(x, out.at[mine], send.at[0], recv.at[0], side)
    first = ring_parts(
        x, lambda p: out.at[at(p, xh, k)], send.at[pl.ds(1, 4)], recv.at[pl.ds(1, 4)]
    )
    second = ring_parts(
        out.at[theirs],
        lambda p: out.at[at(p, 1 - xh, k)],
        send.at[pl.ds(5, 4)],
        recv.at[pl.ds(5, 4)],
    )
    pair = [
        push(x if n == 0 else out.at[b], out.at[b], send.at[9 + n], recv.at[9 + n], twin)
        for n, b in enumerate(held)
    ]
    own = pltpu.make_async_copy(x, out.at[mine], here)

    def begin():
        across.start()
        first[0]()
        pair[0].start()
        own.start()

    def middle():
        across.wait_recv()
        second[0]()
        pair[1].start()

    def relay_first():
        first[1]()
        pair[2].start()
        pair[3].start()

    def relay_second():
        second[1]()
        pair[5].start()
        pair[6].start()

    def end():
        first[2]()
        pair[4].start()
        second[2]()
        pair[7].start()
        for copy in pair:
            copy.wait()
        across.wait_send()
        first[3]()
        second[3]()
        own.wait()

    return begin, middle, relay_first, relay_second, end


def cross_peers():
    c, e, z, xh, k = spot()
    at = lambda z, xh, k: (z * 4 + xh * 2 + k, e)
    return [at(z, 1 - xh, k), at(z, xh, 1 - k)] + [at(lax.rem(z + i, 4), xh, k) for i in (1, 2, 3)]


def open_kernel(packed, x, eight, mine, x_all, here, send, recv, x_send, x_recv):
    c, e, z, xh, k = spot()
    exps = [lax.rem(e + i, EXP) for i in range(1, EXP)]
    peers = [lax.rem(c + i, CTX) for i in range(1, CTX)]
    greet([(c, p) for p in exps] + [(p, e) for p in peers])
    x_begin, x_middle, x_first, x_second, x_end = spread_parts(
        x, x_all, here.at[0], x_send, x_recv
    )
    rows = [
        push(packed, eight.at[e], send.at[i], recv.at[i], (c, p)) for i, p in enumerate(exps)
    ]
    own_rows = pltpu.make_async_copy(packed, eight.at[e], here.at[1])
    for copy in rows:
        copy.start()
    own_rows.start()
    x_begin()
    x_middle()
    for copy in rows:
        copy.wait_recv()
    own_rows.wait()
    heads = [
        push(eight.at[:, head_of(p)], mine.at[c], send.at[6 + i], recv.at[6 + i], (p, e))
        for i, p in enumerate(peers, 1)
    ]
    own_head = pltpu.make_async_copy(eight.at[:, head_of(c)], mine.at[c], here.at[2])
    for p, copy in zip(peers, heads):
        pl.when(owns(p))(copy.start)
    pl.when(owns(c))(own_head.start)
    x_first()
    x_second()
    for p, copy in zip(peers, heads):
        pl.when(owns(p))(copy.wait_send)
        pl.when(owns(c))(copy.wait_recv)
    pl.when(owns(c))(own_head.wait)
    x_end()
    for copy in rows:
        copy.wait_send()


def opening(packed, x, ident):
    shapes = ((EXP, *packed.shape), (CTX, EXP, *packed.shape[1:]), (CTX, *x.shape))
    sems = pltpu.SemaphoreType.DMA
    return pl.pallas_call(
        open_kernel,
        out_shape=[jax.ShapeDtypeStruct(s, low) for s in shapes],
        in_specs=[ANY, ANY],
        out_specs=[ANY] * 3,
        scratch_shapes=[sems((3,)), sems((22,)), sems((22,)), sems((17,)), sems((17,))],
        compiler_params=pltpu.CompilerParams(
            collective_id=ident, has_side_effects=True, vmem_limit_bytes=2 << 20
        ),
    )(packed, x)


def lists_kernel(x, w, x_all, w_all, here, send, recv, w_send, w_recv):
    c, e, z, xh, k = spot()
    greet(cross_peers())
    me = group("z")[1]
    x_begin, x_relay, x_arrive, x_end = ring_parts(x, lambda p: x_all.at[p], send, recv)
    w_begin, w_forward, w_end = quad_parts(w, w_all, here.at[0], w_send, w_recv)
    own = pltpu.make_async_copy(x, x_all.at[me], here.at[1])
    x_begin()
    w_begin()
    own.start()
    x_relay()
    w_forward()
    x_arrive()
    x_end()
    own.wait()
    w_end()


def gather_lists(x, w, ident):
    sems = pltpu.SemaphoreType.DMA
    shapes = ((ZED, *x.shape), (2, 4, *w.shape[1:]))
    return pl.pallas_call(
        lists_kernel,
        out_shape=[jax.ShapeDtypeStruct(s, low) for s in shapes],
        in_specs=[pl.BlockSpec(memory_space=pltpu.VMEM)] * 2,
        out_specs=[ANY] * 2,
        scratch_shapes=[sems((2,)), sems((4,)), sems((4,)), sems((3,)), sems((3,))],
        compiler_params=pltpu.CompilerParams(
            collective_id=ident, has_side_effects=True, vmem_limit_bytes=4 << 20
        ),
    )(x, w)


def return_kernel(x, g, x_out, g_own, g_out, held, total, here, send, recv, g_send, g_recv):
    c, e, z, xh, k = spot()
    greet(cross_peers())
    size, me, device = group("z")
    copies = []
    for i in range(1, size):
        to = lax.rem(me + i, size)
        copies.append(push(x.at[to], x_out.at[i - 1], send.at[i - 1], recv.at[i - 1], device(to)))
    twin, side = group("core")[2](1 - k), group("x")[2](1 - xh)
    across = push(g.at[:, :, 1 - k], held, g_send.at[0], g_recv.at[0], twin)
    across.start()
    for copy in copies:
        copy.start()
    across.wait()

    def add(n, carry):
        a, b, rows = n // 8, n // 4 % 2, pl.ds(pl.multiple_of(n % 4 * 48, 16), 48)
        both = g[a, b, k, rows, :].astype(wide) + held[a, b, rows, :].astype(wide)
        total[a, b, rows, :] = both.astype(low)
        return carry

    lax.fori_loop(0, 16, add, 0)
    other = push(total.at[:, 1 - xh], g_out, g_send.at[1], g_recv.at[1], side)
    other.start()
    own = pltpu.make_async_copy(total.at[:, xh], g_own, here)
    own.start()
    own.wait()
    for copy in copies:
        copy.wait()
    other.wait()


def return_lists(x, g, ident):
    sems = pltpu.SemaphoreType.DMA
    half = (2, *g.shape[3:])
    return pl.pallas_call(
        return_kernel,
        out_shape=[
            jax.ShapeDtypeStruct(s, low) for s in ((ZED - 1, *x.shape[1:]), half, half)
        ],
        in_specs=[ANY, pl.BlockSpec(memory_space=pltpu.VMEM)],
        out_specs=[ANY] * 3,
        scratch_shapes=[
            pltpu.VMEM((2, 2, *g.shape[3:]), low),
            pltpu.VMEM((2, 2, *g.shape[3:]), low),
            sems,
            sems((3,)),
            sems((3,)),
            sems((2,)),
            sems((2,)),
        ],
        compiler_params=pltpu.CompilerParams(
            collective_id=ident, has_side_effects=True, vmem_limit_bytes=7 << 20
        ),
    )(x, g)


def to_heads(x, ident):
    return swaps(ident, (x, "to_heads", None, True))[0]


def from_heads(x, ident):
    return swaps(ident, (x, "from_heads", None, True))[0]


def near_buckets(shape, before):
    offset = (
        lax.broadcasted_iota(jnp.int32, shape, 0)
        - before
        - lax.broadcasted_iota(jnp.int32, shape, 1)
    )
    distance = jnp.abs(offset)
    far = jnp.full(shape, 8, jnp.int32)
    for edge in bucket_edges:
        far = far + (distance >= edge).astype(jnp.int32)
    return jnp.where(distance < 8, distance, far) + jnp.where(offset > 0, BUCKETS // 2, 0)


def tile_rows(chunk, block):
    tile = jnp.clip(chunk - 2 * block + 2, 0, 5)
    return pl.ds(pl.multiple_of(tile * CHUNK, CHUNK), CHUNK)


def chunk_rows(chunk):
    return pl.ds(pl.multiple_of(chunk * CHUNK, CHUNK), CHUNK)


def forward_kernel(
    qkv_ref, table_ref, x_ref, w_ref, p_ref, o_ref, low_ref, inv_ref, x_all, w_all,
    keys, bias, scores, here, x_send, x_recv, w_send, w_recv,
):
    block = pl.program_id(0)
    x_begin, x_middle, x_first, x_second, x_end = spread_parts(
        x_ref, x_all, here.at[0], x_send, x_recv
    )
    w_begin, w_forward, w_end = quad_parts(w_ref, w_all, here.at[1], w_send, w_recv)

    @pl.when(block == 0)
    def _():
        greet(cross_peers())
        x_begin()
        w_begin()

    @pl.when(block == 2)
    def _():
        x_middle()

    @pl.when(block == 4)
    def _():
        x_first()

    @pl.when(block == 6)
    def _():
        x_second()

    @pl.when(block == 0)
    def _():
        keys[...] = qkv_ref[1].T
        ids = near_buckets(bias.shape, 2 * CHUNK)
        tiles = jnp.zeros(ids.shape, wide)
        for b in range(BUCKETS):
            tiles = jnp.where(ids == b, table_ref[b : b + 1, 0:1], tiles)
        bias[...] = tiles

    here = pl.ds(pl.multiple_of(block * QUERIES, QUERIES), QUERIES)
    queries = qkv_ref[0, :, here]

    def score(chunk, top):
        rows = chunk_rows(chunk)
        part = jnp.dot(keys[rows, :], queries, preferred_element_type=wide)
        part = part + bias[tile_rows(chunk, block), :]
        scores[rows, :] = part
        return jnp.maximum(top, jnp.max(part.reshape(CHUNK // 8, 8, QUERIES), axis=0))

    top = lax.fori_loop(
        0, LEN // CHUNK, score, jnp.full((8, QUERIES), -1e30, wide), unroll=4
    )
    top = jnp.max(top, axis=0, keepdims=True)

    def weigh(chunk, total):
        rows = chunk_rows(chunk)
        part = jnp.exp(scores[rows, :] - top)
        p_ref[rows, :] = part.astype(low)
        return total + jnp.sum(part.reshape(CHUNK // 8, 8, QUERIES), axis=0)

    total = lax.fori_loop(0, LEN // CHUNK, weigh, jnp.zeros((8, QUERIES), wide), unroll=4)
    inverse = 1.0 / jnp.sum(total, axis=0, keepdims=True)
    out = jnp.dot(qkv_ref[2], p_ref[...], preferred_element_type=wide) * inverse
    o_ref[...] = out
    low_ref[0] = out.astype(low)
    inv_ref[...] = inverse


    @pl.when(block == LEN // QUERIES - 1)
    def _():
        w_forward()
        x_end()
        w_end()


def attend(qkv, table, x, w, ident):
    whole = lambda *shape: pl.BlockSpec(shape, lambda i: (0,) * len(shape))
    return pl.pallas_call(
        forward_kernel,
        grid=(LEN // QUERIES,),
        out_shape=(
            pltpu.HBM((LEN, LEN), low),
            jax.ShapeDtypeStruct((HEAD_DIM, LEN), wide),
            jax.ShapeDtypeStruct((1, HEAD_DIM, LEN), low),
            jax.ShapeDtypeStruct((1, LEN), wide),
            jax.ShapeDtypeStruct((CTX, *x.shape), low),
            jax.ShapeDtypeStruct((2, 4, *w.shape[1:]), low),
        ),
        in_specs=[whole(3, HEAD_DIM, LEN), whole(BUCKETS, 128), ANY, whole(*w.shape)],
        out_specs=(
            pl.BlockSpec((LEN, QUERIES), lambda i: (0, i)),
            pl.BlockSpec((HEAD_DIM, QUERIES), lambda i: (0, i)),
            pl.BlockSpec((1, HEAD_DIM, QUERIES), lambda i: (0, 0, i)),
            pl.BlockSpec((1, QUERIES), lambda i: (0, i)),
            ANY,
            ANY,
        ),
        scratch_shapes=[
            pltpu.VMEM((LEN, HEAD_DIM), low),
            pltpu.VMEM((6 * CHUNK, QUERIES), wide),
            pltpu.VMEM((LEN, QUERIES), wide),
            pltpu.SemaphoreType.DMA((2,)),
            pltpu.SemaphoreType.DMA((17,)),
            pltpu.SemaphoreType.DMA((17,)),
            pltpu.SemaphoreType.DMA((3,)),
            pltpu.SemaphoreType.DMA((3,)),
        ],
        compiler_params=pltpu.CompilerParams(
            collective_id=ident, has_side_effects=True, vmem_limit_bytes=13 << 20
        ),
    )(qkv, table, x, w)


def backward_kernel(
    qkv_ref, p_ref, o_ref, inv_ref, do_ref, x_ref, g_ref, l_ref,
    grad_ref, sums_ref, x_all, g_out, l_out,
    values, dk, dv, tiles, slopes, here, x_send, x_recv, send, recv,
):
    block = pl.program_id(0)
    x_begin, x_middle, x_first, x_second, x_end = spread_parts(
        x_ref, x_all, here, x_send, x_recv
    )
    size, me, device = group("x")
    across = push(g_ref.at[:, 1 - me], g_out, send.at[0], recv.at[0], device(1 - me))
    size, z, device_z = group("z")
    around = []
    for i in range(1, size):
        to = lax.rem(z + i, size)
        around.append(
            push(l_ref.at[to], l_out.at[i - 1], send.at[i], recv.at[i], device_z(to))
        )

    @pl.when(block == 0)
    def _():
        greet(cross_peers())
        x_begin()

    @pl.when(block == 2)
    def _():
        x_middle()
        across.start()

    @pl.when(block == 3)
    def _():
        x_first()
        for copy in around:
            copy.start()

    @pl.when(block == 5)
    def _():
        x_second()

    @pl.when(block == 0)
    def _():
        values[...] = qkv_ref[2].T
        dk[...] = jnp.zeros(dk.shape, wide)
        dv[...] = jnp.zeros(dv.shape, wide)
        tiles[...] = jnp.zeros(tiles.shape, wide)

    here = pl.ds(pl.multiple_of(block * QUERIES, QUERIES), QUERIES)
    scaled = (do_ref[0].astype(wide) * inv_ref[...]).astype(low)
    delta = jnp.sum(scaled.astype(wide) * o_ref[...], axis=0, keepdims=True)

    def slope(chunk, carry):
        rows = chunk_rows(chunk)
        part = jnp.dot(values[rows, :], scaled, preferred_element_type=wide)
        part = p_ref[rows, :].astype(wide) * (part - delta)
        slopes[rows, :] = part.astype(low)
        near = tile_rows(chunk, block)
        tiles[near, :] = tiles[near, :] + part
        return carry

    lax.fori_loop(0, LEN // CHUNK, slope, 0, unroll=4)
    grad_ref[0, :, here] = jnp.dot(
        qkv_ref[1], slopes[...], preferred_element_type=wide
    ).astype(low)
    queries = qkv_ref[0, :, here].T
    turned = scaled.T

    def gather(chunk, carry):
        rows = pl.ds(pl.multiple_of(chunk * 512, 512), 512)
        dk[rows, :] = dk[rows, :] + jnp.dot(
            slopes[rows, :], queries, preferred_element_type=wide
        )
        dv[rows, :] = dv[rows, :] + jnp.dot(p_ref[rows, :], turned, preferred_element_type=wide)
        return carry

    lax.fori_loop(0, LEN // 512, gather, 0)

    @pl.when(block == LEN // QUERIES - 1)
    def _():
        grad_ref[1] = dk[...].T.astype(low)
        grad_ref[2] = dv[...].T.astype(low)
        sums_ref[...] = tiles[...]
        for copy in around:
            copy.wait()
        x_end()
        across.wait()


def attend_back(qkv, probs, out, inverse, grad_out, x, grads, late, ident):
    whole = lambda *shape: pl.BlockSpec(shape, lambda i: (0,) * len(shape))
    return pl.pallas_call(
        backward_kernel,
        grid=(LEN // QUERIES,),
        out_shape=(
            jax.ShapeDtypeStruct((3, HEAD_DIM, LEN), low),
            jax.ShapeDtypeStruct((6 * CHUNK, QUERIES), wide),
            jax.ShapeDtypeStruct((CTX, *x.shape), low),
            jax.ShapeDtypeStruct(grads.shape[:1] + grads.shape[2:], low),
            jax.ShapeDtypeStruct((ZED - 1, *late.shape[1:]), low),
        ),
        in_specs=[
            whole(3, HEAD_DIM, LEN),
            pl.BlockSpec((LEN, QUERIES), lambda i: (0, i)),
            pl.BlockSpec((HEAD_DIM, QUERIES), lambda i: (0, i)),
            pl.BlockSpec((1, QUERIES), lambda i: (0, i)),
            pl.BlockSpec((1, HEAD_DIM, QUERIES), lambda i: (0, 0, i)),
            ANY,
            ANY,
            ANY,
        ],
        out_specs=(whole(3, HEAD_DIM, LEN), whole(6 * CHUNK, QUERIES), ANY, ANY, ANY),
        scratch_shapes=[
            pltpu.VMEM((LEN, HEAD_DIM), low),
            pltpu.VMEM((LEN, HEAD_DIM), wide),
            pltpu.VMEM((LEN, HEAD_DIM), wide),
            pltpu.VMEM((6 * CHUNK, QUERIES), wide),
            pltpu.VMEM((LEN, QUERIES), low),
            pltpu.SemaphoreType.DMA,
            pltpu.SemaphoreType.DMA((17,)),
            pltpu.SemaphoreType.DMA((17,)),
            pltpu.SemaphoreType.DMA((4,)),
            pltpu.SemaphoreType.DMA((4,)),
        ],
        compiler_params=pltpu.CompilerParams(
            collective_id=ident, has_side_effects=True, vmem_limit_bytes=14 << 20
        ),
    )(
        qkv,
        pltpu.with_memory_space_constraint(probs, pltpu.HBM),
        out, inverse, grad_out, x, grads, late
    )


def finish_kernel(
    rows_ref, late_ref, others_ref, wq_ref, wkv_ref, gain_ref,
    gq_ref, gkv_ref, gout_ref, router_ref, gain_one_ref, gain_two_ref, table_ref,
):
    c, e, z, xh, k = spot()
    late = late_ref[e] + jnp.sum(others_ref[...], axis=0)
    gout_ref[...] = late[:6, :D]
    router_ref[...] = late[:6, D + 67 : D + 83]
    gain_two_ref[...] = late[:6, D + 65 : D + 66]
    parts = [
        jnp.concatenate(
            [rows_ref[h, :, n * HEAD_DIM : (n + 1) * HEAD_DIM] for h in range(HEADS)], axis=1
        )[:6]
        for n in range(3)
    ]
    gq_ref[...] = parts[0]
    gkv_ref[:, :D] = parts[1]
    gkv_ref[:, D:] = parts[2]
    along = jnp.sum(wq_ref[...].astype(wide) * parts[0], axis=1, keepdims=True)
    along = along + jnp.sum(wkv_ref[:, :D].astype(wide) * parts[1], axis=1, keepdims=True)
    along = along + jnp.sum(wkv_ref[:, D:].astype(wide) * parts[2], axis=1, keepdims=True)
    gain_one_ref[...] = along / gain_ref[...]
    device = c * EXP + e
    buckets = rows_ref[pl.ds(device % 4 * 3, 3), 6, :]
    chosen = lax.broadcasted_iota(jnp.int32, buckets.shape, 1) == device // 4
    table_ref[...] = jnp.sum(jnp.where(chosen, buckets, 0.0), axis=1, keepdims=True)


def finish(by_head, late, others, wq, wkv, gain):
    shapes = [(6, D), (6, 2 * D), (6, D), (6, 16), (6, 1), (6, 1), (3, 1)]
    return pl.pallas_call(
        finish_kernel,
        out_shape=[jax.ShapeDtypeStruct(s, wide) for s in shapes],
        compiler_params=pltpu.CompilerParams(vmem_limit_bytes=8 << 20),
    )(by_head, late, others, wq, wkv, gain.astype(wide)[:, None])


def plain(kernel, shapes, megabytes, *args):
    return pl.pallas_call(
        kernel,
        out_shape=[jax.ShapeDtypeStruct(shape, kind) for shape, kind in shapes],
        compiler_params=pltpu.CompilerParams(vmem_limit_bytes=megabytes << 20),
    )(*args)


def iota(shape, axis):
    return lax.broadcasted_iota(jnp.int32, shape, axis)


def pack_kernel(wq_ref, wkv_ref, wo_ref, extra_ref, out_ref):
    empty = jnp.zeros((4, 128), wide)
    extra = extra_ref[...].astype(wide)
    wq, wkv, wo = (ref[...].astype(wide) for ref in (wq_ref, wkv_ref, wo_ref))
    for h in range(HEADS):
        at = h * HEAD_DIM
        query, key = wq[:, at : at + HEAD_DIM], wkv[:, at : at + HEAD_DIM]
        value = wkv[:, D + at : D + at + HEAD_DIM]
        upper = jnp.concatenate([query, key], axis=1)
        lower = jnp.concatenate([value, extra], axis=1)
        out_ref[h] = jnp.concatenate([upper, lower, empty], axis=0).astype(low)
    for n in range(3):
        upper, lower = (wo[:, (2 * n + i) * 128 : (2 * n + i + 1) * 128] for i in range(2))
        out_ref[HEADS + n] = jnp.concatenate([upper, lower, empty], axis=0).astype(low)


def six_rows(rows, first):
    shape = (rows // 16 * 6, rows)
    column = iota((1, rows), 1)
    inner = column % 16 - first
    place = jnp.where((inner >= 0) & (inner < 6), column // 16 * 6 + inner, -1)
    return (iota(shape, 0) == place).astype(low)


def project_kernel(mine_ref, x_ref, eight_ref, qkv_ref, h_ref, table_ref, first_ref, second_ref):
    c, e, z, xh, k = spot()
    mine = mine_ref[...]
    upper = jnp.dot(six_rows(2048, 0), mine, preferred_element_type=wide)
    lower = jnp.dot(six_rows(2048, 6), mine, preferred_element_type=wide)
    lower_turned = lower.T
    gain = lower_turned[64:65, :]
    weight_qk, weight_v = upper.T.astype(low), lower_turned[:64].astype(low)
    for n in range(4):
        rows = slice(n * 512, (n + 1) * 512)
        x = x_ref[rows, :].astype(wide)
        scale = lax.rsqrt(jnp.mean(x * x, axis=1, keepdims=True) + epsilon)
        h = (x * scale * gain).astype(low)
        h_ref[rows, :] = h
        both = dot(weight_qk, h, (1, 1)).astype(low)
        qkv_ref[0, :, rows] = both[:64]
        qkv_ref[1, :, rows] = both[64:]
        qkv_ref[2, :, rows] = dot(weight_v, h, (1, 1)).astype(low)
    head = head_of(c)
    column = jnp.broadcast_to(lower[:, 66:67], (D, 128))
    row = iota((BUCKETS, D), 1)
    wanted = (row // 24 == iota((BUCKETS, D), 0)) & (row % 24 == head // 3 * 6 + head % 3)
    table_ref[...] = jnp.dot(wanted.astype(low), column.astype(low), preferred_element_type=wide)
    pick = [six_rows(128, 0), six_rows(128, 6)]
    part = lambda n, i: jnp.dot(
        pick[i], eight_ref[:, n].reshape(128, 128), preferred_element_type=wide
    )
    first_ref[:, :128] = part(0, 1).astype(low)
    for n in range(3):
        for i in range(2):
            at = 128 + (2 * n + i) * 128
            first_ref[:, at : at + 128] = part(HEADS + n, i).astype(low)
    for pair in range(HEADS // 2):
        pieces = []
        for h in (2 * pair, 2 * pair + 1):
            pieces += [part(h, 0), part(h, 1)[:, :64]]
        pieces = jnp.concatenate(pieces, axis=1).astype(low)
        if pair < 2:
            first_ref[:, 896 + pair * 384 : 896 + (pair + 1) * 384] = pieces
        else:
            second_ref[:, (pair - 2) * 384 : (pair - 1) * 384] = pieces


def route_kernel(
    att_ref, x_ref, cot_ref, route_ref, full_ref,
    residual_ref, h_ref, probs_ref, dispatch_ref, out_ref,
):
    wo, small = full_ref[:, 128:896], full_ref[:, :128]
    gain = small.astype(wide).T[65:66, :]
    attended = att_ref[...].astype(wide).T.astype(low)
    residual = x_ref[...].astype(wide) + jnp.dot(attended, wo, preferred_element_type=wide)
    residual_ref[...] = residual
    scale = lax.rsqrt(jnp.mean(residual * residual, axis=1, keepdims=True) + epsilon)
    h_two = (residual * scale * gain).astype(low)
    h_ref[...] = h_two
    logits = jnp.dot(h_two, small, preferred_element_type=wide)[:, 67:83]
    logits = jnp.exp(logits - jnp.max(logits, axis=1, keepdims=True))
    probs = logits / jnp.sum(logits, axis=1, keepdims=True)
    probs_ref[...] = probs
    route = route_ref[...]
    choose = (route == iota((TOK, 16), 1)).astype(wide)
    before = (iota((TOK, TOK), 1) < iota((TOK, TOK), 0)).astype(low)
    earlier = jnp.dot(before, choose.astype(low), preferred_element_type=wide)
    slot = jnp.sum(earlier * choose, axis=1, keepdims=True).astype(jnp.int32)
    target = route // 2 * SLOTS + route % 2 * CAP + slot
    places = iota((TOK, EXP * SLOTS), 1)
    dispatch = jnp.concatenate(
        [(places == target).astype(wide), (places == target + 2 * CAP).astype(wide)], axis=0
    )
    dispatch_ref[...] = dispatch.astype(low)
    gate = jnp.sum(probs * choose, axis=1, keepdims=True)
    grad_y = (gate * cot_ref[...].astype(wide)).astype(low)
    turned = dispatch.T.astype(low)
    out = jnp.dot(turned[:, :TOK], h_two, preferred_element_type=wide)
    out = out + jnp.dot(turned[:, TOK:], grad_y, preferred_element_type=wide)
    out_ref[...] = out.astype(low)


def combine_kernel(
    back_ref, dispatch_ref, residual_ref, cot_ref, probs_ref, route_ref, h_ref, full_ref, att_ref,
    mixed_ref, grad_ref, grad_att_ref, late_ref,
):
    wo, small = full_ref[:, 128:896], full_ref[:, :128]
    gain = small.astype(wide).T[65:66, :]
    returned = jnp.dot(dispatch_ref[...], back_ref[...], preferred_element_type=wide)
    tokens, grad_h = returned[:TOK], returned[TOK:]
    residual, probs = residual_ref[...], probs_ref[...]
    choose = (route_ref[...] == iota((TOK, 16), 1)).astype(wide)
    gate = jnp.sum(probs * choose, axis=1, keepdims=True)
    mixed_ref[...] = (residual + gate * tokens).astype(low)
    grad = cot_ref[...].astype(wide)
    grad_choice = choose * jnp.sum(grad * tokens, axis=1, keepdims=True)
    grad_logits = probs * (grad_choice - jnp.sum(probs * grad_choice, axis=1, keepdims=True))
    spread = (iota((16, 128), 0) + 67 == iota((16, 128), 1)).astype(low)
    upper = grad_logits.astype(low)
    lower = (grad_logits - upper.astype(wide)).astype(low)
    upper = jnp.dot(upper, spread, preferred_element_type=wide).astype(low)
    lower = jnp.dot(lower, spread, preferred_element_type=wide).astype(low)
    grad_h = grad_h + dot(upper, small, (1, 1)) + dot(lower, small, (1, 1))
    scale = lax.rsqrt(jnp.mean(residual * residual, axis=1, keepdims=True) + epsilon)
    along = grad_h * gain
    mean = jnp.mean(along * residual, axis=1, keepdims=True)
    grad = grad + scale * along - (scale * scale * scale * mean) * residual
    grad_ref[...] = grad
    branch = grad.astype(low)
    grad_att_ref[...] = dot(wo, branch, (1, 1)).astype(low)
    late_ref[:, :D] = jnp.dot(att_ref[...], branch, preferred_element_type=wide).astype(low)
    turned = h_ref[...].astype(wide).T.astype(low)
    extra = jnp.dot(turned, upper, preferred_element_type=wide)
    extra = extra + jnp.dot(turned, lower, preferred_element_type=wide)
    gains = (grad_h * residual * scale).T
    gains = jnp.sum(gains, axis=1, keepdims=True)
    late_ref[:, D:] = jnp.where(iota((D, 128), 1) == 65, gains, extra).astype(low)


def expert_kernel(lists_ref, in_ref, out_ref, partial_ref, grad_in_ref, grad_out_ref):
    for n in range(2):
        rows = lists_ref[:, n].reshape(ZED * 80, D)
        grads = lists_ref[:, 2 + n].reshape(ZED * 80, D)
        weight_in, weight_out = in_ref[n], out_ref[n]
        pre = dot(rows, weight_in, (1, 1))
        square = pre * pre
        bend = jnp.tanh(0.7978845608028654 * (pre + 0.044715 * square * pre))
        hidden = (0.5 * pre * (1.0 + bend)).astype(low)
        slope = 0.5 * (1.0 + bend) + 0.5 * pre * (1.0 - bend * bend) * (
            0.7978845608028654 * (1.0 + 0.134145 * square)
        )
        grad_pre = (dot(grads, weight_out, (1, 1)) * slope).astype(low)
        y = jnp.dot(hidden, weight_out, preferred_element_type=wide).astype(low)
        partial_ref[:, n * 80 : (n + 1) * 80, :] = y.reshape(ZED, 80, D)
        back = jnp.dot(grad_pre, weight_in, preferred_element_type=wide).astype(low)
        partial_ref[:, 160 + n * 80 : 160 + (n + 1) * 80, :] = back.reshape(ZED, 80, D)
        grad_in_ref[n] = dot(grad_pre, rows, (0, 0)).astype(low)
        grad_out_ref[n] = dot(hidden, grads, (0, 0)).astype(low)


def unlist_kernel(partial_ref, others_ref, out_ref):
    c, e, z, xh, k = spot()
    total = partial_ref[z].astype(wide) + jnp.sum(others_ref[...].astype(wide), axis=0)
    row = iota((EXP * SLOTS, 1), 0)
    inner = row % SLOTS
    source = jnp.where(inner < 4 * CAP, inner // CAP * 80 + row // SLOTS * CAP + inner % CAP, -1)
    pick = (iota((EXP * SLOTS, 320), 1) == source).astype(low)
    out = jnp.dot(pick, total.astype(low), preferred_element_type=wide).astype(low)
    out_ref[...] = out.reshape(EXP, SLOTS, D)


def head_weights_kernel(grads_ref, h_ref, tiles_ref, late_ref, others_ref, out_ref, sum_ref):
    c, e, z, xh, k = spot()
    grads = grads_ref[...].reshape(192, LEN)
    product = jnp.dot(grads, h_ref[...], preferred_element_type=wide).astype(low)
    column = iota((1, EXP * TOK), 1)
    place = (column % TOK // 8 * EXP + column // TOK) * 6 + column % 8
    place = jnp.where(column % 8 < 6, place, -1)
    by_owner = (iota((D, EXP * TOK), 0) == place).astype(low)
    product = jnp.dot(product, by_owner, preferred_element_type=wide).T
    tile = lambda n, half: tiles_ref[
        n * CHUNK : (n + 1) * CHUNK, half * TOK : (half + 1) * TOK
    ]
    near = jnp.concatenate([tile(n, 0) + tile(n + 1, 1) for n in (1, 2, 3)], axis=0)
    ids = near_buckets(near.shape, CHUNK)
    lane = iota((1, 192), 1)
    buckets = jnp.zeros((1, 192), wide)
    for b in range(BUCKETS):
        part = jnp.sum(jnp.where(ids == b, near, 0.0), axis=0, keepdims=True)
        if b == BUCKETS // 2 - 1:
            part = part + jnp.sum(tile(0, 0) + tile(0, 1) + tile(1, 1), axis=0, keepdims=True)
        if b == BUCKETS - 1:
            part = part + jnp.sum(tile(4, 0) + tile(5, 0) + tile(5, 1), axis=0, keepdims=True)
        buckets = jnp.where(lane == b, jnp.sum(part, axis=1, keepdims=True), buckets)
    sixth = iota((EXP * TOK, 1), 0) % 8 == 6
    product = jnp.where(sixth, buckets, product)
    out_ref[...] = product.astype(low).reshape(EXP, TOK, 192)
    total = late_ref[z].astype(wide) + jnp.sum(others_ref[...].astype(wide), axis=0)
    sum_ref[...] = total.astype(low)


def owners_kernel(own_ref, others_ref, late_ref, late_others_ref, out_ref, sum_ref):
    c, e, z, xh, k = spot()
    total = own_ref[e].astype(wide) + jnp.sum(others_ref[...].astype(wide), axis=0)
    out_ref[...] = total.reshape(CTX, 8, 192)
    late = late_ref[xh].astype(wide) + late_others_ref[0].astype(wide)
    empty = jnp.zeros((2, 896), wide)
    for n in range(EXP):
        sum_ref[n] = jnp.concatenate([late[6 * n : 6 * n + 6], empty], axis=0)


def tokens_kernel(grads_ref, first_ref, second_ref, x_ref, residual_ref, out_ref):
    grads = grads_ref[...].reshape(3 * D, TOK).astype(wide).T.astype(low)
    grad_h = dot(grads[:, :D], first_ref[:, 896:], (1, 1))
    grad_h = grad_h + dot(grads[:, D:], second_ref[...], (1, 1))
    gain = first_ref[:, :128].astype(wide).T[64:65, :]
    x = x_ref[...].astype(wide)
    scale = lax.rsqrt(jnp.mean(x * x, axis=1, keepdims=True) + epsilon)
    along = grad_h * gain
    mean = jnp.mean(along * x, axis=1, keepdims=True)
    out_ref[...] = residual_ref[...] + scale * along - (scale * scale * scale * mean) * x


def dot(a, b, dims=(1, 0)):
    return lax.dot_general(
        a, b, (((dims[0],), (dims[1],)), ((), ())), preferred_element_type=wide
    )


def shards(
    tokens,
    cotangent,
    routes,
    query_weight,
    kv_weight,
    out_weight,
    norm_gain_one,
    norm_gain_two,
    router_weight,
    bias_table,
    expert_in,
    expert_out,
):
    extra = jnp.concatenate(
        [
            norm_gain_one[:, None],
            norm_gain_two[:, None],
            jnp.pad(bias_table, (0, 3))[:, None],
            router_weight,
            jnp.zeros((6, 45), low),
        ],
        axis=1,
    )
    packed = plain(
        pack_kernel, [((15, 16, 128), low)], 4, query_weight, kv_weight, out_weight, extra
    )[0]
    eight, mine, x_all = opening(packed, tokens[0], 1)
    head_qkv, h_all, head_table, block, block_qkv = plain(
        project_kernel,
        [
            ((3, HEAD_DIM, LEN), low),
            ((LEN, D), low),
            ((BUCKETS, 128), wide),
            ((48, 128 + 2 * D), low),
            ((48, 2 * D), low),
        ],
        28,
        mine.reshape(2048, 128),
        x_all.reshape(LEN, D),
        eight,
    )
    probs, attended, attended_head, inverse, full, experts_out = attend(
        head_qkv, head_table, block, expert_out, 18
    )
    full = full.reshape(D, 2 * D + 128)
    attended_low = from_heads(attended_head, 5).reshape(D, TOK)
    routed = (TOK, D)
    residual, h_two, route_probs, dispatch, outgoing = plain(
        route_kernel,
        [
            (routed, wide),
            (routed, low),
            ((TOK, 16), wide),
            ((2 * TOK, EXP * SLOTS), low),
            ((EXP * SLOTS, D), low),
        ],
        16,
        attended_low,
        tokens[0],
        cotangent[0],
        routes[0],
        full,
    )
    received = swap(outgoing.reshape(EXP, SLOTS, D), "exp", 6, 0).reshape(EXP * SLOTS, D)

    row = jnp.arange(4 * 80, dtype=jnp.int32)
    source = row % 80 // CAP * SLOTS + row // 80 * CAP + row % CAP
    compact = (source[:, None] == jnp.arange(EXP * SLOTS, dtype=jnp.int32)[None, :]).astype(low)
    lists, experts_in = gather_lists(
        dot(compact, received).astype(low), jnp.swapaxes(expert_in, 1, 2), 7
    )
    lists = lists.reshape(ZED, 4, 80, D)
    experts_here = experts_in.reshape(2, D, D), experts_out.reshape(2, D, D)
    partial, grads_in, grads_out = plain(
        expert_kernel,
        [((ZED, 320, D), low), ((2, D, D), low), ((2, D, D), low)],
        28,
        lists,
        *experts_here,
    )
    grads_out = grads_out.reshape(2, 2, 2, 192, D)
    others, grads_own, grads_other = return_lists(partial, grads_out, 8)
    grad_expert_out = grads_own.astype(wide) + grads_other.astype(wide)
    spread = plain(unlist_kernel, [((EXP, SLOTS, D), low)], 12, partial, others)[0]
    expert_grads = grads_in.reshape(2, 2, 2, 192, D)
    back, others = swaps(9, (spread, "exp", 0, True), (expert_grads, "core", 2, False))
    expert_grads = add_up(expert_grads, "core", 2, others).astype(low)
    mixed_rows, grad_residual, grad_attended, late = plain(
        combine_kernel,
        [(routed, low), (routed, wide), ((D, TOK), low), ((D, 896), low)],
        20,
        back.reshape(EXP * SLOTS, D),
        dispatch,
        residual,
        cotangent[0],
        route_probs,
        routes[0],
        h_two,
        full,
        attended_low,
    )
    late = late.reshape(8, 2, 48, 896)
    head_grad, others = swaps(
        10,
        (grad_attended.reshape(1, HEADS, HEAD_DIM, TOK), "to_heads", None, True),
        (late, "core", 1, False),
    )
    late = add_up(late, "core", 1, others).astype(low).reshape(ZED, 2, 48, 896)
    head_grads, tile_sums, qkv_full, others, late_others = attend_back(
        head_qkv, probs, attended, inverse, head_grad, block_qkv, expert_grads, late, 19
    )
    qkv_full = qkv_full.reshape(D, 2 * D)
    grad_expert_in = jnp.swapaxes(add_up(expert_grads, "x", 1, others[None]), 1, 2)

    head_weights, late = plain(
        head_weights_kernel,
        [((EXP, TOK, 192), low), ((2, 48, 896), low)],
        20,
        head_grads,
        h_all,
        tile_sums,
        late,
        late_others,
    )
    others, late_others = swaps(
        11, (head_weights, "exp", 0, False), (late, "x", 0, False)
    )
    head_weights, late = plain(
        owners_kernel,
        [((CTX, 8, 192), wide), ((EXP, 8, 896), wide)],
        8,
        head_weights,
        others,
        late,
        late_others,
    )
    grad_qkv, by_head, others = swaps(
        12,
        (head_grads, "from_heads", None, True),
        (head_weights, "head_rows", None, True),
        (late, "exp", 0, False),
    )
    finished = finish(by_head, late, others, query_weight, kv_weight, norm_gain_one)

    grad_tokens = plain(
        tokens_kernel, [(routed, wide)], 16, grad_qkv, full, qkv_full, tokens[0], grad_residual
    )[0]
    return (
        mixed_rows[None],
        grad_tokens[None],
        *finished[:3],
        finished[4][:, 0],
        finished[5][:, 0],
        finished[3],
        finished[6][:, 0],
        grad_expert_in,
        grad_expert_out,
    )


def solution(mesh):
    rows = P("exp", "ctx", None)
    shared, vector = P(("ctx", "exp"), None), P(("ctx", "exp"))
    expert_in, expert_out = P("exp", None, "ctx"), P("exp", "ctx", None)
    return jax.shard_map(
        shards,
        mesh=mesh,
        in_specs=(rows, rows, rows, shared, shared, shared, vector, vector, shared, vector)
        + (expert_in, expert_out),
        out_specs=(rows, rows, shared, shared, shared, vector, vector, shared, vector)
        + (expert_in, expert_out),
        check_vma=False,
    )
```

```python
import functools

import jax
import jax.numpy as jnp
from jax import lax
from jax.experimental import pallas as pl
from jax.experimental.pallas import tpu as pltpu
from jax.sharding import PartitionSpec as P

MESH = pl.DeviceIdType.MESH
HEADS = 12
HEAD_DIM = 64
BUCKETS = 32
TOK = 128
D = 768
CAP = 10
SLOTS = 48
CTX, EXP, ZED = 16, 8, 4
LEN = TOK * CTX
QUERIES = 256
CHUNK = 128
epsilon = 1e-06
bucket_edges = (12, 16, 23, 32, 46, 64, 91)
low = jnp.bfloat16
wide = jnp.float32
ANY = pl.BlockSpec(memory_space=pl.ANY)


def spot():
    c, e = lax.axis_index("ctx"), lax.axis_index("exp")
    return c, e, c // 4, (c // 2) % 2, c % 2


def greet(peers):
    barrier = pltpu.get_barrier_semaphore()
    for peer in peers:
        pl.semaphore_signal(barrier, inc=1, device_id=peer, device_id_type=MESH)
    pl.semaphore_wait(barrier, len(peers))


def push(src, dst, send, recv, to):
    return pltpu.make_async_remote_copy(
        src_ref=src, dst_ref=dst, send_sem=send, recv_sem=recv, device_id=to, device_id_type=MESH
    )


def group(kind):
    c, e, z, xh, k = spot()
    if kind == "exp":
        return EXP, e, lambda i: (c, i)
    if kind == "z":
        return ZED, z, lambda i: (i * 4 + xh * 2 + k, e)
    if kind == "x":
        return 2, xh, lambda i: (z * 4 + i * 2 + k, e)
    if kind == "core":
        return 2, k, lambda i: (z * 4 + xh * 2 + i, e)
    if kind == "quad":
        return 4, xh * 2 + k, lambda i: (z * 4 + i, e)
    return CTX, c, lambda i: (i, e)


SIZES = {"exp": EXP, "z": ZED, "x": 2, "core": 2, "quad": 4}


def head_of(c):
    return jnp.minimum((c // 4) * 3 + c % 4, HEADS - 1)


def owns(c):
    return c % 4 < 3


def columns(c):
    return pl.ds(pl.multiple_of(c * TOK, TOK), TOK)


def when(condition, step):
    if condition is None:
        step()
    else:
        pl.when(condition)(step)


def heads_parts(kind, me, x, out):
    if kind == "to_heads":
        return lambda to: x.at[:, head_of(to)], out.at[:, :, columns(me)], None, owns
    if kind == "from_heads":
        return lambda to: x.at[:, :, columns(to)], out.at[head_of(me)], owns, None
    return lambda to: x.at[to], out.at[head_of(me)], owns, None


def swaps_kernel(plan, *refs):
    n = len(plan)
    xs, outs, (send, recv, here) = refs[:n], refs[n : 2 * n], refs[2 * n :]
    kinds = dict.fromkeys("ctx" if kind not in SIZES else kind for kind, axis, keep in plan)
    if "ctx" in kinds:
        kinds = [kind for kind in kinds if kind in ("ctx", "exp")]
    peers = []
    for kind in kinds:
        size, me, device = group(kind)
        peers += [device(lax.rem(me + i, size)) for i in range(1, size)]
    greet(peers)
    copies, count = [], 0
    for (kind, axis, keep), x, out in zip(plan, xs, outs):
        size, me, device = group(kind)
        if kind in SIZES:
            part = lambda i: x if axis is None else x.at[(slice(None),) * axis + (i,)]
            sends = receives = None
        else:
            part, place, sends, receives = heads_parts(kind, me, x, out)
        for i in range(1, size):
            to, source = lax.rem(me + i, size), lax.rem(me + size - i, size)
            if kind in SIZES:
                place = out.at[me if keep else i - 1]
            copy = push(part(to), place, send.at[count], recv.at[count], device(to))
            if sends is not None:
                out_if, in_if = sends(me), sends(source)
            elif receives is not None:
                out_if, in_if = receives(to), receives(me)
            else:
                out_if = in_if = None
            when(out_if, copy.start)
            copies.append((copy, out_if, in_if))
            count += 1
    own = []
    for n, ((kind, axis, keep), x, out) in enumerate(zip(plan, xs, outs)):
        size, me, device = group(kind)
        if kind in SIZES and keep:
            part = x if axis is None else x.at[(slice(None),) * axis + (me,)]
            own.append((pltpu.make_async_copy(part, out.at[me], here.at[n]), None))
        elif kind not in SIZES:
            part, place, sends, receives = heads_parts(kind, me, x, out)
            own.append((pltpu.make_async_copy(part(me), place, here.at[n]), owns(me)))
    for copy, condition in own:
        when(condition, copy.start)
    for copy, out_if, in_if in copies:
        when(out_if, copy.wait_send)
        when(in_if, copy.wait_recv)
    for copy, condition in own:
        when(condition, copy.wait)


def swaps(ident, *items):
    shapes, total = [], 0
    for x, kind, axis, keep in items:
        block = x.shape if axis is None else x.shape[:axis] + x.shape[axis + 1 :]
        if kind == "to_heads":
            shape = (x.shape[0], HEAD_DIM, LEN)
        elif kind == "from_heads":
            shape = (HEADS, x.shape[0], HEAD_DIM, TOK)
        elif kind == "head_rows":
            shape = (HEADS, *x.shape[1:])
        else:
            shape = (SIZES[kind] - (not keep), *block)
        shapes.append(jax.ShapeDtypeStruct(shape, x.dtype))
        total += SIZES.get(kind, CTX) - 1
    return pl.pallas_call(
        functools.partial(swaps_kernel, [item[1:] for item in items]),
        out_shape=shapes,
        in_specs=[ANY] * len(items),
        out_specs=[ANY] * len(items),
        scratch_shapes=[
            pltpu.SemaphoreType.DMA((total,)),
            pltpu.SemaphoreType.DMA((total,)),
            pltpu.SemaphoreType.DMA((len(items),)),
        ],
        compiler_params=pltpu.CompilerParams(
            collective_id=ident, has_side_effects=True, vmem_limit_bytes=2 << 20
        ),
    )(*[item[0] for item in items])


def swap(x, kind, ident, axis=None):
    return swaps(ident, (x, kind, axis, True))[0]


def add_up(x, kind, axis, others):
    mine = lax.dynamic_index_in_dim(x, group(kind)[1], axis, keepdims=False)
    return mine.astype(wide) + jnp.sum(others.astype(wide), axis=0)


def quad_slab(out, xh, k):
    return out.at[:, xh * 2 + k]


def quad_parts(w, out, here, send, recv):
    c, e, z, xh, k = spot()
    side, twin = (z * 4 + (1 - xh) * 2 + k, e), (z * 4 + xh * 2 + 1 - k, e)
    mine, theirs = quad_slab(out, xh, k), quad_slab(out, 1 - xh, k)
    across = push(w, mine, send.at[0], recv.at[0], side)
    pair = push(w, mine, send.at[1], recv.at[1], twin)
    hand = push(theirs, theirs, send.at[2], recv.at[2], twin)
    own = pltpu.make_async_copy(w, mine, here)

    def begin():
        across.start()
        pair.start()
        own.start()

    def forward():
        across.wait_recv()
        hand.start()

    def end():
        across.wait_send()
        pair.wait()
        hand.wait()
        own.wait()

    return begin, forward, end


def ring_parts(src, at, send, recv):
    c, e, z, xh, k = spot()
    size, me, device = group("z")
    above, below, beyond = (lax.rem(me + i, 4) for i in (1, 3, 2))
    rows = src.shape[0]
    cut = rows // 32 * 16
    upper, lower = pl.ds(0, rows - cut), pl.ds(rows - cut, cut)
    up = push(src, at(me), send.at[0], recv.at[0], device(above))
    down = push(src, at(me), send.at[1], recv.at[1], device(below))
    on_up = at(below).at[upper, :]
    on_down = at(above).at[lower, :]
    on_up = push(on_up, on_up, send.at[2], recv.at[2], device(above))
    on_down = push(on_down, on_down, send.at[3], recv.at[3], device(below))

    def begin():
        up.start()
        down.start()

    def relay():
        up.wait_recv()
        on_up.start()
        down.wait_recv()
        on_down.start()

    def arrive():
        on_up.wait_recv()
        on_down.wait_recv()

    def end():
        for copy in (up, down, on_up, on_down):
            copy.wait_send()

    return begin, relay, arrive, end


def spread_parts(x, out, here, send, recv):
    c, e, z, xh, k = spot()
    at = lambda z, xh, k: z * 4 + xh * 2 + k
    around = [lax.rem(z + i, 4) for i in (3, 1, 2)]
    side, twin = (at(z, 1 - xh, k), e), (at(z, xh, 1 - k), e)
    mine, theirs = at(z, xh, k), at(z, 1 - xh, k)
    held = [mine, theirs] + [at(p, xh, k) for p in around] + [at(p, 1 - xh, k) for p in around]
    across = push(x, out.at[mine], send.at[0], recv.at[0], side)
    first = ring_parts(
        x, lambda p: out.at[at(p, xh, k)], send.at[pl.ds(1, 4)], recv.at[pl.ds(1, 4)]
    )
    second = ring_parts(
        out.at[theirs],
        lambda p: out.at[at(p, 1 - xh, k)],
        send.at[pl.ds(5, 4)],
        recv.at[pl.ds(5, 4)],
    )
    pair = [
        push(x if n == 0 else out.at[b], out.at[b], send.at[9 + n], recv.at[9 + n], twin)
        for n, b in enumerate(held)
    ]
    own = pltpu.make_async_copy(x, out.at[mine], here)

    def begin():
        across.start()
        first[0]()
        pair[0].start()
        own.start()

    def middle():
        across.wait_recv()
        second[0]()
        pair[1].start()

    def relay_first():
        first[1]()
        pair[2].start()
        pair[3].start()

    def relay_second():
        second[1]()
        pair[5].start()
        pair[6].start()

    def end():
        first[2]()
        pair[4].start()
        second[2]()
        pair[7].start()
        for copy in pair:
            copy.wait()
        across.wait_send()
        first[3]()
        second[3]()
        own.wait()

    return begin, middle, relay_first, relay_second, end


def cross_peers():
    c, e, z, xh, k = spot()
    at = lambda z, xh, k: (z * 4 + xh * 2 + k, e)
    return [at(z, 1 - xh, k), at(z, xh, 1 - k)] + [at(lax.rem(z + i, 4), xh, k) for i in (1, 2, 3)]


def open_kernel(packed, x, eight, mine, x_all, here, send, recv, x_send, x_recv):
    c, e, z, xh, k = spot()
    exps = [lax.rem(e + i, EXP) for i in range(1, EXP)]
    peers = [lax.rem(c + i, CTX) for i in range(1, CTX)]
    greet([(c, p) for p in exps] + [(p, e) for p in peers])
    x_begin, x_middle, x_first, x_second, x_end = spread_parts(
        x, x_all, here.at[0], x_send, x_recv
    )
    rows = [
        push(packed, eight.at[e], send.at[i], recv.at[i], (c, p)) for i, p in enumerate(exps)
    ]
    own_rows = pltpu.make_async_copy(packed, eight.at[e], here.at[1])
    for copy in rows:
        copy.start()
    own_rows.start()
    x_begin()
    x_middle()
    for copy in rows:
        copy.wait_recv()
    own_rows.wait()
    heads = [
        push(eight.at[:, head_of(p)], mine.at[c], send.at[6 + i], recv.at[6 + i], (p, e))
        for i, p in enumerate(peers, 1)
    ]
    own_head = pltpu.make_async_copy(eight.at[:, head_of(c)], mine.at[c], here.at[2])
    for p, copy in zip(peers, heads):
        pl.when(owns(p))(copy.start)
    pl.when(owns(c))(own_head.start)
    x_first()
    x_second()
    for p, copy in zip(peers, heads):
        pl.when(owns(p))(copy.wait_send)
        pl.when(owns(c))(copy.wait_recv)
    pl.when(owns(c))(own_head.wait)
    x_end()
    for copy in rows:
        copy.wait_send()


def opening(packed, x, ident):
    shapes = ((EXP, *packed.shape), (CTX, EXP, *packed.shape[1:]), (CTX, *x.shape))
    sems = pltpu.SemaphoreType.DMA
    return pl.pallas_call(
        open_kernel,
        out_shape=[jax.ShapeDtypeStruct(s, low) for s in shapes],
        in_specs=[ANY, ANY],
        out_specs=[ANY] * 3,
        scratch_shapes=[sems((3,)), sems((22,)), sems((22,)), sems((17,)), sems((17,))],
        compiler_params=pltpu.CompilerParams(
            collective_id=ident, has_side_effects=True, vmem_limit_bytes=2 << 20
        ),
    )(packed, x)


def lists_kernel(x, w, x_all, w_all, here, send, recv, w_send, w_recv):
    c, e, z, xh, k = spot()
    greet(cross_peers())
    me = group("z")[1]
    x_begin, x_relay, x_arrive, x_end = ring_parts(x, lambda p: x_all.at[p], send, recv)
    w_begin, w_forward, w_end = quad_parts(w, w_all, here.at[0], w_send, w_recv)
    own = pltpu.make_async_copy(x, x_all.at[me], here.at[1])
    x_begin()
    w_begin()
    own.start()
    x_relay()
    w_forward()
    x_arrive()
    x_end()
    own.wait()
    w_end()


def gather_lists(x, w, ident):
    sems = pltpu.SemaphoreType.DMA
    shapes = ((ZED, *x.shape), (2, 4, *w.shape[1:]))
    return pl.pallas_call(
        lists_kernel,
        out_shape=[jax.ShapeDtypeStruct(s, low) for s in shapes],
        in_specs=[pl.BlockSpec(memory_space=pltpu.VMEM)] * 2,
        out_specs=[ANY] * 2,
        scratch_shapes=[sems((2,)), sems((4,)), sems((4,)), sems((3,)), sems((3,))],
        compiler_params=pltpu.CompilerParams(
            collective_id=ident, has_side_effects=True, vmem_limit_bytes=4 << 20
        ),
    )(x, w)


def return_kernel(x, g, x_out, g_own, g_out, held, total, here, send, recv, g_send, g_recv):
    c, e, z, xh, k = spot()
    greet(cross_peers())
    size, me, device = group("z")
    copies = []
    for i in range(1, size):
        to = lax.rem(me + i, size)
        copies.append(push(x.at[to], x_out.at[i - 1], send.at[i - 1], recv.at[i - 1], device(to)))
    twin, side = group("core")[2](1 - k), group("x")[2](1 - xh)
    across = push(g.at[:, :, 1 - k], held, g_send.at[0], g_recv.at[0], twin)
    across.start()
    for copy in copies:
        copy.start()
    across.wait()

    def add(n, carry):
        a, b, rows = n // 8, n // 4 % 2, pl.ds(pl.multiple_of(n % 4 * 48, 16), 48)
        both = g[a, b, k, rows, :].astype(wide) + held[a, b, rows, :].astype(wide)
        total[a, b, rows, :] = both.astype(low)
        return carry

    lax.fori_loop(0, 16, add, 0)
    other = push(total.at[:, 1 - xh], g_out, g_send.at[1], g_recv.at[1], side)
    other.start()
    own = pltpu.make_async_copy(total.at[:, xh], g_own, here)
    own.start()
    own.wait()
    for copy in copies:
        copy.wait()
    other.wait()


def return_lists(x, g, ident):
    sems = pltpu.SemaphoreType.DMA
    half = (2, *g.shape[3:])
    return pl.pallas_call(
        return_kernel,
        out_shape=[
            jax.ShapeDtypeStruct(s, low) for s in ((ZED - 1, *x.shape[1:]), half, half)
        ],
        in_specs=[ANY, pl.BlockSpec(memory_space=pltpu.VMEM)],
        out_specs=[ANY] * 3,
        scratch_shapes=[
            pltpu.VMEM((2, 2, *g.shape[3:]), low),
            pltpu.VMEM((2, 2, *g.shape[3:]), low),
            sems,
            sems((3,)),
            sems((3,)),
            sems((2,)),
            sems((2,)),
        ],
        compiler_params=pltpu.CompilerParams(
            collective_id=ident, has_side_effects=True, vmem_limit_bytes=7 << 20
        ),
    )(x, g)


def to_heads(x, ident):
    return swaps(ident, (x, "to_heads", None, True))[0]


def from_heads(x, ident):
    return swaps(ident, (x, "from_heads", None, True))[0]


def near_buckets(shape, before):
    offset = (
        lax.broadcasted_iota(jnp.int32, shape, 0)
        - before
        - lax.broadcasted_iota(jnp.int32, shape, 1)
    )
    distance = jnp.abs(offset)
    far = jnp.full(shape, 8, jnp.int32)
    for edge in bucket_edges:
        far = far + (distance >= edge).astype(jnp.int32)
    return jnp.where(distance < 8, distance, far) + jnp.where(offset > 0, BUCKETS // 2, 0)


def tile_rows(chunk, block):
    tile = jnp.clip(chunk - 2 * block + 2, 0, 5)
    return pl.ds(pl.multiple_of(tile * CHUNK, CHUNK), CHUNK)


def chunk_rows(chunk):
    return pl.ds(pl.multiple_of(chunk * CHUNK, CHUNK), CHUNK)


def forward_kernel(
    qkv_ref, table_ref, x_ref, w_ref, p_ref, o_ref, low_ref, inv_ref, x_all, w_all,
    keys, bias, scores, here, x_send, x_recv, w_send, w_recv,
):
    block = pl.program_id(0)
    x_begin, x_middle, x_first, x_second, x_end = spread_parts(
        x_ref, x_all, here.at[0], x_send, x_recv
    )
    w_begin, w_forward, w_end = quad_parts(w_ref, w_all, here.at[1], w_send, w_recv)

    @pl.when(block == 0)
    def _():
        greet(cross_peers())
        x_begin()
        w_begin()

    @pl.when(block == 2)
    def _():
        x_middle()

    @pl.when(block == 4)
    def _():
        x_first()

    @pl.when(block == 6)
    def _():
        x_second()

    @pl.when(block == 0)
    def _():
        keys[...] = qkv_ref[1].T
        ids = near_buckets(bias.shape, 2 * CHUNK)
        tiles = jnp.zeros(ids.shape, wide)
        for b in range(BUCKETS):
            tiles = jnp.where(ids == b, table_ref[b : b + 1, 0:1], tiles)
        bias[...] = tiles

    here = pl.ds(pl.multiple_of(block * QUERIES, QUERIES), QUERIES)
    queries = qkv_ref[0, :, here]

    def score(chunk, top):
        rows = chunk_rows(chunk)
        part = jnp.dot(keys[rows, :], queries, preferred_element_type=wide)
        part = part + bias[tile_rows(chunk, block), :]
        scores[rows, :] = part
        return jnp.maximum(top, jnp.max(part.reshape(CHUNK // 8, 8, QUERIES), axis=0))

    top = lax.fori_loop(
        0, LEN // CHUNK, score, jnp.full((8, QUERIES), -1e30, wide), unroll=4
    )
    top = jnp.max(top, axis=0, keepdims=True)

    def weigh(chunk, total):
        rows = chunk_rows(chunk)
        part = jnp.exp(scores[rows, :] - top)
        p_ref[rows, :] = part.astype(low)
        return total + jnp.sum(part.reshape(CHUNK // 8, 8, QUERIES), axis=0)

    total = lax.fori_loop(0, LEN // CHUNK, weigh, jnp.zeros((8, QUERIES), wide), unroll=4)
    inverse = 1.0 / jnp.sum(total, axis=0, keepdims=True)
    out = jnp.dot(qkv_ref[2], p_ref[...], preferred_element_type=wide) * inverse
    o_ref[...] = out
    low_ref[0] = out.astype(low)
    inv_ref[...] = inverse


    @pl.when(block == LEN // QUERIES - 1)
    def _():
        w_forward()
        x_end()
        w_end()


def attend(qkv, table, x, w, ident):
    whole = lambda *shape: pl.BlockSpec(shape, lambda i: (0,) * len(shape))
    return pl.pallas_call(
        forward_kernel,
        grid=(LEN // QUERIES,),
        out_shape=(
            pltpu.HBM((LEN, LEN), low),
            pltpu.HBM((HEAD_DIM, LEN), wide),
            jax.ShapeDtypeStruct((1, HEAD_DIM, LEN), low),
            jax.ShapeDtypeStruct((1, LEN), wide),
            pltpu.HBM((CTX, *x.shape), low),
            pltpu.HBM((2, 4, *w.shape[1:]), low),
        ),
        in_specs=[whole(3, HEAD_DIM, LEN), whole(BUCKETS, 128), ANY, whole(*w.shape)],
        out_specs=(
            pl.BlockSpec((LEN, QUERIES), lambda i: (0, i)),
            pl.BlockSpec((HEAD_DIM, QUERIES), lambda i: (0, i)),
            pl.BlockSpec((1, HEAD_DIM, QUERIES), lambda i: (0, 0, i)),
            pl.BlockSpec((1, QUERIES), lambda i: (0, i)),
            ANY,
            ANY,
        ),
        scratch_shapes=[
            pltpu.VMEM((LEN, HEAD_DIM), low),
            pltpu.VMEM((6 * CHUNK, QUERIES), wide),
            pltpu.VMEM((LEN, QUERIES), wide),
            pltpu.SemaphoreType.DMA((2,)),
            pltpu.SemaphoreType.DMA((17,)),
            pltpu.SemaphoreType.DMA((17,)),
            pltpu.SemaphoreType.DMA((3,)),
            pltpu.SemaphoreType.DMA((3,)),
        ],
        compiler_params=pltpu.CompilerParams(
            collective_id=ident, has_side_effects=True, vmem_limit_bytes=13 << 20
        ),
    )(qkv, table, x, w)


def backward_kernel(
    qkv_ref, p_ref, o_ref, inv_ref, do_ref, x_ref, g_ref, l_ref,
    grad_ref, sums_ref, x_all, g_out, l_out,
    values, dk, dv, tiles, slopes, here, x_send, x_recv, send, recv,
):
    block = pl.program_id(0)
    x_begin, x_middle, x_first, x_second, x_end = spread_parts(
        x_ref, x_all, here, x_send, x_recv
    )
    size, me, device = group("x")
    across = push(g_ref.at[:, 1 - me], g_out, send.at[0], recv.at[0], device(1 - me))
    size, z, device_z = group("z")
    around = []
    for i in range(1, size):
        to = lax.rem(z + i, size)
        around.append(
            push(l_ref.at[to], l_out.at[i - 1], send.at[i], recv.at[i], device_z(to))
        )

    @pl.when(block == 0)
    def _():
        greet(cross_peers())
        x_begin()

    @pl.when(block == 2)
    def _():
        x_middle()
        across.start()

    @pl.when(block == 3)
    def _():
        x_first()
        for copy in around:
            copy.start()

    @pl.when(block == 5)
    def _():
        x_second()

    @pl.when(block == 0)
    def _():
        values[...] = qkv_ref[2].T
        dk[...] = jnp.zeros(dk.shape, wide)
        dv[...] = jnp.zeros(dv.shape, wide)
        tiles[...] = jnp.zeros(tiles.shape, wide)

    here = pl.ds(pl.multiple_of(block * QUERIES, QUERIES), QUERIES)
    scaled = (do_ref[0].astype(wide) * inv_ref[...]).astype(low)
    delta = jnp.sum(scaled.astype(wide) * o_ref[...], axis=0, keepdims=True)

    def slope(chunk, carry):
        rows = chunk_rows(chunk)
        part = jnp.dot(values[rows, :], scaled, preferred_element_type=wide)
        part = p_ref[rows, :].astype(wide) * (part - delta)
        slopes[rows, :] = part.astype(low)
        near = tile_rows(chunk, block)
        tiles[near, :] = tiles[near, :] + part
        return carry

    lax.fori_loop(0, LEN // CHUNK, slope, 0, unroll=4)
    grad_ref[0, :, here] = jnp.dot(
        qkv_ref[1], slopes[...], preferred_element_type=wide
    ).astype(low)
    queries = qkv_ref[0, :, here].T
    turned = scaled.T

    def gather(chunk, carry):
        rows = pl.ds(pl.multiple_of(chunk * 512, 512), 512)
        dk[rows, :] = dk[rows, :] + jnp.dot(
            slopes[rows, :], queries, preferred_element_type=wide
        )
        dv[rows, :] = dv[rows, :] + jnp.dot(p_ref[rows, :], turned, preferred_element_type=wide)
        return carry

    lax.fori_loop(0, LEN // 512, gather, 0)

    @pl.when(block == LEN // QUERIES - 1)
    def _():
        grad_ref[1] = dk[...].T.astype(low)
        grad_ref[2] = dv[...].T.astype(low)
        sums_ref[...] = tiles[...]
        for copy in around:
            copy.wait()
        x_end()
        across.wait()


def attend_back(qkv, probs, out, inverse, grad_out, x, grads, late, ident):
    whole = lambda *shape: pl.BlockSpec(shape, lambda i: (0,) * len(shape))
    return pl.pallas_call(
        backward_kernel,
        grid=(LEN // QUERIES,),
        out_shape=(
            jax.ShapeDtypeStruct((3, HEAD_DIM, LEN), low),
            jax.ShapeDtypeStruct((6 * CHUNK, QUERIES), wide),
            pltpu.HBM((CTX, *x.shape), low),
            pltpu.HBM(grads.shape[:1] + grads.shape[2:], low),
            jax.ShapeDtypeStruct((ZED - 1, *late.shape[1:]), low),
        ),
        in_specs=[
            whole(3, HEAD_DIM, LEN),
            pl.BlockSpec((LEN, QUERIES), lambda i: (0, i)),
            pl.BlockSpec((HEAD_DIM, QUERIES), lambda i: (0, i)),
            pl.BlockSpec((1, QUERIES), lambda i: (0, i)),
            pl.BlockSpec((1, HEAD_DIM, QUERIES), lambda i: (0, 0, i)),
            ANY,
            ANY,
            ANY,
        ],
        out_specs=(whole(3, HEAD_DIM, LEN), whole(6 * CHUNK, QUERIES), ANY, ANY, ANY),
        scratch_shapes=[
            pltpu.VMEM((LEN, HEAD_DIM), low),
            pltpu.VMEM((LEN, HEAD_DIM), wide),
            pltpu.VMEM((LEN, HEAD_DIM), wide),
            pltpu.VMEM((6 * CHUNK, QUERIES), wide),
            pltpu.VMEM((LEN, QUERIES), low),
            pltpu.SemaphoreType.DMA,
            pltpu.SemaphoreType.DMA((17,)),
            pltpu.SemaphoreType.DMA((17,)),
            pltpu.SemaphoreType.DMA((4,)),
            pltpu.SemaphoreType.DMA((4,)),
        ],
        compiler_params=pltpu.CompilerParams(
            collective_id=ident, has_side_effects=True, vmem_limit_bytes=14 << 20
        ),
    )(
        qkv,
        pltpu.with_memory_space_constraint(probs, pltpu.HBM),
        out, inverse, grad_out, x, grads, late
    )


def finish_kernel(
    rows_ref, late_ref, others_ref, wq_ref, wkv_ref, gain_ref,
    gq_ref, gkv_ref, gout_ref, router_ref, gain_one_ref, gain_two_ref, table_ref,
):
    c, e, z, xh, k = spot()
    late = late_ref[e] + jnp.sum(others_ref[...], axis=0)
    gout_ref[...] = late[:6, :D]
    router_ref[...] = late[:6, D + 67 : D + 83]
    gain_two_ref[...] = late[:6, D + 65 : D + 66]
    parts = [
        jnp.concatenate(
            [rows_ref[h, :, n * HEAD_DIM : (n + 1) * HEAD_DIM] for h in range(HEADS)], axis=1
        )[:6]
        for n in range(3)
    ]
    gq_ref[...] = parts[0]
    gkv_ref[:, :D] = parts[1]
    gkv_ref[:, D:] = parts[2]
    along = jnp.sum(wq_ref[...].astype(wide) * parts[0], axis=1, keepdims=True)
    along = along + jnp.sum(wkv_ref[:, :D].astype(wide) * parts[1], axis=1, keepdims=True)
    along = along + jnp.sum(wkv_ref[:, D:].astype(wide) * parts[2], axis=1, keepdims=True)
    gain_one_ref[...] = along / gain_ref[...]
    device = c * EXP + e
    buckets = rows_ref[pl.ds(device % 4 * 3, 3), 6, :]
    chosen = lax.broadcasted_iota(jnp.int32, buckets.shape, 1) == device // 4
    table_ref[...] = jnp.sum(jnp.where(chosen, buckets, 0.0), axis=1, keepdims=True)


def finish(by_head, late, others, wq, wkv, gain):
    shapes = [(6, D), (6, 2 * D), (6, D), (6, 16), (6, 1), (6, 1), (3, 1)]
    return pl.pallas_call(
        finish_kernel,
        out_shape=[jax.ShapeDtypeStruct(s, wide) for s in shapes],
        compiler_params=pltpu.CompilerParams(vmem_limit_bytes=8 << 20),
    )(by_head, late, others, wq, wkv, gain.astype(wide)[:, None])


def plain(kernel, shapes, megabytes, *args):
    return pl.pallas_call(
        kernel,
        out_shape=[jax.ShapeDtypeStruct(shape, kind) for shape, kind in shapes],
        compiler_params=pltpu.CompilerParams(vmem_limit_bytes=megabytes << 20),
    )(*args)


def iota(shape, axis):
    return lax.broadcasted_iota(jnp.int32, shape, axis)


def pack_kernel(wq_ref, wkv_ref, wo_ref, extra_ref, out_ref):
    empty = jnp.zeros((4, 128), wide)
    extra = extra_ref[...].astype(wide)
    wq, wkv, wo = (ref[...].astype(wide) for ref in (wq_ref, wkv_ref, wo_ref))
    for h in range(HEADS):
        at = h * HEAD_DIM
        query, key = wq[:, at : at + HEAD_DIM], wkv[:, at : at + HEAD_DIM]
        value = wkv[:, D + at : D + at + HEAD_DIM]
        upper = jnp.concatenate([query, key], axis=1)
        lower = jnp.concatenate([value, extra], axis=1)
        out_ref[h] = jnp.concatenate([upper, lower, empty], axis=0).astype(low)
    for n in range(3):
        upper, lower = (wo[:, (2 * n + i) * 128 : (2 * n + i + 1) * 128] for i in range(2))
        out_ref[HEADS + n] = jnp.concatenate([upper, lower, empty], axis=0).astype(low)


def six_rows(rows, first):
    shape = (rows // 16 * 6, rows)
    column = iota((1, rows), 1)
    inner = column % 16 - first
    place = jnp.where((inner >= 0) & (inner < 6), column // 16 * 6 + inner, -1)
    return (iota(shape, 0) == place).astype(low)


def project_kernel(mine_ref, x_ref, eight_ref, qkv_ref, h_ref, table_ref, first_ref, second_ref):
    c, e, z, xh, k = spot()
    mine = mine_ref[...]
    upper = jnp.dot(six_rows(2048, 0), mine, preferred_element_type=wide)
    lower = jnp.dot(six_rows(2048, 6), mine, preferred_element_type=wide)
    lower_turned = lower.T
    gain = lower_turned[64:65, :]
    weight_qk, weight_v = upper.T.astype(low), lower_turned[:64].astype(low)
    for n in range(4):
        rows = slice(n * 512, (n + 1) * 512)
        x = x_ref[rows, :].astype(wide)
        scale = lax.rsqrt(jnp.mean(x * x, axis=1, keepdims=True) + epsilon)
        h = (x * scale * gain).astype(low)
        h_ref[rows, :] = h
        both = dot(weight_qk, h, (1, 1)).astype(low)
        qkv_ref[0, :, rows] = both[:64]
        qkv_ref[1, :, rows] = both[64:]
        qkv_ref[2, :, rows] = dot(weight_v, h, (1, 1)).astype(low)
    head = head_of(c)
    column = jnp.broadcast_to(lower[:, 66:67], (D, 128))
    row = iota((BUCKETS, D), 1)
    wanted = (row // 24 == iota((BUCKETS, D), 0)) & (row % 24 == head // 3 * 6 + head % 3)
    table_ref[...] = jnp.dot(wanted.astype(low), column.astype(low), preferred_element_type=wide)
    pick = [six_rows(128, 0), six_rows(128, 6)]
    part = lambda n, i: jnp.dot(
        pick[i], eight_ref[:, n].reshape(128, 128), preferred_element_type=wide
    )
    first_ref[:, :128] = part(0, 1).astype(low)
    for n in range(3):
        for i in range(2):
            at = 128 + (2 * n + i) * 128
            first_ref[:, at : at + 128] = part(HEADS + n, i).astype(low)
    for pair in range(HEADS // 2):
        pieces = []
        for h in (2 * pair, 2 * pair + 1):
            pieces += [part(h, 0), part(h, 1)[:, :64]]
        pieces = jnp.concatenate(pieces, axis=1).astype(low)
        if pair < 2:
            first_ref[:, 896 + pair * 384 : 896 + (pair + 1) * 384] = pieces
        else:
            second_ref[:, (pair - 2) * 384 : (pair - 1) * 384] = pieces


def route_kernel(
    att_ref, x_ref, cot_ref, route_ref, full_ref,
    residual_ref, h_ref, probs_ref, dispatch_ref, out_ref,
):
    wo, small = full_ref[:, 128:896], full_ref[:, :128]
    gain = small.astype(wide).T[65:66, :]
    attended = att_ref[...].astype(wide).T.astype(low)
    residual = x_ref[...].astype(wide) + jnp.dot(attended, wo, preferred_element_type=wide)
    residual_ref[...] = residual
    scale = lax.rsqrt(jnp.mean(residual * residual, axis=1, keepdims=True) + epsilon)
    h_two = (residual * scale * gain).astype(low)
    h_ref[...] = h_two
    logits = jnp.dot(h_two, small, preferred_element_type=wide)[:, 67:83]
    logits = jnp.exp(logits - jnp.max(logits, axis=1, keepdims=True))
    probs = logits / jnp.sum(logits, axis=1, keepdims=True)
    probs_ref[...] = probs
    route = route_ref[...]
    choose = (route == iota((TOK, 16), 1)).astype(wide)
    before = (iota((TOK, TOK), 1) < iota((TOK, TOK), 0)).astype(low)
    earlier = jnp.dot(before, choose.astype(low), preferred_element_type=wide)
    slot = jnp.sum(earlier * choose, axis=1, keepdims=True).astype(jnp.int32)
    target = route // 2 * SLOTS + route % 2 * CAP + slot
    places = iota((TOK, EXP * SLOTS), 1)
    dispatch = jnp.concatenate(
        [(places == target).astype(wide), (places == target + 2 * CAP).astype(wide)], axis=0
    )
    dispatch_ref[...] = dispatch.astype(low)
    gate = jnp.sum(probs * choose, axis=1, keepdims=True)
    grad_y = (gate * cot_ref[...].astype(wide)).astype(low)
    turned = dispatch.T.astype(low)
    out = jnp.dot(turned[:, :TOK], h_two, preferred_element_type=wide)
    out = out + jnp.dot(turned[:, TOK:], grad_y, preferred_element_type=wide)
    out_ref[...] = out.astype(low)


def combine_kernel(
    back_ref, dispatch_ref, residual_ref, cot_ref, probs_ref, route_ref, h_ref, full_ref, att_ref,
    mixed_ref, grad_ref, grad_att_ref, late_ref,
):
    wo, small = full_ref[:, 128:896], full_ref[:, :128]
    gain = small.astype(wide).T[65:66, :]
    returned = jnp.dot(dispatch_ref[...], back_ref[...], preferred_element_type=wide)
    tokens, grad_h = returned[:TOK], returned[TOK:]
    residual, probs = residual_ref[...], probs_ref[...]
    choose = (route_ref[...] == iota((TOK, 16), 1)).astype(wide)
    gate = jnp.sum(probs * choose, axis=1, keepdims=True)
    mixed_ref[...] = (residual + gate * tokens).astype(low)
    grad = cot_ref[...].astype(wide)
    grad_choice = choose * jnp.sum(grad * tokens, axis=1, keepdims=True)
    grad_logits = probs * (grad_choice - jnp.sum(probs * grad_choice, axis=1, keepdims=True))
    spread = (iota((16, 128), 0) + 67 == iota((16, 128), 1)).astype(low)
    upper = grad_logits.astype(low)
    lower = (grad_logits - upper.astype(wide)).astype(low)
    upper = jnp.dot(upper, spread, preferred_element_type=wide).astype(low)
    lower = jnp.dot(lower, spread, preferred_element_type=wide).astype(low)
    grad_h = grad_h + dot(upper, small, (1, 1)) + dot(lower, small, (1, 1))
    scale = lax.rsqrt(jnp.mean(residual * residual, axis=1, keepdims=True) + epsilon)
    along = grad_h * gain
    mean = jnp.mean(along * residual, axis=1, keepdims=True)
    grad = grad + scale * along - (scale * scale * scale * mean) * residual
    grad_ref[...] = grad
    branch = grad.astype(low)
    grad_att_ref[...] = dot(wo, branch, (1, 1)).astype(low)
    late_ref[:, :D] = jnp.dot(att_ref[...], branch, preferred_element_type=wide).astype(low)
    turned = h_ref[...].astype(wide).T.astype(low)
    extra = jnp.dot(turned, upper, preferred_element_type=wide)
    extra = extra + jnp.dot(turned, lower, preferred_element_type=wide)
    gains = (grad_h * residual * scale).T
    gains = jnp.sum(gains, axis=1, keepdims=True)
    late_ref[:, D:] = jnp.where(iota((D, 128), 1) == 65, gains, extra).astype(low)


def expert_kernel(lists_ref, in_ref, out_ref, partial_ref, grad_in_ref, grad_out_ref):
    for n in range(2):
        rows = lists_ref[:, n].reshape(ZED * 80, D)
        grads = lists_ref[:, 2 + n].reshape(ZED * 80, D)
        weight_in, weight_out = in_ref[n], out_ref[n]
        pre = dot(rows, weight_in, (1, 1))
        square = pre * pre
        bend = jnp.tanh(0.7978845608028654 * (pre + 0.044715 * square * pre))
        hidden = (0.5 * pre * (1.0 + bend)).astype(low)
        slope = 0.5 * (1.0 + bend) + 0.5 * pre * (1.0 - bend * bend) * (
            0.7978845608028654 * (1.0 + 0.134145 * square)
        )
        grad_pre = (dot(grads, weight_out, (1, 1)) * slope).astype(low)
        y = jnp.dot(hidden, weight_out, preferred_element_type=wide).astype(low)
        partial_ref[:, n * 80 : (n + 1) * 80, :] = y.reshape(ZED, 80, D)
        back = jnp.dot(grad_pre, weight_in, preferred_element_type=wide).astype(low)
        partial_ref[:, 160 + n * 80 : 160 + (n + 1) * 80, :] = back.reshape(ZED, 80, D)
        grad_in_ref[n] = dot(grad_pre, rows, (0, 0)).astype(low)
        grad_out_ref[n] = dot(hidden, grads, (0, 0)).astype(low)


def unlist_kernel(partial_ref, others_ref, out_ref):
    c, e, z, xh, k = spot()
    total = partial_ref[z].astype(wide) + jnp.sum(others_ref[...].astype(wide), axis=0)
    row = iota((EXP * SLOTS, 1), 0)
    inner = row % SLOTS
    source = jnp.where(inner < 4 * CAP, inner // CAP * 80 + row // SLOTS * CAP + inner % CAP, -1)
    pick = (iota((EXP * SLOTS, 320), 1) == source).astype(low)
    out = jnp.dot(pick, total.astype(low), preferred_element_type=wide).astype(low)
    out_ref[...] = out.reshape(EXP, SLOTS, D)


def head_weights_kernel(grads_ref, h_ref, tiles_ref, late_ref, others_ref, out_ref, sum_ref):
    c, e, z, xh, k = spot()
    grads = grads_ref[...].reshape(192, LEN)
    product = jnp.dot(grads, h_ref[...], preferred_element_type=wide).astype(low)
    column = iota((1, EXP * TOK), 1)
    place = (column % TOK // 8 * EXP + column // TOK) * 6 + column % 8
    place = jnp.where(column % 8 < 6, place, -1)
    by_owner = (iota((D, EXP * TOK), 0) == place).astype(low)
    product = jnp.dot(product, by_owner, preferred_element_type=wide).T
    tile = lambda n, half: tiles_ref[
        n * CHUNK : (n + 1) * CHUNK, half * TOK : (half + 1) * TOK
    ]
    near = jnp.concatenate([tile(n, 0) + tile(n + 1, 1) for n in (1, 2, 3)], axis=0)
    ids = near_buckets(near.shape, CHUNK)
    lane = iota((1, 192), 1)
    buckets = jnp.zeros((1, 192), wide)
    for b in range(BUCKETS):
        part = jnp.sum(jnp.where(ids == b, near, 0.0), axis=0, keepdims=True)
        if b == BUCKETS // 2 - 1:
            part = part + jnp.sum(tile(0, 0) + tile(0, 1) + tile(1, 1), axis=0, keepdims=True)
        if b == BUCKETS - 1:
            part = part + jnp.sum(tile(4, 0) + tile(5, 0) + tile(5, 1), axis=0, keepdims=True)
        buckets = jnp.where(lane == b, jnp.sum(part, axis=1, keepdims=True), buckets)
    sixth = iota((EXP * TOK, 1), 0) % 8 == 6
    product = jnp.where(sixth, buckets, product)
    out_ref[...] = product.astype(low).reshape(EXP, TOK, 192)
    total = late_ref[z].astype(wide) + jnp.sum(others_ref[...].astype(wide), axis=0)
    sum_ref[...] = total.astype(low)


def halves_kernel(late_ref, late_others_ref, grads_ref, others_ref, late_out, grads_out):
    k = spot()[4]
    late = late_ref[:, k].astype(wide) + late_others_ref[0].astype(wide)
    late_out[...] = late.astype(low).reshape(ZED, 2, 48, 896)
    grads = grads_ref[:, :, k].astype(wide) + others_ref[0].astype(wide)
    grads_out[...] = grads.astype(low)


def owners_kernel(own_ref, others_ref, late_ref, late_others_ref, out_ref, sum_ref):
    c, e, z, xh, k = spot()
    total = own_ref[e].astype(wide) + jnp.sum(others_ref[...].astype(wide), axis=0)
    out_ref[...] = total.reshape(CTX, 8, 192)
    late = late_ref[xh].astype(wide) + late_others_ref[0].astype(wide)
    empty = jnp.zeros((2, 896), wide)
    for n in range(EXP):
        sum_ref[n] = jnp.concatenate([late[6 * n : 6 * n + 6], empty], axis=0)


def tokens_kernel(grads_ref, first_ref, second_ref, x_ref, residual_ref, out_ref):
    grads = grads_ref[...].reshape(3 * D, TOK).astype(wide).T.astype(low)
    grad_h = dot(grads[:, :D], first_ref[:, 896:], (1, 1))
    grad_h = grad_h + dot(grads[:, D:], second_ref[...], (1, 1))
    gain = first_ref[:, :128].astype(wide).T[64:65, :]
    x = x_ref[...].astype(wide)
    scale = lax.rsqrt(jnp.mean(x * x, axis=1, keepdims=True) + epsilon)
    along = grad_h * gain
    mean = jnp.mean(along * x, axis=1, keepdims=True)
    out_ref[...] = residual_ref[...] + scale * along - (scale * scale * scale * mean) * x


def dot(a, b, dims=(1, 0)):
    return lax.dot_general(
        a, b, (((dims[0],), (dims[1],)), ((), ())), preferred_element_type=wide
    )


def shards(
    tokens,
    cotangent,
    routes,
    query_weight,
    kv_weight,
    out_weight,
    norm_gain_one,
    norm_gain_two,
    router_weight,
    bias_table,
    expert_in,
    expert_out,
):
    extra = jnp.concatenate(
        [
            norm_gain_one[:, None],
            norm_gain_two[:, None],
            jnp.pad(bias_table, (0, 3))[:, None],
            router_weight,
            jnp.zeros((6, 45), low),
        ],
        axis=1,
    )
    packed = plain(
        pack_kernel, [((15, 16, 128), low)], 4, query_weight, kv_weight, out_weight, extra
    )[0]
    eight, mine, x_all = opening(packed, tokens[0], 1)
    head_qkv, h_all, head_table, block, block_qkv = plain(
        project_kernel,
        [
            ((3, HEAD_DIM, LEN), low),
            ((LEN, D), low),
            ((BUCKETS, 128), wide),
            ((48, 128 + 2 * D), low),
            ((48, 2 * D), low),
        ],
        28,
        mine.reshape(2048, 128),
        x_all.reshape(LEN, D),
        eight,
    )
    probs, attended, attended_head, inverse, full, experts_out = attend(
        head_qkv, head_table, block, expert_out, 18
    )
    full = full.reshape(D, 2 * D + 128)
    attended_low = from_heads(attended_head, 5).reshape(D, TOK)
    routed = (TOK, D)
    residual, h_two, route_probs, dispatch, outgoing = plain(
        route_kernel,
        [
            (routed, wide),
            (routed, low),
            ((TOK, 16), wide),
            ((2 * TOK, EXP * SLOTS), low),
            ((EXP * SLOTS, D), low),
        ],
        16,
        attended_low,
        tokens[0],
        cotangent[0],
        routes[0],
        full,
    )
    received = swap(outgoing.reshape(EXP, SLOTS, D), "exp", 6, 0).reshape(EXP * SLOTS, D)

    row = jnp.arange(4 * 80, dtype=jnp.int32)
    source = row % 80 // CAP * SLOTS + row // 80 * CAP + row % CAP
    compact = (source[:, None] == jnp.arange(EXP * SLOTS, dtype=jnp.int32)[None, :]).astype(low)
    lists, experts_in = gather_lists(
        dot(compact, received).astype(low), jnp.swapaxes(expert_in, 1, 2), 7
    )
    lists = lists.reshape(ZED, 4, 80, D)
    experts_here = experts_in.reshape(2, D, D), experts_out.reshape(2, D, D)
    partial, grads_in, grads_out = plain(
        expert_kernel,
        [((ZED, 320, D), low), ((2, D, D), low), ((2, D, D), low)],
        28,
        lists,
        *experts_here,
    )
    grads_out = grads_out.reshape(2, 2, 2, 192, D)
    others, grads_own, grads_other = return_lists(partial, grads_out, 8)
    grad_expert_out = grads_own.astype(wide) + grads_other.astype(wide)
    spread = plain(unlist_kernel, [((EXP, SLOTS, D), low)], 12, partial, others)[0]
    expert_grads = grads_in.reshape(2, 2, 2, 192, D)
    back, expert_others = swaps(9, (spread, "exp", 0, True), (expert_grads, "core", 2, False))
    mixed_rows, grad_residual, grad_attended, late = plain(
        combine_kernel,
        [(routed, low), (routed, wide), ((D, TOK), low), ((D, 896), low)],
        20,
        back.reshape(EXP * SLOTS, D),
        dispatch,
        residual,
        cotangent[0],
        route_probs,
        routes[0],
        h_two,
        full,
        attended_low,
    )
    late = late.reshape(8, 2, 48, 896)
    head_grad, others = swaps(
        10,
        (grad_attended.reshape(1, HEADS, HEAD_DIM, TOK), "to_heads", None, True),
        (late, "core", 1, False),
    )
    late, expert_grads = plain(
        halves_kernel,
        [((ZED, 2, 48, 896), low), ((2, 2, 192, D), low)],
        14,
        late,
        others,
        expert_grads,
        expert_others,
    )
    head_grads, tile_sums, qkv_full, others, late_others = attend_back(
        head_qkv, probs, attended, inverse, head_grad, block_qkv, expert_grads, late, 19
    )
    qkv_full = qkv_full.reshape(D, 2 * D)
    grad_expert_in = jnp.swapaxes(add_up(expert_grads, "x", 1, others[None]), 1, 2)

    head_weights, late = plain(
        head_weights_kernel,
        [((EXP, TOK, 192), low), ((2, 48, 896), low)],
        20,
        head_grads,
        h_all,
        tile_sums,
        late,
        late_others,
    )
    others, late_others = swaps(
        11, (head_weights, "exp", 0, False), (late, "x", 0, False)
    )
    head_weights, late = plain(
        owners_kernel,
        [((CTX, 8, 192), wide), ((EXP, 8, 896), wide)],
        8,
        head_weights,
        others,
        late,
        late_others,
    )
    grad_qkv, by_head, others = swaps(
        12,
        (head_grads, "from_heads", None, True),
        (head_weights, "head_rows", None, True),
        (late, "exp", 0, False),
    )
    finished = finish(by_head, late, others, query_weight, kv_weight, norm_gain_one)

    grad_tokens = plain(
        tokens_kernel, [(routed, wide)], 16, grad_qkv, full, qkv_full, tokens[0], grad_residual
    )[0]
    return (
        mixed_rows[None],
        grad_tokens[None],
        *finished[:3],
        finished[4][:, 0],
        finished[5][:, 0],
        finished[3],
        finished[6][:, 0],
        grad_expert_in,
        grad_expert_out,
    )


def solution(mesh):
    rows = P("exp", "ctx", None)
    shared, vector = P(("ctx", "exp"), None), P(("ctx", "exp"))
    expert_in, expert_out = P("exp", None, "ctx"), P("exp", "ctx", None)
    return jax.shard_map(
        shards,
        mesh=mesh,
        in_specs=(rows, rows, rows, shared, shared, shared, vector, vector, shared, vector)
        + (expert_in, expert_out),
        out_specs=(rows, rows, shared, shared, shared, vector, vector, shared, vector)
        + (expert_in, expert_out),
        check_vma=False,
    )
```
